256 devices in a mesh: batch: 32 (over x, y, core), head: 8 (over z).
Axes of the slice: x: 4, y: 4, z: 8, core: 2. Of those that a mesh axis runs over, the one named last changes fastest.
Arguments:
- queries: bfloat16 [1024, 16384], P('batch', 'head'), may hold values from -16 to 16
- new_kv: bfloat16 [2, 1024, 1024], P(None, 'batch', 'head'), may hold values from -16 to 16
- prefix_kv: bfloat16 [2, 65536, 1024], P(None, 'batch', 'head'), may hold values from -16 to 16
- suffix_kv: bfloat16 [2, 8192, 16, 1024], P(None, 'batch', None, 'head'), may hold values from -16 to 16
- page_table: int32 [1024, 8], P('batch'), may hold values from 0 to 8191, as said below
- suffix_len: int32 [1024], P('batch'), may hold values from 1 to 128
- prompt_of: int32 [1024], P('batch'), may hold values from 0 to 7, as said below
- out_weight: bfloat16 [16384, 16384], P('head', 'batch'), may hold values from -0.046875 to 0.046875
Outputs:
- projected: bfloat16 [1024, 16384], P('head', 'batch')
The draws below stay inside these ranges and needn't reach their ends.
Inputs may be any that keep to these rules, and one draw needn't show every extreme that they name: `prompt_of`: each aligned block of 32 completions holds exactly 4 completions of every prompt. `page_table`: the rows of an aligned block b of 32 completions name every page of [b * 32 * 8, (b + 1) * 32 * 8) once.
All inputs are finite; a program needn't handle non-finite values.
Results may differ from the reference program's by a relative error of at most 0.0057.
Values may be sent and summed in bfloat16 or wider, within the bound.
No kernel may reach another device: no remote copies, remote signals or barrier semaphores. Data moves between devices by JAX's collectives and lax.ppermute only.
A program may use at most 64 MiB of HBM per device.

```python
import jax
import jax.numpy as jnp
from jax import lax

D = 16384
HQ = 128
KVH = 8
DH = 128
SAMPLES = 128
PAGE = 16
PAGES = 8
COMP_DEV = 32
COMPLETIONS = 1024
PROMPTS = 8
SPAN = 4
PREFIX_DEV = 2048
SUFFIX = 128
PREFIX_ROWS = 65536
POOL = 8192


def lifted_rows(key, rows, heads):
    base_key = jax.random.fold_in(key, 0)
    base = jax.random.normal(base_key, (rows, heads, DH), jnp.float32)
    return jnp.clip(base, -16.0, 16.0).reshape(rows, heads * DH)


def drawn_rows(key, rows, width):
    return jnp.clip(jax.random.normal(key, (rows, width), jnp.float32), -16.0, 16.0)


def draw_queries(key, part):
    key = jax.random.fold_in(key, 11)
    values = lifted_rows(key, COMPLETIONS, HQ)
    return values.astype(jnp.bfloat16)


def draw_new_kv(key, part):
    key = jax.random.fold_in(key, 12)
    key_one, key_two = jax.random.split(key)
    keys = lifted_rows(key_one, COMPLETIONS, KVH)
    values = drawn_rows(key_two, COMPLETIONS, KVH * DH)
    return jnp.stack([keys, values]).astype(jnp.bfloat16)


def draw_prefix_kv(key, part):
    key = jax.random.fold_in(key, 13)
    key_one, key_two = jax.random.split(key)
    keys = lifted_rows(key_one, PREFIX_ROWS, KVH)
    values = drawn_rows(key_two, PREFIX_ROWS, KVH * DH)
    return jnp.stack([keys, values]).astype(jnp.bfloat16)


def draw_suffix_kv(key, part):
    key = jax.random.fold_in(key, 14)
    key_one, key_two = jax.random.split(key)
    keys = lifted_rows(key_one, POOL * PAGE, KVH)
    values = drawn_rows(key_two, POOL * PAGE, KVH * DH)
    return jnp.stack([keys, values]).reshape(2, POOL, PAGE, KVH * DH).astype(jnp.bfloat16)


def draw_page_table(key, part):
    key = jax.random.fold_in(key, 15)
    blocks = COMPLETIONS // COMP_DEV
    keys = jax.random.split(key, blocks)
    perms = jax.vmap(lambda k: jax.random.permutation(k, COMP_DEV * PAGES))(keys)
    offsets = jnp.arange(blocks, dtype=jnp.int32)[:, None] * (COMP_DEV * PAGES)
    return (perms.astype(jnp.int32) + offsets).reshape(COMPLETIONS, PAGES).astype(jnp.int32)


def draw_suffix_len(key, part):
    key = jax.random.fold_in(key, 16)
    key_cap, key_len, key_spot = jax.random.split(key, 3)
    blocks = COMPLETIONS // COMP_DEV
    caps = jax.random.randint(key_cap, (blocks, 1), 1, 5, dtype=jnp.int32) * SUFFIX // 4
    lens = jax.random.randint(key_len, (blocks, COMP_DEV), 1, caps + 1, dtype=jnp.int32)
    spot = jax.random.randint(key_spot, (), 0, COMPLETIONS, dtype=jnp.int32)
    return lens.reshape(COMPLETIONS).at[spot].set(SUFFIX).astype(jnp.int32)


def draw_prompt_of(key, part):
    key = jax.random.fold_in(key, 17)
    blocks = COMPLETIONS // COMP_DEV
    keys = jax.random.split(key, blocks)
    perms = jax.vmap(lambda k: jax.random.permutation(k, COMP_DEV))(keys)
    return (perms.astype(jnp.int32) % PROMPTS).reshape(COMPLETIONS).astype(jnp.int32)


def steps_of(key, extent, cuts, least, high):
    gain = 1.0
    for axis_at, blocks in cuts:
        heights = jax.random.uniform(jax.random.fold_in(jax.random.fold_in(key, 6), axis_at), (blocks,), jnp.float32, least / len(cuts), high / len(cuts))
        gain = gain * jnp.repeat(jnp.exp(heights), extent[axis_at] // blocks).reshape((-1,) + (1,) * (len(extent) - 1 - axis_at))
    return gain


def centred(key, dims, scale, bound, cuts=(), held_as=jnp.bfloat16):
    array = jax.random.normal(key, dims, jnp.float32) * scale
    if len(cuts) > 0:
        array = steps_of(key, dims, cuts, -0.22, 0.18) * array
    return jnp.clip(array, min=-bound, max=bound).astype(held_as)


def setup_inputs(seed: int = 0) -> dict:
    key_list = jax.random.split(jax.random.key(seed), 9)
    queries = draw_queries(jax.random.fold_in(key_list[8], 71), 0)
    new_kv = draw_new_kv(jax.random.fold_in(key_list[8], 71), 0)
    prefix_kv = draw_prefix_kv(jax.random.fold_in(key_list[8], 71), 0)
    suffix_kv = draw_suffix_kv(jax.random.fold_in(key_list[8], 71), 0)
    page_table = draw_page_table(jax.random.fold_in(key_list[8], 71), 0)
    suffix_len = draw_suffix_len(jax.random.fold_in(key_list[8], 71), 0)
    prompt_of = draw_prompt_of(jax.random.fold_in(key_list[8], 71), 0)
    out_weight = centred(key_list[7], (HQ * DH, D), (HQ * DH) ** -0.5, 0.046875, ((0, 8), (1, 32)))
    return dict(queries=queries, new_kv=new_kv, prefix_kv=prefix_kv, suffix_kv=suffix_kv, page_table=page_table, suffix_len=suffix_len, prompt_of=prompt_of, out_weight=out_weight)


big_negative = -1.0e30


def reference(queries, new_kv, prefix_kv, suffix_kv, page_table, suffix_len, prompt_of, out_weight):
    group = HQ // KVH
    scale = DH ** -0.5
    order = jnp.argsort(prompt_of * COMPLETIONS + jnp.arange(COMPLETIONS, dtype=jnp.int32)).astype(jnp.int32)
    back = jnp.argsort(order).astype(jnp.int32)
    positions = jnp.arange(SUFFIX, dtype=jnp.int32)

    def one_head(head):
        start = head * DH
        query = lax.dynamic_slice_in_dim(queries, head * group * DH, group * DH, 1)
        query = query.reshape(COMPLETIONS, group, DH).astype(jnp.float32)
        own_key = lax.dynamic_slice_in_dim(new_kv[0], start, DH, 1).astype(jnp.float32)
        own_value = lax.dynamic_slice_in_dim(new_kv[1], start, DH, 1).astype(jnp.float32)
        pages = lax.dynamic_slice_in_dim(suffix_kv, start, DH, 3)[:, page_table]
        pages = pages.reshape(2, COMPLETIONS, SUFFIX, DH).astype(jnp.float32)
        scores = jnp.einsum("cge,cse->cgs", query, pages[0]) * scale
        valid = positions[None, None, :] < suffix_len[:, None, None]
        scores = jnp.where(valid, scores, big_negative)
        own = jnp.einsum("cge,ce->cg", query, own_key) * scale
        speak = jnp.maximum(jnp.max(scores, axis=2), own)
        weights = jnp.exp(scores - speak[..., None])
        own_weight = jnp.exp(own - speak)
        stotal = jnp.sum(weights, axis=2) + own_weight
        rounded = lax.optimization_barrier(weights.astype(jnp.bfloat16)).astype(jnp.float32)
        own_rounded = lax.optimization_barrier(own_weight.astype(jnp.bfloat16)).astype(jnp.float32)
        smixed = jnp.einsum("cgs,cse->cge", rounded, pages[1]) + own_rounded[..., None] * own_value[:, None, :]

        prefix = lax.dynamic_slice_in_dim(prefix_kv, start, DH, 2)
        prefix = prefix.reshape(2, PROMPTS, SPAN, PREFIX_DEV, DH).transpose(1, 0, 2, 3, 4)
        grouped = query[order].reshape(PROMPTS, SAMPLES, group, DH)

        def one_prompt(items):
            rows, keys_values = items
            sc = jnp.einsum("sge,bke->sgbk", rows, keys_values[0].astype(jnp.float32)) * scale
            peak = jnp.max(sc, axis=3)
            wts = jnp.exp(sc - peak[..., None])
            total = jnp.sum(wts, axis=3)
            wr = lax.optimization_barrier(wts.astype(jnp.bfloat16)).astype(jnp.float32)
            mixed = jnp.einsum("sgbk,bke->sgbe", wr, keys_values[1].astype(jnp.float32))
            top = jnp.max(peak, axis=2)
            factor = jnp.exp(peak - top[..., None])
            return jnp.sum(mixed * factor[..., None], axis=2), jnp.sum(total * factor, axis=2), top

        pmixed, ptotal, ppeak = lax.map(one_prompt, (grouped, prefix))
        pmixed = pmixed.reshape(COMPLETIONS, group, DH)[back]
        ptotal = ptotal.reshape(COMPLETIONS, group)[back]
        ppeak = ppeak.reshape(COMPLETIONS, group)[back]
        top = jnp.maximum(ppeak, speak)
        first = jnp.exp(ppeak - top)
        second = jnp.exp(speak - top)
        attended = (pmixed * first[..., None] + smixed * second[..., None]) / (ptotal * first + stotal * second)[..., None]
        return attended.astype(jnp.bfloat16)

    heads = lax.map(one_head, jnp.arange(KVH, dtype=jnp.int32))
    attended = heads.transpose(1, 0, 2, 3).reshape(COMPLETIONS, HQ * DH)
    return jnp.dot(attended, out_weight, preferred_element_type=jnp.float32).astype(jnp.bfloat16)
```

```python
import jax
import jax.numpy as jnp
from jax import lax
from jax.experimental import pallas as pl
from jax.experimental.pallas import tpu as pltpu
from jax.sharding import PartitionSpec as P

DH = 128
GROUP = 16
SCALE = DH**-0.5
LOG2E = 1.4426950408889634
BATCH = 32
HEADS = 8
VMEM = pl.BlockSpec(memory_space=pltpu.VMEM)
SMEM = pl.BlockSpec(memory_space=pltpu.SMEM)
F32 = jnp.float32
BF16 = jnp.bfloat16
NT = (((1,), (1,)), ((), ()))
NN = (((1,), (0,)), ((), ()))


def params():
    return pltpu.CompilerParams(vmem_limit_bytes=48 * 1024 * 1024)


def dot(a, b, dims=NN):
    return lax.dot_general(a, b, dims, preferred_element_type=F32)


def lanes():
    return lax.broadcasted_iota(jnp.int32, (GROUP, DH), 1)


def split_tile(tile, step):
    high = tile.astype(BF16).astype(F32)
    rest = tile - high
    middle = rest.astype(BF16).astype(F32)
    low = rest - middle
    joined = high + pltpu.roll(middle, step, 1) + pltpu.roll(low, 2 * step, 1)
    return joined.astype(BF16)


def join_tile(tile, step):
    wide = tile.astype(F32)
    return (wide + pltpu.roll(wide, DH - step, 1)) + pltpu.roll(wide, DH - 2 * step, 1)


def sort_body(place, prompt, q, o0, o1, o2, o3, held, seen):
    lane = lanes()
    tile = jnp.zeros((GROUP, DH), F32)
    for p in range(8):
        seen[p] = 0
    for r in range(32):
        p = prompt[r]
        k = seen[p]
        seen[p] = k + 1
        held[(4 * p + k) ^ place[0]] = q[r]
        tile = jnp.where(lane == r, (4 * p + k).astype(F32), tile)
    for i, out in enumerate((o0, o1, o2, o3)):
        out[0:8] = held[8 * i : 8 * i + 8]
        out[8] = tile.astype(BF16)


def sort_queries(place, prompt, q):
    out = jax.ShapeDtypeStruct((9, GROUP, DH), BF16)
    return pl.pallas_call(
        sort_body,
        out_shape=[out] * 4,
        in_specs=[SMEM, SMEM, VMEM],
        out_specs=[VMEM] * 4,
        scratch_shapes=[pltpu.VMEM((32, GROUP, DH), BF16), pltpu.SMEM((8,), jnp.int32)],
        compiler_params=params(),
        name="sort_queries",
    )(place, prompt, q)


def regroup_body(place, a0, a1, a2, a3, same, other):
    for i, a in enumerate((a0, a1, a2, a3)):
        same[4 * i : 4 * i + 4] = a[0:4]
        other[4 * i : 4 * i + 4] = a[4:8]

    for i, a in enumerate((a0, a1, a2, a3)):

        @pl.when(place[2] ^ (place[4] >> 1) == i)
        def _(a=a):
            same[16] = a[8]
            other[16] = a[8]


def regroup(place, parts):
    out = jax.ShapeDtypeStruct((17, GROUP, DH), BF16)
    return pl.pallas_call(
        regroup_body,
        out_shape=[out, out],
        in_specs=[SMEM] + [VMEM] * 4,
        out_specs=[VMEM] * 2,
        compiler_params=params(),
        name="regroup",
    )(place, *parts)


def suffix_body(place, prompt, table, length, q, new, pool, o0, o1, o2, o3, scores, weights, held, tiles, seen):
    lane = lanes()
    base = place[1]
    for n in range(32):
        keys = jnp.concatenate([pool[0, table[n, j] - base] for j in range(8)], axis=0)
        s = dot(q[n], keys, NT) * SCALE
        scores[n] = jnp.where(lane < length[n], s, -1e30)
    own_keys = new[0].astype(F32)
    own_values = new[1].astype(F32)
    own = jnp.stack(
        [
            jnp.sum(q[n].astype(F32) * own_keys[n : n + 1], axis=1, keepdims=True)
            for n in range(32)
        ]
    ) * SCALE
    s = scores[...]
    peak = jnp.maximum(jnp.max(s, axis=2, keepdims=True), own)
    w = jnp.exp(s - peak)
    own_weight = jnp.exp(own - peak)
    total = jnp.sum(w, axis=2, keepdims=True) + own_weight
    weights[...] = w.astype(BF16)
    own_weight = own_weight.astype(BF16).astype(F32)
    mass = peak + jnp.log(total)
    inverse = 1.0 / total
    tiles[...] = jnp.zeros_like(tiles)
    for p in range(8):
        seen[p] = 0
    for n in range(32):
        values = jnp.concatenate([pool[1, table[n, j] - base] for j in range(8)], axis=0)
        mixed = dot(weights[n], values) + own_weight[n] * own_values[n : n + 1]
        p = prompt[n]
        k = seen[p]
        seen[p] = k + 1
        slot = (4 * p + k) ^ place[0]
        held[slot] = (mixed * inverse[n]).astype(BF16)
        at = slot >> 3
        tiles[at] = jnp.where(lane == (slot & 7), mass[n], tiles[at])
    for i, out in enumerate((o0, o1, o2, o3)):
        out[0:8] = held[8 * i : 8 * i + 8]
        out[8] = split_tile(tiles[i], 8)


def suffix_parts(place, prompt, table, length, q, new, pool):
    out = jax.ShapeDtypeStruct((9, GROUP, DH), BF16)
    return pl.pallas_call(
        suffix_body,
        out_shape=[out] * 4,
        in_specs=[SMEM, SMEM, SMEM, SMEM, VMEM, VMEM, VMEM],
        out_specs=[VMEM] * 4,
        scratch_shapes=[
            pltpu.VMEM((32, GROUP, DH), F32),
            pltpu.VMEM((32, GROUP, DH), BF16),
            pltpu.VMEM((32, GROUP, DH), BF16),
            pltpu.VMEM((4, GROUP, DH), F32),
            pltpu.SMEM((8,), jnp.int32),
        ],
        compiler_params=params(),
        cost_estimate=pl.CostEstimate(flops=40_000_000, bytes_accessed=3_000_000, transcendentals=70000),
        name="suffix_parts",
    )(place, prompt, table, length, q, new, pool)


ROWS = 128


def prefix_block(q, kv0, kv1):
    s0 = dot(q, kv0[0], NT)
    s1 = dot(q, kv1[0], NT)
    peak = jnp.maximum(jnp.max(s0, axis=1, keepdims=True), jnp.max(s1, axis=1, keepdims=True))
    w0 = jnp.exp2((s0 - peak) * (SCALE * LOG2E))
    w1 = jnp.exp2((s1 - peak) * (SCALE * LOG2E))
    total = jnp.sum(w0, axis=1, keepdims=True) + jnp.sum(w1, axis=1, keepdims=True)
    mixed = dot(w0.astype(BF16), kv0[1]) + dot(w1.astype(BF16), kv1[1])
    return mixed / total, peak * SCALE + jnp.log(total)


def prefix_send_body(qa, qb, kv0, kv1, out):
    lane = lanes()
    tile = jnp.zeros((GROUP, DH), F32)
    count = ROWS // GROUP
    for half, q in enumerate((qa, qb)):
        for i in range(256 // ROWS):
            rows = q[i * count : (i + 1) * count].reshape(ROWS, DH)
            mixed, mass = prefix_block(rows, kv0, kv1)
            at = half * 16 + i * count
            out[at : at + count] = mixed.reshape(count, GROUP, DH).astype(BF16)
            for n in range(count):
                tile = jnp.where(lane == at + n, mass[n * GROUP : (n + 1) * GROUP], tile)
    out[32] = split_tile(tile, 32)


def prefix_keep_body(qa, qb, kv0, kv1, out, masses):
    count = ROWS // GROUP
    for half, q in enumerate((qa, qb)):
        for i in range(256 // ROWS):
            rows = q[i * count : (i + 1) * count].reshape(ROWS, DH)
            mixed, mass = prefix_block(rows, kv0, kv1)
            at = half * 16 + i * count
            out[at : at + count] = mixed.reshape(count, GROUP, DH)
            masses[at : at + count] = jnp.broadcast_to(mass, (ROWS, DH)).reshape(count, GROUP, DH)


PREFIX_COST = pl.CostEstimate(
    flops=4 * 512 * 4096 * 128, bytes_accessed=2_500_000, transcendentals=512 * 4096
)


def prefix_send(qa, qb, kv0, kv1):
    return pl.pallas_call(
        prefix_send_body,
        out_shape=jax.ShapeDtypeStruct((33, GROUP, DH), BF16),
        in_specs=[VMEM] * 4,
        out_specs=VMEM,
        compiler_params=params(),
        cost_estimate=PREFIX_COST,
        name="prefix_send",
    )(qa, qb, kv0, kv1)


def prefix_keep(qa, qb, kv0, kv1):
    out = jax.ShapeDtypeStruct((32, GROUP, DH), F32)
    return pl.pallas_call(
        prefix_keep_body,
        out_shape=[out, out],
        in_specs=[VMEM] * 4,
        out_specs=[VMEM, VMEM],
        compiler_params=params(),
        cost_estimate=PREFIX_COST,
        name="prefix_keep",
    )(qa, qb, kv0, kv1)


def combine_body(place, mine, masses, message, s0, s1, s2, s3, far, out, held):
    x, y_high, z = place[2], place[3], place[4]
    theirs = join_tile(message[32], 32)
    near = [join_tile(s[8], 8) for s in (s0, s1, s2, s3)]
    across = [join_tile(far[5 * i + 4], 8) for i in range(4)]
    for g in range(2):
        for kx in range(4):
            for k in range(4):
                n = g * 16 + kx * 4 + k
                a, la = mine[n], masses[n]
                b = message[n].astype(F32)
                lb = jnp.broadcast_to(theirs[:, n : n + 1], (GROUP, DH))
                if g == 0:
                    s = (s0, s1, s2, s3)[kx][k].astype(F32)
                    ls = jnp.broadcast_to(near[kx][:, k : k + 1], (GROUP, DH))
                else:
                    s = far[5 * kx + k].astype(F32)
                    ls = jnp.broadcast_to(across[kx][:, 4 + k : 5 + k], (GROUP, DH))
                top = jnp.maximum(jnp.maximum(la, lb), ls)
                ea, eb, es = jnp.exp(la - top), jnp.exp(lb - top), jnp.exp(ls - top)
                row = (ea * a + eb * b + es * s) / (ea + eb + es)
                target = (x ^ kx) * 2 + (y_high ^ g)
                held[((target - z) & 7) * 4 + k] = row
    for h in range(GROUP):
        out[:, h * DH : (h + 1) * DH] = held[:, h, :].astype(BF16)


def combine(place, mine, masses, message, near, far):
    return pl.pallas_call(
        combine_body,
        out_shape=jax.ShapeDtypeStruct((32, GROUP * DH), BF16),
        in_specs=[SMEM] + [VMEM] * 8,
        out_specs=VMEM,
        scratch_shapes=[pltpu.VMEM((32, GROUP, DH), F32)],
        compiler_params=params(),
        name="combine",
    )(place, mine, masses, message, *near, far)


def project_body(*refs):
    blocks, weight, out, left, right = refs[:8], refs[8], refs[9], refs[10], refs[11]
    low = lax.broadcasted_iota(jnp.int32, (8, 512), 0) < 4
    for i, block in enumerate(blocks):
        total = dot(block[...], weight[...])
        for g in range(4):
            even, odd = [], []
            for j in (0, 2):
                first = total[j * 32 + g * 8 : j * 32 + g * 8 + 8]
                second = total[(j + 1) * 32 + g * 8 : (j + 1) * 32 + g * 8 + 8]
                even.append(jnp.where(low, first, pltpu.roll(second, 4, 0)))
                odd.append(jnp.where(low, pltpu.roll(first, 4, 0), second))
            even, odd = jnp.concatenate(even, axis=0), jnp.concatenate(odd, axis=0)
            out[2 * g, i * 16 : i * 16 + 16] = even
            out[2 * g + 1, i * 16 : i * 16 + 16] = odd
            if g == 2:
                left[i * 16 : i * 16 + 16] = even[:, :256].astype(BF16)
                right[i * 16 : i * 16 + 16] = even[:, 256:].astype(BF16)


def project(blocks, weight):
    half = jax.ShapeDtypeStruct((128, 256), BF16)
    return pl.pallas_call(
        project_body,
        out_shape=[jax.ShapeDtypeStruct((8, 128, 512), F32), half, half],
        in_specs=[VMEM] * 9,
        out_specs=[VMEM] * 3,
        compiler_params=params(),
        name="project",
    )(*blocks, weight)


def finish_body(place, own, left, right, orders, out):
    x, y, core, z = place[2], place[3] * 2 + place[5], place[6], place[4]
    lane = lanes()
    order = jnp.zeros((GROUP, DH), F32)
    for block in range(4):
        dy = (2 * (z & 1) + block // 2) ^ y
        tile = orders[((block % 2) ^ core) * 4 + dy].astype(F32)
        order = jnp.where(lane >> 5 == block, pltpu.roll(tile, 32 * block, 1), order)
    order = order.astype(jnp.int32)
    prompt, k = order >> 2, order & 3
    block = lane >> 5
    far = block & 1
    dx = (prompt >> 1) ^ x
    dy = (2 * (prompt & 1) + (block >> 1)) ^ y
    first = jnp.where(far == 0, dx, dy)
    second = jnp.where(far == 0, dy, dx)
    source = ((far ^ core) * 16 + second * 4 + first) * 4 + k
    row = lax.broadcasted_iota(jnp.int32, (128, 128), 0)
    pick = (row == source[0:1]).astype(F32).astype(BF16)
    total = own[...] + left[...].astype(F32) + right[...].astype(F32)
    out[...] = dot(pick, total.astype(BF16), (((0,), (0,)), ((), ()))).astype(BF16)


def finish(place, own, left, right, orders):
    return pl.pallas_call(
        finish_body,
        out_shape=jax.ShapeDtypeStruct((128, 512), BF16),
        in_specs=[SMEM] + [VMEM] * 4,
        out_specs=VMEM,
        compiler_params=params(),
        name="finish",
    )(place, own, left, right, orders)


def along(value, shift, k):
    return lax.ppermute(value, "batch", [(i, i ^ (k << shift)) for i in range(BATCH)])


def along_x(value, k):
    return along(value, 3, k)


def along_y(value, k):
    return along(value, 1, k)


def other_core(value):
    return along(value, 0, 1)


def turned(value, k, phase):
    pairs = [(i, i ^ (k << (3 if (i & 1) == phase else 1))) for i in range(BATCH)]
    return lax.ppermute(value, "batch", pairs)


def up(value):
    return lax.ppermute(value, "head", [(i, (i + 1) % HEADS) for i in range(HEADS)])


def down(value):
    return lax.ppermute(value, "head", [(i, (i - 1) % HEADS) for i in range(HEADS)])


def shards(queries, new_kv, prefix_kv, suffix_kv, page_table, suffix_len, prompt_of, out_weight):
    me = lax.axis_index("batch")
    z = lax.axis_index("head")
    x, y, core = me // 8, (me // 2) % 4, me % 2
    place = [8 * x + 4 * (y // 2), me * 256, x, y // 2, z, y % 2, core]
    place = jnp.stack(place).astype(jnp.int32)

    prefix_other = other_core(prefix_kv)

    q = queries.reshape(32, GROUP, DH)
    sent = sort_queries(place, prompt_of, q)
    by_x = [sent[0]] + [along_x(sent[k], k) for k in (1, 2, 3)]
    same, other = regroup(place, by_x)
    from1, from3, from2 = along_y(same, 1), along_y(other, 3), along_y(other, 2)
    orders = jnp.stack([same[16], from1[16], from2[16], from3[16]])
    orders = jnp.concatenate([orders, other_core(orders)], axis=0)

    suffix = suffix_parts(place, prompt_of, page_table, suffix_len, q, new_kv, suffix_kv)
    near = [suffix[0]] + [along_x(suffix[k], k) for k in (1, 2, 3)]
    far = along_y(jnp.concatenate([a[4:] for a in near], axis=0), 2)

    message = along_y(prefix_send(from1, from3, prefix_kv, prefix_other), 1)
    mine, masses = prefix_keep(same, from2, prefix_kv, prefix_other)
    attended = combine(place, mine, masses, message, near, far)

    parts = [attended] + [turned(attended, k, 0) for k in (1, 2, 3)]
    ring0 = jnp.concatenate(parts, axis=0)
    ring1, ring3 = turned(ring0, 1, 1), turned(ring0, 3, 1)
    ring2 = jnp.concatenate([turned(ring3[:64], 1, 1), turned(ring1[64:], 3, 1)], axis=0)
    mine_all = [ring0, ring1, ring2, ring3]
    blocks = mine_all + [other_core(a) for a in mine_all]

    partial, left, right = project(blocks, out_weight)
    from_up, from_down = down(left), up(right)
    low = jnp.concatenate([partial[5][:, :256] + from_up.astype(F32), partial[5][:, 256:]], axis=1)
    high = jnp.concatenate([partial[3][:, :256], partial[3][:, 256:] + from_down.astype(F32)], axis=1)
    from_up, from_down = down(low.astype(BF16)), up(high.astype(BF16))
    for step in (2, 1):
        low = partial[8 - step] + from_up.astype(F32)
        high = partial[step] + from_down.astype(F32)
        from_up, from_down = down(low.astype(BF16)), up(high.astype(BF16))

    return finish(place, partial[0], from_up, from_down, orders)


def solution(mesh):
    placed = (
        P("batch", "head"),
        P(None, "batch", "head"),
        P(None, "batch", "head"),
        P(None, "batch", None, "head"),
        P("batch", None),
        P("batch"),
        P("batch"),
        P("head", "batch"),
    )
    return jax.shard_map(
        shards, mesh=mesh, in_specs=placed, out_specs=P("head", "batch"), check_vma=False
    )
```

```python
import jax
import jax.numpy as jnp
from jax import lax
from jax.experimental import pallas as pl
from jax.experimental.pallas import tpu as pltpu
from jax.sharding import PartitionSpec as P

DH = 128
GROUP = 16
SCALE = DH**-0.5
LOG2E = 1.4426950408889634
BATCH = 32
HEADS = 8
VMEM = pl.BlockSpec(memory_space=pltpu.VMEM)
SMEM = pl.BlockSpec(memory_space=pltpu.SMEM)
F32 = jnp.float32
BF16 = jnp.bfloat16
NT = (((1,), (1,)), ((), ()))
NN = (((1,), (0,)), ((), ()))


ANY = pl.BlockSpec(memory_space=pl.ANY)


def params(mib=16):
    return pltpu.CompilerParams(vmem_limit_bytes=mib * 1024 * 1024)


def dot(a, b, dims=NN):
    return lax.dot_general(a, b, dims, preferred_element_type=F32)


def lanes():
    return lax.broadcasted_iota(jnp.int32, (GROUP, DH), 1)


def split_tile(tile, step):
    high = tile.astype(BF16).astype(F32)
    rest = tile - high
    middle = rest.astype(BF16).astype(F32)
    low = rest - middle
    joined = high + pltpu.roll(middle, step, 1) + pltpu.roll(low, 2 * step, 1)
    return joined.astype(BF16)


def join_tile(tile, step):
    wide = tile.astype(F32)
    return (wide + pltpu.roll(wide, DH - step, 1)) + pltpu.roll(wide, DH - 2 * step, 1)


def sort_body(place, prompt_in, q_in, o0, o1, o2, o3, q_out, prompt, q, wide, held, seen, sems):
    copies = [
        pltpu.make_async_copy(prompt_in, prompt, sems.at[0]),
        pltpu.make_async_copy(q_in, q, sems.at[1]),
    ]
    for copy in copies:
        copy.start()
    for copy in copies:
        copy.wait()
    lane = lanes()
    tile = jnp.zeros((GROUP, DH), F32)
    for p in range(8):
        seen[p] = 0
    for h in range(GROUP):
        wide[:, h, :] = q[:, h * DH : (h + 1) * DH].astype(F32)
    for r in range(32):
        p = prompt[r]
        k = seen[p]
        seen[p] = k + 1
        row = wide[r].astype(BF16)
        q_out[r] = row
        held[(4 * p + k) ^ place[0]] = row
        tile = jnp.where(lane == r, (4 * p + k).astype(F32), tile)
    for i, out in enumerate((o0, o1, o2, o3)):
        out[0:8] = held[8 * i : 8 * i + 8]
        out[8] = tile.astype(BF16)


def sort_queries(place, prompt, q):
    out = jax.ShapeDtypeStruct((9, GROUP, DH), BF16)
    return pl.pallas_call(
        sort_body,
        out_shape=[out] * 4 + [jax.ShapeDtypeStruct((32, GROUP, DH), BF16)],
        in_specs=[SMEM, ANY, ANY],
        out_specs=[VMEM] * 5,
        scratch_shapes=[
            pltpu.SMEM((32,), jnp.int32),
            pltpu.VMEM((32, GROUP * DH), BF16),
            pltpu.VMEM((32, GROUP, DH), F32),
            pltpu.VMEM((32, GROUP, DH), BF16),
            pltpu.SMEM((8,), jnp.int32),
            pltpu.SemaphoreType.DMA((2,)),
        ],
        compiler_params=params(),
        name="sort_queries",
    )(place, prompt, q)


def regroup_body(place, a0, a1, a2, a3, same, other):
    for i, a in enumerate((a0, a1, a2, a3)):
        same[4 * i : 4 * i + 4] = a[0:4]
        other[4 * i : 4 * i + 4] = a[4:8]

    for i, a in enumerate((a0, a1, a2, a3)):

        @pl.when(place[2] ^ (place[4] >> 1) == i)
        def _(a=a):
            same[16] = a[8]
            other[16] = a[8]


def regroup(place, parts):
    out = jax.ShapeDtypeStruct((17, GROUP, DH), BF16)
    return pl.pallas_call(
        regroup_body,
        out_shape=[out, out],
        in_specs=[SMEM] + [VMEM] * 4,
        out_specs=[VMEM] * 2,
        compiler_params=params(),
        name="regroup",
    )(place, *parts)


def suffix_body(
    place, prompt_in, table_in, length_in, q, new_in, pool_in, o0, o1, o2, o3,
    prompt, table, length, new, pool, scores, weights, held, tiles, seen, sems,
):
    pairs = [
        (pool_in.at[0], pool.at[0]),
        (table_in, table),
        (length_in, length),
        (new_in, new),
        (prompt_in, prompt),
        (pool_in.at[1], pool.at[1]),
    ]
    copies = [pltpu.make_async_copy(a, b, sems.at[i]) for i, (a, b) in enumerate(pairs)]
    for copy in copies:
        copy.start()
    for copy in copies[:5]:
        copy.wait()
    lane = lanes()
    base = place[1]
    for n in range(32):
        keys = jnp.concatenate([pool[0, table[n, j] - base] for j in range(8)], axis=0)
        s = dot(q[n], keys, NT) * SCALE
        scores[n] = jnp.where(lane < length[n], s, -1e30)
    own_keys = new[0].astype(F32)
    own_values = new[1].astype(F32)
    own = jnp.stack(
        [
            jnp.sum(q[n].astype(F32) * own_keys[n : n + 1], axis=1, keepdims=True)
            for n in range(32)
        ]
    ) * SCALE
    s = scores[...]
    peak = jnp.maximum(jnp.max(s, axis=2, keepdims=True), own)
    w = jnp.exp(s - peak)
    own_weight = jnp.exp(own - peak)
    total = jnp.sum(w, axis=2, keepdims=True) + own_weight
    weights[...] = w.astype(BF16)
    own_weight = own_weight.astype(BF16).astype(F32)
    mass = peak + jnp.log(total)
    inverse = 1.0 / total
    tiles[...] = jnp.zeros_like(tiles)
    copies[5].wait()
    for p in range(8):
        seen[p] = 0
    for n in range(32):
        values = jnp.concatenate([pool[1, table[n, j] - base] for j in range(8)], axis=0)
        mixed = dot(weights[n], values) + own_weight[n] * own_values[n : n + 1]
        p = prompt[n]
        k = seen[p]
        seen[p] = k + 1
        slot = (4 * p + k) ^ place[0]
        held[slot] = (mixed * inverse[n]).astype(BF16)
        at = slot >> 3
        tiles[at] = jnp.where(lane == (slot & 7), mass[n], tiles[at])
    for i, out in enumerate((o0, o1, o2, o3)):
        out[0:8] = held[8 * i : 8 * i + 8]
        out[8] = split_tile(tiles[i], 8)


def suffix_parts(place, prompt, table, length, q, new, pool):
    out = jax.ShapeDtypeStruct((9, GROUP, DH), BF16)
    return pl.pallas_call(
        suffix_body,
        out_shape=[out] * 4,
        in_specs=[SMEM, ANY, ANY, ANY, VMEM, ANY, ANY],
        out_specs=[VMEM] * 4,
        scratch_shapes=[
            pltpu.SMEM((32,), jnp.int32),
            pltpu.SMEM((32, 8), jnp.int32),
            pltpu.SMEM((32,), jnp.int32),
            pltpu.VMEM((2, 32, DH), BF16),
            pltpu.VMEM((2, 256, GROUP, DH), BF16),
            pltpu.VMEM((32, GROUP, DH), F32),
            pltpu.VMEM((32, GROUP, DH), BF16),
            pltpu.VMEM((32, GROUP, DH), BF16),
            pltpu.VMEM((4, GROUP, DH), F32),
            pltpu.SMEM((8,), jnp.int32),
            pltpu.SemaphoreType.DMA((6,)),
        ],
        compiler_params=params(),
        cost_estimate=pl.CostEstimate(flops=40_000_000, bytes_accessed=3_000_000, transcendentals=70000),
        name="suffix_parts",
    )(place, prompt, table, length, q, new, pool)


ROWS = 128


def prefix_part(q, kv):
    s = dot(q, kv[0], NT)
    peak = jnp.max(s, axis=1, keepdims=True)
    w = jnp.exp2((s - peak) * (SCALE * LOG2E))
    return dot(w.astype(BF16), kv[1]), peak * SCALE, jnp.sum(w, axis=1, keepdims=True)


def prefix_block(q, kv0, kv1):
    mixed0, peak0, total0 = prefix_part(q, kv0)
    mixed1, peak1, total1 = prefix_part(q, kv1)
    top = jnp.maximum(peak0, peak1)
    f0, f1 = jnp.exp(peak0 - top), jnp.exp(peak1 - top)
    total = total0 * f0 + total1 * f1
    return (mixed0 * f0 + mixed1 * f1) * (1.0 / total), top + jnp.log(total)


def prefix_send_body(qa, qb, kv0, kv1, out):
    lane = lanes()
    tile = jnp.zeros((GROUP, DH), F32)
    count = ROWS // GROUP
    for half, q in enumerate((qa, qb)):
        for i in range(256 // ROWS):
            rows = q[i * count : (i + 1) * count].reshape(ROWS, DH)
            mixed, mass = prefix_block(rows, kv0, kv1)
            at = half * 16 + i * count
            out[at : at + count] = mixed.reshape(count, GROUP, DH).astype(BF16)
            for n in range(count):
                tile = jnp.where(lane == at + n, mass[n * GROUP : (n + 1) * GROUP], tile)
    out[32] = split_tile(tile, 32)


def prefix_keep_body(qa, qb, kv0, kv1, out, masses):
    count = ROWS // GROUP
    for half, q in enumerate((qa, qb)):
        for i in range(256 // ROWS):
            rows = q[i * count : (i + 1) * count].reshape(ROWS, DH)
            mixed, mass = prefix_block(rows, kv0, kv1)
            at = half * 16 + i * count
            out[at : at + count] = mixed.reshape(count, GROUP, DH)
            masses[at : at + count] = jnp.broadcast_to(mass, (ROWS, DH)).reshape(count, GROUP, DH)


PREFIX_COST = pl.CostEstimate(
    flops=4 * 512 * 4096 * 128, bytes_accessed=2_500_000, transcendentals=512 * 4096
)


def prefix_send(qa, qb, kv0, kv1):
    return pl.pallas_call(
        prefix_send_body,
        out_shape=jax.ShapeDtypeStruct((33, GROUP, DH), BF16),
        in_specs=[VMEM] * 4,
        out_specs=VMEM,
        compiler_params=params(24),
        cost_estimate=PREFIX_COST,
        name="prefix_send",
    )(qa, qb, kv0, kv1)


def prefix_keep(qa, qb, kv0, kv1):
    out = jax.ShapeDtypeStruct((32, GROUP, DH), F32)
    return pl.pallas_call(
        prefix_keep_body,
        out_shape=[out, out],
        in_specs=[VMEM] * 4,
        out_specs=[VMEM, VMEM],
        compiler_params=params(24),
        cost_estimate=PREFIX_COST,
        name="prefix_keep",
    )(qa, qb, kv0, kv1)


def combine_body(place, mine, masses, message, s0, s1, s2, s3, far, out, held):
    x, y_high, z = place[2], place[3], place[4]
    theirs = join_tile(message[32], 32)
    near = [join_tile(s[8], 8) for s in (s0, s1, s2, s3)]
    across = [join_tile(far[5 * i + 4], 8) for i in range(4)]
    for g in range(2):
        for kx in range(4):
            for k in range(4):
                n = g * 16 + kx * 4 + k
                a, la = mine[n], masses[n]
                b = message[n].astype(F32)
                lb = jnp.broadcast_to(theirs[:, n : n + 1], (GROUP, DH))
                if g == 0:
                    s = (s0, s1, s2, s3)[kx][k].astype(F32)
                    ls = jnp.broadcast_to(near[kx][:, k : k + 1], (GROUP, DH))
                else:
                    s = far[5 * kx + k].astype(F32)
                    ls = jnp.broadcast_to(across[kx][:, 4 + k : 5 + k], (GROUP, DH))
                top = jnp.maximum(jnp.maximum(la, lb), ls)
                ea, eb, es = jnp.exp(la - top), jnp.exp(lb - top), jnp.exp(ls - top)
                row = (ea * a + eb * b + es * s) / (ea + eb + es)
                target = (x ^ kx) * 2 + (y_high ^ g)
                held[((target - z) & 7) * 4 + k] = row
    for h in range(GROUP):
        out[:, h * DH : (h + 1) * DH] = held[:, h, :].astype(BF16)


def combine(place, mine, masses, message, near, far):
    return pl.pallas_call(
        combine_body,
        out_shape=jax.ShapeDtypeStruct((32, GROUP * DH), BF16),
        in_specs=[SMEM] + [VMEM] * 8,
        out_specs=VMEM,
        scratch_shapes=[pltpu.VMEM((32, GROUP, DH), F32)],
        compiler_params=params(),
        name="combine",
    )(place, mine, masses, message, *near, far)


def by_target(total):
    low = lax.broadcasted_iota(jnp.int32, (8, total.shape[1]), 0) < 4
    chunks = []
    for g in range(4):
        even, odd = [], []
        for j in (0, 2):
            first = total[j * 32 + g * 8 : j * 32 + g * 8 + 8]
            second = total[(j + 1) * 32 + g * 8 : (j + 1) * 32 + g * 8 + 8]
            even.append(jnp.where(low, first, pltpu.roll(second, 4, 0)))
            odd.append(jnp.where(low, pltpu.roll(first, 4, 0), second))
        chunks += [jnp.concatenate(even, axis=0), jnp.concatenate(odd, axis=0)]
    return chunks


def project_body(count, *refs):
    blocks, weights, out = refs[:count], refs[count : count + 2], refs[count + 2]
    for i, block in enumerate(blocks):
        for side, weight in enumerate(weights):
            for d, chunk in enumerate(by_target(dot(block[...], weight[...]))):
                out[d, i * 16 : i * 16 + 16, side * 512 : side * 512 + 512] = chunk


def project(blocks, weights):
    count = len(blocks)
    return pl.pallas_call(
        lambda *refs: project_body(count, *refs),
        out_shape=jax.ShapeDtypeStruct((8, 16 * count, 1024), F32),
        in_specs=[VMEM] * (count + 2),
        out_specs=VMEM,
        compiler_params=params(),
        cost_estimate=pl.CostEstimate(
            flops=count * 2 * 128 * 2048 * 1024, bytes_accessed=4_500_000, transcendentals=0
        ),
        name="project",
    )(*blocks, *weights)


def last_body(block, w0, w1, first, second, up, down, up4, down4, keep):
    for side, weight in enumerate((w0, w1)):
        columns = slice(side * 512, side * 512 + 512)
        chunks = by_target(dot(block[...], weight[...]))
        for d, chunk in enumerate(chunks):
            whole = jnp.concatenate([first[d, :, columns], second[d, :, columns], chunk], axis=0)
            if d in (0, 2, 6):
                keep[(0, 2, 6).index(d), :, columns] = whole
            elif d in (3, 1):
                up[(3, 1).index(d), :, columns] = whole.astype(BF16)
            elif d in (5, 7):
                down[(5, 7).index(d), :, columns] = whole.astype(BF16)
            elif side == 0:
                up4[...] = whole.astype(BF16)
            else:
                down4[...] = whole.astype(BF16)


def project_last(block, weights, first, second):
    pair = jax.ShapeDtypeStruct((2, 64, 1024), BF16)
    half = jax.ShapeDtypeStruct((64, 512), BF16)
    return pl.pallas_call(
        last_body,
        out_shape=[pair, pair, half, half, jax.ShapeDtypeStruct((3, 64, 1024), F32)],
        in_specs=[VMEM] * 5,
        out_specs=[VMEM] * 5,
        compiler_params=params(),
        name="project_last",
    )(block, *weights, first, second)


def middle_body(keep, below, above, below4, above4, up, down):
    u = keep[1] + below[0].astype(F32)
    up[:, :512] = (u[:, :512] + below4[...].astype(F32)).astype(BF16)
    up[:, 512:] = u[:, 512:].astype(BF16)
    d = keep[2] + above[0].astype(F32)
    down[:, :512] = d[:, :512].astype(BF16)
    down[:, 512:] = (d[:, 512:] + above4[...].astype(F32)).astype(BF16)


def middle(keep, below, above, below4, above4):
    out = jax.ShapeDtypeStruct((64, 1024), BF16)
    return pl.pallas_call(
        middle_body,
        out_shape=[out, out],
        in_specs=[VMEM] * 5,
        out_specs=[VMEM] * 2,
        compiler_params=params(),
        name="middle",
    )(keep, below, above, below4, above4)


def total_body(keep, below, above, below2, above2, own, other):
    near = keep[0] + below[1].astype(F32) + above[1].astype(F32)
    total = (near + below2[...].astype(F32) + above2[...].astype(F32)).astype(BF16)
    own[...] = total[:, :512]
    other[...] = total[:, 512:]


def total(keep, below, above, below2, above2):
    out = jax.ShapeDtypeStruct((64, 512), BF16)
    return pl.pallas_call(
        total_body,
        out_shape=[out, out],
        in_specs=[VMEM] * 5,
        out_specs=[VMEM] * 2,
        compiler_params=params(),
        name="total",
    )(keep, below, above, below2, above2)


def order_body(place, orders, pick):
    x, y, core, z = place[2], place[3] * 2 + place[5], place[6], place[4]
    lane = lanes()
    order = jnp.zeros((GROUP, DH), F32)
    for block in range(4):
        dy = (2 * (z & 1) + block // 2) ^ y
        tile = orders[((block % 2) ^ core) * 4 + dy].astype(F32)
        order = jnp.where(lane >> 5 == block, pltpu.roll(tile, 32 * block, 1), order)
    order = order.astype(jnp.int32)
    prompt, k = order >> 2, order & 3
    block = lane >> 5
    far = block & 1
    dx = (prompt >> 1) ^ x
    dy = (2 * (prompt & 1) + (block >> 1)) ^ y
    first = jnp.where(far == 0, dx, dy)
    second = jnp.where(far == 0, dy, dx)
    second = jnp.where(second >= 2, 5 - second, second)
    source = ((far ^ core) * 16 + second * 4 + first) * 4 + k
    row = lax.broadcasted_iota(jnp.int32, (128, 128), 0)
    pick[...] = (row == source[0:1]).astype(F32).astype(BF16)


def order_rows(place, orders):
    return pl.pallas_call(
        order_body,
        out_shape=jax.ShapeDtypeStruct((128, 128), BF16),
        in_specs=[SMEM, VMEM],
        out_specs=VMEM,
        compiler_params=params(),
        name="order_rows",
    )(place, orders)


def finish_body(own, other, pick, out):
    dims = (((0,), (0,)), ((), ()))
    mixed = dot(pick[0:64], own[...], dims) + dot(pick[64:128], other[...], dims)
    out[...] = mixed.astype(BF16)


def finish(own, other, pick):
    return pl.pallas_call(
        finish_body,
        out_shape=jax.ShapeDtypeStruct((128, 512), BF16),
        in_specs=[VMEM] * 3,
        out_specs=VMEM,
        compiler_params=params(),
        name="finish",
    )(own, other, pick)


def along(value, shift, k):
    return lax.ppermute(value, "batch", [(i, i ^ (k << shift)) for i in range(BATCH)])


def along_x(value, k):
    return along(value, 3, k)


def along_y(value, k):
    return along(value, 1, k)


def other_core(value):
    return along(value, 0, 1)


def turned(value, k, phase):
    pairs = [(i, i ^ (k << (3 if (i & 1) == phase else 1))) for i in range(BATCH)]
    return lax.ppermute(value, "batch", pairs)


def along_z(value, k):
    return lax.ppermute(value, "head", [(i, (i + k) % HEADS) for i in range(HEADS)])


def shards(queries, new_kv, prefix_kv, suffix_kv, page_table, suffix_len, prompt_of, out_weight):
    me = lax.axis_index("batch")
    z = lax.axis_index("head")
    x, y, core = me // 8, (me // 2) % 4, me % 2
    place = [8 * x + 4 * (y // 2), me * 256, x, y // 2, z, y % 2, core]
    place = jnp.stack(place).astype(jnp.int32)

    prefix_other = other_core(prefix_kv)
    weights = [out_weight, other_core(out_weight)]

    *sent, q = sort_queries(place, prompt_of, queries)
    by_x = [sent[0]] + [along_x(sent[k], k) for k in (1, 2, 3)]
    same, other = regroup(place, by_x)
    from1, from3, from2 = along_y(same, 1), along_y(other, 3), along_y(other, 2)

    q, same = lax.optimization_barrier((q, same))
    suffix = suffix_parts(place, prompt_of, page_table, suffix_len, q, new_kv, suffix_kv)
    near = [suffix[0]] + [along_x(suffix[k], k) for k in (1, 2, 3)]
    far = along_y(jnp.concatenate([a[4:] for a in near], axis=0), 2)

    message = along_y(prefix_send(from1, from3, prefix_kv, prefix_other), 1)
    mine, masses = prefix_keep(same, from2, prefix_kv, prefix_other)
    attended = combine(place, mine, masses, message, near, far)

    orders = jnp.stack([same[16], from1[16], from2[16], from3[16]])
    orders = jnp.concatenate([orders, other_core(orders)], axis=0)
    pick = order_rows(place, orders)

    parts = [attended] + [turned(attended, k, 0) for k in (1, 2, 3)]
    ring0 = jnp.concatenate(parts, axis=0)
    ring1, ring3 = turned(ring0, 1, 1), turned(ring0, 3, 1)
    ring2 = jnp.concatenate([turned(ring3[:64], 1, 1), turned(ring1[64:], 3, 1)], axis=0)
    first = project([ring0], weights)
    second = project([ring1, ring3], weights)
    up, down, up4, down4, keep = project_last(ring2, weights, first, second)

    below4, above4 = along_z(up4, 2), along_z(down4, -2)
    below, above = along_z(up, 1), along_z(down, -1)
    up2, down2 = middle(keep, below, above, below4, above4)
    below2, above2 = along_z(up2, 2), along_z(down2, -2)
    own, other = total(keep, below, above, below2, above2)
    return finish(own, other_core(other), pick)


def solution(mesh):
    placed = (
        P("batch", "head"),
        P(None, "batch", "head"),
        P(None, "batch", "head"),
        P(None, "batch", None, "head"),
        P("batch", None),
        P("batch"),
        P("batch"),
        P("head", "batch"),
    )
    return jax.shard_map(
        shards, mesh=mesh, in_specs=placed, out_specs=P("head", "batch"), check_vma=False
    )
```

```python
import jax
import jax.numpy as jnp
from jax import lax
from jax.experimental import pallas as pl
from jax.experimental.pallas import tpu as pltpu
from jax.sharding import PartitionSpec as P

DH = 128
GROUP = 16
SCALE = DH**-0.5
LOG2E = 1.4426950408889634
BATCH = 32
HEADS = 8
VMEM = pl.BlockSpec(memory_space=pltpu.VMEM)
SMEM = pl.BlockSpec(memory_space=pltpu.SMEM)
F32 = jnp.float32
BF16 = jnp.bfloat16
NT = (((1,), (1,)), ((), ()))
NN = (((1,), (0,)), ((), ()))


ANY = pl.BlockSpec(memory_space=pl.ANY)


def params(mib=16):
    return pltpu.CompilerParams(vmem_limit_bytes=mib * 1024 * 1024)


def dot(a, b, dims=NN):
    return lax.dot_general(a, b, dims, preferred_element_type=F32)


def lanes():
    return lax.broadcasted_iota(jnp.int32, (GROUP, DH), 1)


def split_tile(tile, step):
    high = tile.astype(BF16).astype(F32)
    rest = tile - high
    middle = rest.astype(BF16).astype(F32)
    low = rest - middle
    joined = high + pltpu.roll(middle, step, 1) + pltpu.roll(low, 2 * step, 1)
    return joined.astype(BF16)


def join_tile(tile, step):
    wide = tile.astype(F32)
    return (wide + pltpu.roll(wide, DH - step, 1)) + pltpu.roll(wide, DH - 2 * step, 1)


def local_body(
    place, q_in, prompt_in, table_in, length_in, new_in, pool_in, o0, o1, o2, o3,
    q, prompt, table, length, new, pool, wide, scores, weights, slots, sems,
):
    pairs = [
        (q_in, q),
        (prompt_in, prompt),
        (table_in, table),
        (length_in, length),
        (new_in, new),
        (pool_in.at[0], pool.at[0]),
        (pool_in.at[1], pool.at[1]),
    ]
    copies = [pltpu.make_async_copy(a, b, sems.at[i]) for i, (a, b) in enumerate(pairs)]
    for copy in copies:
        copy.start()
    outs = (o0, o1, o2, o3)
    lane = lanes()
    copies[0].wait()
    for h in range(GROUP):
        wide[:, h, :] = q[:, h * DH : (h + 1) * DH].astype(F32)
    copies[1].wait()
    for p in range(8):
        slots[32 + p] = 0
    order = jnp.zeros((GROUP, DH), F32)
    for n in range(32):
        p = prompt[n]
        k = slots[32 + p]
        slots[32 + p] = k + 1
        slots[n] = (4 * p + k) ^ place[0]
        order = jnp.where(lane == n, (4 * p + k).astype(F32), order)
    for copy in copies[2:6]:
        copy.wait()
    base = place[1]
    for n in range(32):
        keys = jnp.concatenate([pool[0, table[n, j] - base] for j in range(8)], axis=0)
        s = dot(wide[n].astype(BF16), keys, NT) * SCALE
        scores[n] = jnp.where(lane < length[n], s, -1e30)
    own_keys = new[0].astype(F32)
    own_values = new[1].astype(F32)
    own = jnp.stack(
        [jnp.sum(wide[n] * own_keys[n : n + 1], axis=1, keepdims=True) for n in range(32)]
    ) * SCALE
    s = scores[...]
    peak = jnp.maximum(jnp.max(s, axis=2, keepdims=True), own)
    w = jnp.exp(s - peak)
    own_weight = jnp.exp(own - peak)
    total = jnp.sum(w, axis=2, keepdims=True) + own_weight
    weights[...] = w.astype(BF16)
    own_weight = own_weight.astype(BF16).astype(F32)
    mass = peak + jnp.log(total)
    inverse = 1.0 / total
    copies[6].wait()
    for n in range(32):
        values = jnp.concatenate([pool[1, table[n, j] - base] for j in range(8)], axis=0)
        mixed = dot(weights[n], values) + own_weight[n] * own_values[n : n + 1]
        scores[slots[n]] = mixed * inverse[n]
    held = [jnp.zeros((GROUP, DH), F32) for _ in range(4)]
    for n in range(32):
        slot = slots[n]
        weights[slot] = wide[n].astype(BF16)
        for i in range(4):
            held[i] = jnp.where(lane + 8 * i == slot, jnp.where(lane < 8, mass[n], 0.0), held[i])
    for i, out in enumerate(outs):
        out[0:8] = weights[8 * i : 8 * i + 8]
        out[8] = order.astype(BF16)
        out[9:17] = scores[8 * i : 8 * i + 8].astype(BF16)
        out[17] = split_tile(jnp.where(lane < 8, held[i], 0.0), 8)


def local_parts(place, q, prompt, table, length, new, pool):
    out = jax.ShapeDtypeStruct((18, GROUP, DH), BF16)
    return pl.pallas_call(
        local_body,
        out_shape=[out] * 4,
        in_specs=[SMEM] + [ANY] * 6,
        out_specs=[VMEM] * 4,
        scratch_shapes=[
            pltpu.VMEM((32, GROUP * DH), BF16),
            pltpu.SMEM((32,), jnp.int32),
            pltpu.SMEM((32, 8), jnp.int32),
            pltpu.SMEM((32,), jnp.int32),
            pltpu.VMEM((2, 32, DH), BF16),
            pltpu.VMEM((2, 256, GROUP, DH), BF16),
            pltpu.VMEM((32, GROUP, DH), F32),
            pltpu.VMEM((32, GROUP, DH), F32),
            pltpu.VMEM((32, GROUP, DH), BF16),
            pltpu.SMEM((40,), jnp.int32),
            pltpu.SemaphoreType.DMA((7,)),
        ],
        compiler_params=params(56),
        name="local_parts",
    )(place, q, prompt, table, length, new, pool)


def regroup_body(place, a0, a1, a2, a3, same, other, far):
    for i, a in enumerate((a0, a1, a2, a3)):
        same[4 * i : 4 * i + 4] = a[0:4]
        other[4 * i : 4 * i + 4] = a[4:8]
        far[5 * i : 5 * i + 5] = a[13:18]

        @pl.when(place[2] ^ (place[4] >> 1) == i)
        def _(a=a):
            same[16] = a[8]
            other[16] = a[8]


def regroup(place, parts):
    out = jax.ShapeDtypeStruct((17, GROUP, DH), BF16)
    return pl.pallas_call(
        regroup_body,
        out_shape=[out, out, jax.ShapeDtypeStruct((20, GROUP, DH), BF16)],
        in_specs=[SMEM] + [VMEM] * 4,
        out_specs=[VMEM] * 3,
        compiler_params=params(),
        name="regroup",
    )(place, *parts)


ROWS = 128


def prefix_part(q, kv):
    s = dot(q, kv[0], NT)
    peak = jnp.max(s, axis=1, keepdims=True)
    w = jnp.exp2((s - peak) * (SCALE * LOG2E))
    return dot(w.astype(BF16), kv[1]), peak * SCALE, jnp.sum(w, axis=1, keepdims=True)


def prefix_block(q, kv0, kv1):
    mixed0, peak0, total0 = prefix_part(q, kv0)
    mixed1, peak1, total1 = prefix_part(q, kv1)
    top = jnp.maximum(peak0, peak1)
    f0, f1 = jnp.exp(peak0 - top), jnp.exp(peak1 - top)
    total = total0 * f0 + total1 * f1
    return (mixed0 * f0 + mixed1 * f1) * (1.0 / total), top + jnp.log(total)


COUNT = ROWS // GROUP


def prefix_send_body(qa, qb, kv0, kv1, after, out):
    lane = lanes()
    tile = jnp.zeros((GROUP, DH), F32)
    for half, q in enumerate((qa, qb)):
        for i in range(256 // ROWS):
            rows = q[i * COUNT : (i + 1) * COUNT].reshape(ROWS, DH)
            mixed, mass = prefix_block(rows, kv0, kv1)
            at = half * 16 + i * COUNT
            out[at : at + COUNT] = mixed.reshape(COUNT, GROUP, DH).astype(BF16)
            for n in range(COUNT):
                tile = jnp.where(lane == at + n, mass[n * GROUP : (n + 1) * GROUP], tile)
    out[32] = split_tile(tile, 32)


def prefix_keep_body(q, kv0, kv1, out, masses):
    for i in range(256 // ROWS):
        rows = q[i * COUNT : (i + 1) * COUNT].reshape(ROWS, DH)
        mixed, mass = prefix_block(rows, kv0, kv1)
        at = i * COUNT
        out[at : at + COUNT] = mixed.reshape(COUNT, GROUP, DH)
        masses[at : at + COUNT] = jnp.broadcast_to(mass, (ROWS, DH)).reshape(COUNT, GROUP, DH)


def prefix_cost(rows):
    return pl.CostEstimate(
        flops=4 * rows * 4096 * 128, bytes_accessed=2_500_000, transcendentals=rows * 4096
    )


def prefix_send(qa, qb, kv0, kv1, after):
    return pl.pallas_call(
        prefix_send_body,
        out_shape=jax.ShapeDtypeStruct((33, GROUP, DH), BF16),
        in_specs=[VMEM] * 4 + [ANY],
        out_specs=VMEM,
        compiler_params=params(24),
        cost_estimate=prefix_cost(512),
        name="prefix_send",
    )(qa, qb, kv0, kv1, after)


def prefix_keep(q, kv0, kv1):
    out = jax.ShapeDtypeStruct((16, GROUP, DH), F32)
    return pl.pallas_call(
        prefix_keep_body,
        out_shape=[out, out],
        in_specs=[VMEM] * 3,
        out_specs=[VMEM, VMEM],
        compiler_params=params(24),
        cost_estimate=prefix_cost(256),
        name="prefix_keep",
    )(q, kv0, kv1)


def combine_body(
    place, own, own_masses, cross, cross_masses, message, s0, s1, s2, s3, far, out, held
):
    x, y_high, z = place[2], place[3], place[4]
    theirs = join_tile(message[32], 32)
    near = [join_tile(s[17], 8) for s in (s0, s1, s2, s3)]
    across = [join_tile(far[5 * i + 4], 8) for i in range(4)]
    for g in range(2):
        for kx in range(4):
            for k in range(4):
                n = g * 16 + kx * 4 + k
                at = kx * 4 + k
                a, la = ((own, own_masses), (cross, cross_masses))[g]
                a, la = a[at], la[at]
                b = message[n].astype(F32)
                lb = jnp.broadcast_to(theirs[:, n : n + 1], (GROUP, DH))
                if g == 0:
                    s = (s0, s1, s2, s3)[kx][9 + k].astype(F32)
                    ls = jnp.broadcast_to(near[kx][:, k : k + 1], (GROUP, DH))
                else:
                    s = far[5 * kx + k].astype(F32)
                    ls = jnp.broadcast_to(across[kx][:, 4 + k : 5 + k], (GROUP, DH))
                top = jnp.maximum(jnp.maximum(la, lb), ls)
                ea, eb, es = jnp.exp(la - top), jnp.exp(lb - top), jnp.exp(ls - top)
                row = (ea * a + eb * b + es * s) / (ea + eb + es)
                target = (x ^ kx) * 2 + (y_high ^ g)
                held[((target - z) & 7) * 4 + k] = row
    for h in range(GROUP):
        out[:, h * DH : (h + 1) * DH] = held[:, h, :].astype(BF16)


def combine(place, own, cross, message, near, far):
    return pl.pallas_call(
        combine_body,
        out_shape=jax.ShapeDtypeStruct((32, GROUP * DH), BF16),
        in_specs=[SMEM] + [VMEM] * 10,
        out_specs=VMEM,
        scratch_shapes=[pltpu.VMEM((32, GROUP, DH), F32)],
        compiler_params=params(),
        name="combine",
    )(place, *own, *cross, message, *near, far)


def by_target(total):
    low = lax.broadcasted_iota(jnp.int32, (8, total.shape[1]), 0) < 4
    chunks = []
    for g in range(4):
        even, odd = [], []
        for j in (0, 2):
            first = total[j * 32 + g * 8 : j * 32 + g * 8 + 8]
            second = total[(j + 1) * 32 + g * 8 : (j + 1) * 32 + g * 8 + 8]
            even.append(jnp.where(low, first, pltpu.roll(second, 4, 0)))
            odd.append(jnp.where(low, pltpu.roll(first, 4, 0), second))
        chunks += [jnp.concatenate(even, axis=0), jnp.concatenate(odd, axis=0)]
    return chunks


def project_body(count, *refs):
    blocks, weights, out = refs[:count], refs[count : count + 2], refs[count + 2]
    for i, block in enumerate(blocks):
        for side, weight in enumerate(weights):
            for d, chunk in enumerate(by_target(dot(block[...], weight[...]))):
                out[d, i * 16 : i * 16 + 16, side * 512 : side * 512 + 512] = chunk


def project(blocks, weights):
    count = len(blocks)
    return pl.pallas_call(
        lambda *refs: project_body(count, *refs),
        out_shape=jax.ShapeDtypeStruct((8, 16 * count, 1024), F32),
        in_specs=[VMEM] * (count + 2),
        out_specs=VMEM,
        compiler_params=params(),
        cost_estimate=pl.CostEstimate(
            flops=count * 2 * 128 * 2048 * 1024, bytes_accessed=4_500_000, transcendentals=0
        ),
        name="project",
    )(*blocks, *weights)


def last_body(block, w0, w1, first, second, up, down, keep):
    for side, weight in enumerate((w0, w1)):
        columns = slice(side * 512, side * 512 + 512)
        chunks = by_target(dot(block[...], weight[...]))
        for d, chunk in enumerate(chunks):
            whole = jnp.concatenate([first[d, :, columns], second[d, :, columns], chunk], axis=0)
            if d in (0, 3, 5):
                keep[(0, 3, 5).index(d), :, columns] = whole
            elif d in (1, 6):
                up[2 * (1, 6).index(d) + side] = whole.astype(BF16)
            elif d in (7, 2):
                down[2 * (7, 2).index(d) + side] = whole.astype(BF16)
            elif side == 0:
                up[4] = whole.astype(BF16)
            else:
                down[4] = whole.astype(BF16)


def project_last(block, weights, first, second):
    out = jax.ShapeDtypeStruct((5, 64, 512), BF16)
    return pl.pallas_call(
        last_body,
        out_shape=[out, out, jax.ShapeDtypeStruct((3, 64, 1024), F32)],
        in_specs=[VMEM] * 5,
        out_specs=[VMEM] * 3,
        compiler_params=params(),
        name="project_last",
    )(block, *weights, first, second)


def middle_body(keep, below, above, up, down):
    far = below[4].astype(F32), above[4].astype(F32)
    up[:, :512] = (keep[1, :, :512] + above[2].astype(F32) + far[0]).astype(BF16)
    up[:, 512:] = (keep[1, :, 512:] + above[3].astype(F32)).astype(BF16)
    down[:, :512] = (keep[2, :, :512] + below[2].astype(F32)).astype(BF16)
    down[:, 512:] = (keep[2, :, 512:] + below[3].astype(F32) + far[1]).astype(BF16)


def middle(keep, below, above):
    out = jax.ShapeDtypeStruct((64, 1024), BF16)
    return pl.pallas_call(
        middle_body,
        out_shape=[out, out],
        in_specs=[VMEM] * 3,
        out_specs=[VMEM] * 2,
        compiler_params=params(),
        name="middle",
    )(keep, below, above)


def total_body(keep, below, above, below3, above3, own, other):
    for side, out in enumerate((own, other)):
        columns = slice(side * 512, side * 512 + 512)
        near = keep[0, :, columns] + below[side].astype(F32) + above[side].astype(F32)
        far = below3[:, columns].astype(F32) + above3[:, columns].astype(F32)
        out[...] = (near + far).astype(BF16)


def total(keep, below, above, below3, above3):
    out = jax.ShapeDtypeStruct((64, 512), BF16)
    return pl.pallas_call(
        total_body,
        out_shape=[out, out],
        in_specs=[VMEM] * 5,
        out_specs=[VMEM] * 2,
        compiler_params=params(),
        name="total",
    )(keep, below, above, below3, above3)


def order_body(place, orders, pick):
    x, y, core, z = place[2], place[3] * 2 + place[5], place[6], place[4]
    lane = lanes()
    order = jnp.zeros((GROUP, DH), F32)
    for block in range(4):
        dy = (2 * (z & 1) + block // 2) ^ y
        tile = orders[((block % 2) ^ core) * 4 + dy].astype(F32)
        order = jnp.where(lane >> 5 == block, pltpu.roll(tile, 32 * block, 1), order)
    order = order.astype(jnp.int32)
    prompt, k = order >> 2, order & 3
    block = lane >> 5
    far = block & 1
    dx = (prompt >> 1) ^ x
    dy = (2 * (prompt & 1) + (block >> 1)) ^ y
    first = jnp.where(far == 0, dx, dy)
    second = jnp.where(far == 0, dy, dx)
    first = jnp.where(first >= 2, 5 - first, first)
    second = jnp.where(second >= 2, 5 - second, second)
    source = ((far ^ core) * 16 + second * 4 + first) * 4 + k
    row = lax.broadcasted_iota(jnp.int32, (128, 128), 0)
    pick[...] = (row == source[0:1]).astype(F32).astype(BF16)


def order_rows(place, orders):
    return pl.pallas_call(
        order_body,
        out_shape=jax.ShapeDtypeStruct((128, 128), BF16),
        in_specs=[SMEM, VMEM],
        out_specs=VMEM,
        compiler_params=params(),
        name="order_rows",
    )(place, orders)


def finish_body(own, other, pick, out):
    dims = (((0,), (0,)), ((), ()))
    mixed = dot(pick[0:64], own[...], dims) + dot(pick[64:128], other[...], dims)
    out[...] = mixed.astype(BF16)


def finish(own, other, pick):
    return pl.pallas_call(
        finish_body,
        out_shape=jax.ShapeDtypeStruct((128, 512), BF16),
        in_specs=[VMEM] * 3,
        out_specs=VMEM,
        compiler_params=params(),
        name="finish",
    )(own, other, pick)


def along(value, shift, k):
    return lax.ppermute(value, "batch", [(i, i ^ (k << shift)) for i in range(BATCH)])


def along_x(value, k):
    return along(value, 3, k)


def along_y(value, k):
    return along(value, 1, k)


def other_core(value):
    return along(value, 0, 1)


def turned(value, k, phase):
    pairs = [(i, i ^ (k << (3 if (i & 1) == phase else 1))) for i in range(BATCH)]
    return lax.ppermute(value, "batch", pairs)


def along_z(value, k):
    return lax.ppermute(value, "head", [(i, (i + k) % HEADS) for i in range(HEADS)])


def shards(queries, new_kv, prefix_kv, suffix_kv, page_table, suffix_len, prompt_of, out_weight):
    me = lax.axis_index("batch")
    z = lax.axis_index("head")
    x, y, core = me // 8, (me // 2) % 4, me % 2
    place = [8 * x + 4 * (y // 2), me * 256, x, y // 2, z, y % 2, core]
    place = jnp.stack(place).astype(jnp.int32)

    prefix_other = other_core(prefix_kv)
    weights = [out_weight, other_core(out_weight)]

    sent = local_parts(place, queries, prompt_of, page_table, suffix_len, new_kv, suffix_kv)
    by_x = [sent[0]] + [along_x(sent[k], k) for k in (1, 2, 3)]
    same, other, far = regroup(place, by_x)
    from1, from3, from2 = along_y(same, 1), along_y(other, 3), along_y(other, 2)
    far = along_y(far, 2)

    own = prefix_keep(same, prefix_kv, prefix_other)
    message = along_y(prefix_send(from1, from3, prefix_kv, prefix_other, own[1]), 1)
    cross = prefix_keep(from2, prefix_kv, prefix_other)
    attended = combine(place, own, cross, message, by_x, far)

    orders = jnp.stack([same[16], from1[16], from2[16], from3[16]])
    orders = jnp.concatenate([orders, other_core(orders)], axis=0)
    pick = order_rows(place, orders)

    pair = jnp.concatenate([attended, turned(attended, 1, 0)], axis=0)
    ring0 = jnp.concatenate([pair, turned(pair, 3, 0)], axis=0)
    ring1, ring3 = turned(ring0, 1, 1), turned(ring0, 3, 1)
    ring2 = jnp.concatenate([turned(ring3[:64], 1, 1), turned(ring1[64:], 3, 1)], axis=0)
    first = project([ring0], weights)
    second = project([ring1, ring3], weights)
    up, down, keep = project_last(ring2, weights, first, second)

    below, above = along_z(up, 1), along_z(down, -1)
    up3, down3 = middle(keep, below, above)
    below3, above3 = along_z(up3, 3), along_z(down3, -3)
    own, other = total(keep, below, above, below3, above3)
    return finish(own, other_core(other), pick)


def solution(mesh):
    placed = (
        P("batch", "head"),
        P(None, "batch", "head"),
        P(None, "batch", "head"),
        P(None, "batch", None, "head"),
        P("batch", None),
        P("batch"),
        P("batch"),
        P("head", "batch"),
    )
    return jax.shard_map(
        shards, mesh=mesh, in_specs=placed, out_specs=P("head", "batch"), check_vma=False
    )
```

```python
import jax
import jax.numpy as jnp
from jax import lax
from jax.experimental import pallas as pl
from jax.experimental.pallas import tpu as pltpu
from jax.sharding import PartitionSpec as P

DH = 128
GROUP = 16
SCALE = DH**-0.5
LOG2E = 1.4426950408889634
BATCH = 32
HEADS = 8
VMEM = pl.BlockSpec(memory_space=pltpu.VMEM)
SMEM = pl.BlockSpec(memory_space=pltpu.SMEM)
F32 = jnp.float32
BF16 = jnp.bfloat16
NT = (((1,), (1,)), ((), ()))
NN = (((1,), (0,)), ((), ()))


ANY = pl.BlockSpec(memory_space=pl.ANY)
HBM = pl.BlockSpec(memory_space=pltpu.HBM)


def params(mib=16):
    return pltpu.CompilerParams(vmem_limit_bytes=mib * 1024 * 1024)


def dot(a, b, dims=NN):
    return lax.dot_general(a, b, dims, preferred_element_type=F32)


def lanes():
    return lax.broadcasted_iota(jnp.int32, (GROUP, DH), 1)


def split_tile(tile, step):
    high = tile.astype(BF16).astype(F32)
    rest = tile - high
    middle = rest.astype(BF16).astype(F32)
    low = rest - middle
    joined = high + pltpu.roll(middle, step, 1) + pltpu.roll(low, 2 * step, 1)
    return joined.astype(BF16)


def join_tile(tile, step):
    wide = tile.astype(F32)
    return (wide + pltpu.roll(wide, DH - step, 1)) + pltpu.roll(wide, DH - 2 * step, 1)


def local_body(
    place, q_in, prompt_in, table_in, length_in, new_in, pool_in, o0, o1, o2, o3,
    q, prompt, table, length, new, pool, wide, scores, weights, slots, sems,
):
    pairs = [
        (q_in, q),
        (prompt_in, prompt),
        (table_in, table),
        (length_in, length),
        (new_in, new),
        (pool_in.at[0], pool.at[0]),
        (pool_in.at[1], pool.at[1]),
    ]
    copies = [pltpu.make_async_copy(a, b, sems.at[i]) for i, (a, b) in enumerate(pairs)]
    for copy in copies:
        copy.start()
    outs = (o0, o1, o2, o3)
    lane = lanes()
    copies[0].wait()
    for h in range(GROUP):
        wide[:, h, :] = q[:, h * DH : (h + 1) * DH].astype(F32)
    copies[1].wait()
    for p in range(8):
        slots[32 + p] = 0
    order = jnp.zeros((GROUP, DH), F32)
    for n in range(32):
        p = prompt[n]
        k = slots[32 + p]
        slots[32 + p] = k + 1
        slots[n] = (4 * p + k) ^ place[0]
        order = jnp.where(lane == n, (4 * p + k).astype(F32), order)
    for copy in copies[2:6]:
        copy.wait()
    base = place[1]
    for n in range(32):
        keys = jnp.concatenate([pool[0, table[j, n] - base] for j in range(8)], axis=0)
        s = dot(wide[n].astype(BF16), keys, NT) * SCALE
        scores[n] = jnp.where(lane < length[n], s, -1e30)
    own_keys = new[0].astype(F32)
    own_values = new[1].astype(F32)
    own = jnp.stack(
        [jnp.sum(wide[n] * own_keys[n : n + 1], axis=1, keepdims=True) for n in range(32)]
    ) * SCALE
    s = scores[...]
    peak = jnp.maximum(jnp.max(s, axis=2, keepdims=True), own)
    w = jnp.exp(s - peak)
    own_weight = jnp.exp(own - peak)
    total = jnp.sum(w, axis=2, keepdims=True) + own_weight
    weights[...] = w.astype(BF16)
    own_weight = own_weight.astype(BF16).astype(F32)
    mass = peak + jnp.log(total)
    inverse = 1.0 / total
    copies[6].wait()
    for n in range(32):
        values = jnp.concatenate([pool[1, table[j, n] - base] for j in range(8)], axis=0)
        mixed = dot(weights[n], values) + own_weight[n] * own_values[n : n + 1]
        scores[slots[n]] = mixed * inverse[n]
    held = [jnp.zeros((GROUP, DH), F32) for _ in range(4)]
    for n in range(32):
        slot = slots[n]
        weights[slot] = wide[n].astype(BF16)
        for i in range(4):
            held[i] = jnp.where(lane + 8 * i == slot, jnp.where(lane < 8, mass[n], 0.0), held[i])
    for i, out in enumerate(outs):
        out[0:8] = weights[8 * i : 8 * i + 8]
        out[8] = order.astype(BF16)
        out[9:17] = scores[8 * i : 8 * i + 8].astype(BF16)
        out[17] = split_tile(jnp.where(lane < 8, held[i], 0.0), 8)


def local_parts(place, q, prompt, table, length, new, pool):
    out = jax.ShapeDtypeStruct((18, GROUP, DH), BF16)
    return pl.pallas_call(
        local_body,
        out_shape=[out] * 4,
        in_specs=[SMEM] + [HBM] * 6,
        out_specs=[VMEM] * 4,
        scratch_shapes=[
            pltpu.VMEM((32, GROUP * DH), BF16),
            pltpu.SMEM((32,), jnp.int32),
            pltpu.SMEM((8, 32), jnp.int32),
            pltpu.SMEM((32,), jnp.int32),
            pltpu.VMEM((2, 32, DH), BF16),
            pltpu.VMEM((2, 256, GROUP, DH), BF16),
            pltpu.VMEM((32, GROUP, DH), F32),
            pltpu.VMEM((32, GROUP, DH), F32),
            pltpu.VMEM((32, GROUP, DH), BF16),
            pltpu.SMEM((40,), jnp.int32),
            pltpu.SemaphoreType.DMA((7,)),
        ],
        compiler_params=params(56),
        name="local_parts",
    )(place, q, prompt, table, length, new, pool)


def regroup_body(place, a0, a1, a2, a3, same, other, far):
    for i, a in enumerate((a0, a1, a2, a3)):
        same[4 * i : 4 * i + 4] = a[0:4]
        other[4 * i : 4 * i + 4] = a[4:8]
        far[5 * i : 5 * i + 5] = a[13:18]

        @pl.when(place[2] ^ (place[4] >> 1) == i)
        def _(a=a):
            same[16] = a[8]
            other[16] = a[8]


def regroup(place, parts):
    out = jax.ShapeDtypeStruct((17, GROUP, DH), BF16)
    return pl.pallas_call(
        regroup_body,
        out_shape=[out, out, jax.ShapeDtypeStruct((20, GROUP, DH), BF16)],
        in_specs=[SMEM] + [VMEM] * 4,
        out_specs=[VMEM] * 3,
        compiler_params=params(),
        name="regroup",
    )(place, *parts)


ROWS = 128


def prefix_part(q, kv):
    s = dot(q, kv[0], NT)
    peak = jnp.max(s, axis=1, keepdims=True)
    w = jnp.exp2((s - peak) * (SCALE * LOG2E))
    return dot(w.astype(BF16), kv[1]), peak * SCALE, jnp.sum(w, axis=1, keepdims=True)


def prefix_block(q, kv0, kv1):
    mixed0, peak0, total0 = prefix_part(q, kv0)
    mixed1, peak1, total1 = prefix_part(q, kv1)
    top = jnp.maximum(peak0, peak1)
    f0, f1 = jnp.exp(peak0 - top), jnp.exp(peak1 - top)
    total = total0 * f0 + total1 * f1
    return (mixed0 * f0 + mixed1 * f1) * (1.0 / total), top + jnp.log(total)


COUNT = ROWS // GROUP


def prefix_send_body(qa, qb, kv0, kv1, later, out):
    lane = lanes()
    tile = jnp.zeros((GROUP, DH), F32)
    for half, q in enumerate((qa, qb)):
        for i in range(256 // ROWS):
            rows = q[i * COUNT : (i + 1) * COUNT].reshape(ROWS, DH)
            mixed, mass = prefix_block(rows, kv0, kv1)
            at = half * 16 + i * COUNT
            out[at : at + COUNT] = mixed.reshape(COUNT, GROUP, DH).astype(BF16)
            for n in range(COUNT):
                tile = jnp.where(lane == at + n, mass[n * GROUP : (n + 1) * GROUP], tile)
    out[32] = split_tile(tile, 32)


def prefix_keep_body(q, kv0, kv1, out, masses):
    for i in range(256 // ROWS):
        rows = q[i * COUNT : (i + 1) * COUNT].reshape(ROWS, DH)
        mixed, mass = prefix_block(rows, kv0, kv1)
        at = i * COUNT
        out[at : at + COUNT] = mixed.reshape(COUNT, GROUP, DH)
        masses[at : at + COUNT] = jnp.broadcast_to(mass, (ROWS, DH)).reshape(COUNT, GROUP, DH)


def prefix_first_body(q, kv0_in, kv1_in, out, masses, kv0, kv1, sems):
    copies = [
        pltpu.make_async_copy(kv0_in, kv0, sems.at[0]),
        pltpu.make_async_copy(kv1_in, kv1, sems.at[1]),
    ]
    for copy in copies:
        copy.start()
    for copy in copies:
        copy.wait()
    prefix_keep_body(q, kv0, kv1, out, masses)


def prefix_cost(rows):
    return pl.CostEstimate(
        flops=4 * rows * 4096 * 128, bytes_accessed=2_500_000, transcendentals=rows * 4096
    )


def prefix_send(qa, qb, kv0, kv1, later):
    return pl.pallas_call(
        prefix_send_body,
        out_shape=jax.ShapeDtypeStruct((33, GROUP, DH), BF16),
        in_specs=[VMEM] * 4 + [ANY],
        out_specs=VMEM,
        compiler_params=params(24),
        cost_estimate=prefix_cost(512),
        name="prefix_send",
    )(qa, qb, kv0, kv1, later)


def prefix_keep(q, kv0, kv1):
    out = jax.ShapeDtypeStruct((16, GROUP, DH), F32)
    return pl.pallas_call(
        prefix_keep_body,
        out_shape=[out, out],
        in_specs=[VMEM] * 3,
        out_specs=[VMEM, VMEM],
        compiler_params=params(24),
        cost_estimate=prefix_cost(256),
        name="prefix_keep",
    )(q, kv0, kv1)


def prefix_first(q, kv0, kv1):
    out = jax.ShapeDtypeStruct((16, GROUP, DH), F32)
    held = jax.ShapeDtypeStruct(kv0.shape, BF16)
    return pl.pallas_call(
        prefix_first_body,
        out_shape=[out, out, held, held],
        in_specs=[VMEM, HBM, HBM],
        out_specs=[VMEM] * 4,
        scratch_shapes=[pltpu.SemaphoreType.DMA((2,))],
        compiler_params=params(24),
        cost_estimate=prefix_cost(256),
        name="prefix_first",
    )(q, kv0, kv1)


def combine_body(
    place, own, own_masses, cross, cross_masses, message, s0, s1, s2, s3, far, out, held
):
    x, y_high, z = place[2], place[3], place[4]
    theirs = join_tile(message[32], 32)
    near = [join_tile(s[17], 8) for s in (s0, s1, s2, s3)]
    across = [join_tile(far[5 * i + 4], 8) for i in range(4)]
    for g in range(2):
        for kx in range(4):
            for k in range(4):
                n = g * 16 + kx * 4 + k
                at = kx * 4 + k
                a, la = ((own, own_masses), (cross, cross_masses))[g]
                a, la = a[at], la[at]
                b = message[n].astype(F32)
                lb = jnp.broadcast_to(theirs[:, n : n + 1], (GROUP, DH))
                if g == 0:
                    s = (s0, s1, s2, s3)[kx][9 + k].astype(F32)
                    ls = jnp.broadcast_to(near[kx][:, k : k + 1], (GROUP, DH))
                else:
                    s = far[5 * kx + k].astype(F32)
                    ls = jnp.broadcast_to(across[kx][:, 4 + k : 5 + k], (GROUP, DH))
                top = jnp.maximum(jnp.maximum(la, lb), ls)
                ea, eb, es = jnp.exp(la - top), jnp.exp(lb - top), jnp.exp(ls - top)
                row = (ea * a + eb * b + es * s) / (ea + eb + es)
                target = (x ^ kx) * 2 + (y_high ^ g)
                held[((target - z) & 7) * 4 + k] = row
    for h in range(GROUP):
        out[:, h * DH : (h + 1) * DH] = held[:, h, :].astype(BF16)


def combine(place, own, cross, message, near, far):
    return pl.pallas_call(
        combine_body,
        out_shape=jax.ShapeDtypeStruct((32, GROUP * DH), BF16),
        in_specs=[SMEM] + [VMEM] * 10,
        out_specs=VMEM,
        scratch_shapes=[pltpu.VMEM((32, GROUP, DH), F32)],
        compiler_params=params(),
        name="combine",
    )(place, *own, *cross, message, *near, far)


def by_target(total):
    low = lax.broadcasted_iota(jnp.int32, (8, total.shape[1]), 0) < 4
    chunks = []
    for g in range(4):
        even, odd = [], []
        for j in (0, 2):
            first = total[j * 32 + g * 8 : j * 32 + g * 8 + 8]
            second = total[(j + 1) * 32 + g * 8 : (j + 1) * 32 + g * 8 + 8]
            even.append(jnp.where(low, first, pltpu.roll(second, 4, 0)))
            odd.append(jnp.where(low, pltpu.roll(first, 4, 0), second))
        chunks += [jnp.concatenate(even, axis=0), jnp.concatenate(odd, axis=0)]
    return chunks


def project_body(sizes, *refs):
    blocks, weights, out = refs[: sum(sizes)], refs[sum(sizes) : sum(sizes) + 2], refs[-1]
    at = 0
    for i, size in enumerate(sizes):
        block = jnp.concatenate([b[...] for b in blocks[at : at + size]], axis=0)
        at += size
        for side, weight in enumerate(weights):
            for d, chunk in enumerate(by_target(dot(block, weight[...]))):
                out[d, i * 16 : i * 16 + 16, side * 512 : side * 512 + 512] = chunk


def project(blocks, weights):
    sizes = [len(block) for block in blocks]
    pieces = [piece for block in blocks for piece in block]
    return pl.pallas_call(
        lambda *refs: project_body(sizes, *refs),
        out_shape=jax.ShapeDtypeStruct((8, 16 * len(sizes), 1024), F32),
        in_specs=[VMEM] * (len(pieces) + 2),
        out_specs=VMEM,
        compiler_params=params(),
        cost_estimate=pl.CostEstimate(
            flops=len(sizes) * 2 * 128 * 2048 * 1024, bytes_accessed=4_500_000, transcendentals=0
        ),
        name="project",
    )(*pieces, *weights)


def last_body(*refs):
    pieces, (w0, w1, first, second, up, down, keep) = refs[:-7], refs[-7:]
    block = jnp.concatenate([piece[...] for piece in pieces], axis=0)
    for side, weight in enumerate((w0, w1)):
        columns = slice(side * 512, side * 512 + 512)
        for d, chunk in enumerate(by_target(dot(block, weight[...]))):
            whole = jnp.concatenate([first[d, :, columns], second[d, :, columns], chunk], axis=0)
            if d != 4:
                keep[d, :, columns] = whole
            elif side == 0:
                up[...] = whole.astype(BF16)
            else:
                down[...] = whole.astype(BF16)


def project_last(pieces, weights, first, second):
    out = jax.ShapeDtypeStruct((64, 512), BF16)
    return pl.pallas_call(
        last_body,
        out_shape=[out, out, jax.ShapeDtypeStruct((8, 64, 1024), F32)],
        in_specs=[VMEM] * (len(pieces) + 4),
        out_specs=[VMEM] * 3,
        compiler_params=params(),
        name="project_last",
    )(*pieces, *weights, first, second)


def step_body(near, keep, below, above, up, down):
    low, high = keep.at[near], keep.at[8 - near]
    if below.shape[1] == 512:
        up[:, :512] = (low[:, :512] + below[...].astype(F32)).astype(BF16)
        up[:, 512:] = low[:, 512:].astype(BF16)
        down[:, :512] = high[:, :512].astype(BF16)
        down[:, 512:] = (high[:, 512:] + above[...].astype(F32)).astype(BF16)
    else:
        up[...] = (low[...] + below[...].astype(F32)).astype(BF16)
        down[...] = (high[...] + above[...].astype(F32)).astype(BF16)


def step(near, keep, below, above):
    out = jax.ShapeDtypeStruct((64, 1024), BF16)
    return pl.pallas_call(
        lambda *refs: step_body(near, *refs),
        out_shape=[out, out],
        in_specs=[VMEM] * 3,
        out_specs=[VMEM] * 2,
        compiler_params=params(),
        name="step",
    )(keep, below, above)


def total_body(keep, below, above, own, other):
    for side, out in enumerate((own, other)):
        columns = slice(side * 512, side * 512 + 512)
        near = below[:, columns].astype(F32) + above[:, columns].astype(F32)
        out[...] = (keep[0, :, columns] + near).astype(BF16)


def total(keep, below, above):
    out = jax.ShapeDtypeStruct((64, 512), BF16)
    return pl.pallas_call(
        total_body,
        out_shape=[out, out],
        in_specs=[VMEM] * 3,
        out_specs=[VMEM] * 2,
        compiler_params=params(),
        name="total",
    )(keep, below, above)


def order_body(place, orders, pick):
    x, y, core, z = place[2], place[3] * 2 + place[5], place[6], place[4]
    lane = lanes()
    order = jnp.zeros((GROUP, DH), F32)
    for block in range(4):
        dy = (2 * (z & 1) + block // 2) ^ y
        tile = orders[((block % 2) ^ core) * 4 + dy].astype(F32)
        order = jnp.where(lane >> 5 == block, pltpu.roll(tile, 32 * block, 1), order)
    order = order.astype(jnp.int32)
    prompt, k = order >> 2, order & 3
    block = lane >> 5
    far = block & 1
    dx = (prompt >> 1) ^ x
    dy = (2 * (prompt & 1) + (block >> 1)) ^ y
    first = jnp.where(far == 0, dx, dy)
    second = jnp.where(far == 0, dy, dx)
    first = jnp.where(first >= 2, 5 - first, first)
    second = jnp.where(second >= 2, 5 - second, second)
    source = ((far ^ core) * 16 + second * 4 + first) * 4 + k
    row = lax.broadcasted_iota(jnp.int32, (128, 128), 0)
    pick[...] = (row == source[0:1]).astype(F32).astype(BF16)


def order_rows(place, orders):
    return pl.pallas_call(
        order_body,
        out_shape=jax.ShapeDtypeStruct((128, 128), BF16),
        in_specs=[SMEM, VMEM],
        out_specs=VMEM,
        compiler_params=params(),
        name="order_rows",
    )(place, orders)


def finish_body(own, other, pick, out):
    dims = (((0,), (0,)), ((), ()))
    mixed = dot(pick[0:64], own[...], dims) + dot(pick[64:128], other[...], dims)
    out[...] = mixed.astype(BF16)


def finish(own, other, pick):
    return pl.pallas_call(
        finish_body,
        out_shape=jax.ShapeDtypeStruct((128, 512), BF16),
        in_specs=[VMEM] * 3,
        out_specs=VMEM,
        compiler_params=params(),
        name="finish",
    )(own, other, pick)


def along(value, shift, k):
    return lax.ppermute(value, "batch", [(i, i ^ (k << shift)) for i in range(BATCH)])


def along_x(value, k):
    return along(value, 3, k)


def along_y(value, k):
    return along(value, 1, k)


def other_core(value):
    return along(value, 0, 1)


def turned(value, k, phase):
    pairs = [(i, i ^ (k << (3 if (i & 1) == phase else 1))) for i in range(BATCH)]
    return lax.ppermute(value, "batch", pairs)


def along_z(value, k):
    return lax.ppermute(value, "head", [(i, (i + k) % HEADS) for i in range(HEADS)])


def shards(queries, new_kv, prefix_kv, suffix_kv, page_table, suffix_len, prompt_of, out_weight):
    me = lax.axis_index("batch")
    z = lax.axis_index("head")
    x, y, core = me // 8, (me // 2) % 4, me % 2
    place = [8 * x + 4 * (y // 2), me * 256, x, y // 2, z, y % 2, core]
    place = jnp.stack(place).astype(jnp.int32)

    prefix_other = other_core(prefix_kv)
    weights = [out_weight, other_core(out_weight)]

    sent = local_parts(place, queries, prompt_of, page_table.T, suffix_len, new_kv, suffix_kv)
    by_x = [sent[0]] + [along_x(sent[k], k) for k in (1, 2, 3)]
    same, other, far = regroup(place, by_x)
    from1, from3, from2 = along_y(same, 1), along_y(other, 3), along_y(other, 2)
    far = along_y(far, 2)

    *own, kv0, kv1 = prefix_first(same, prefix_kv, prefix_other)
    message = along_y(prefix_send(from1, from3, kv0, kv1, from2), 1)
    cross = prefix_keep(from2, kv0, kv1)
    attended = combine(place, own, cross, message, by_x, far)

    orders = jnp.stack([same[16], from1[16], from2[16], from3[16]])
    orders = jnp.concatenate([orders, other_core(orders)], axis=0)
    pick = order_rows(place, orders)

    next1 = turned(attended, 1, 0)
    lower = jnp.concatenate([attended, next1], axis=0)
    upper = jnp.concatenate([turned(attended, 3, 0), turned(next1, 3, 0)], axis=0)
    low1, low3 = turned(lower, 1, 1), turned(lower, 3, 1)
    high1, high3 = turned(upper, 1, 1), turned(upper, 3, 1)
    low2 = [turned(low3[:32], 1, 1), turned(low3[32:], 1, 1)]
    high2 = [turned(high1[:32], 3, 1), turned(high1[32:], 3, 1)]
    first = project([[lower, upper]], weights)
    second = project([[low1, high1], [low3, high3]], weights)
    below, above, keep = project_last(low2 + high2, weights, first, second)

    for near in (3, 2, 1):
        below, above = along_z(below, 1), along_z(above, -1)
        below, above = step(near, keep, below, above)
    own, other = total(keep, along_z(below, 1), along_z(above, -1))
    return finish(own, other_core(other), pick)


def solution(mesh):
    placed = (
        P("batch", "head"),
        P(None, "batch", "head"),
        P(None, "batch", "head"),
        P(None, "batch", None, "head"),
        P("batch", None),
        P("batch"),
        P("batch"),
        P("head", "batch"),
    )
    return jax.shard_map(
        shards, mesh=mesh, in_specs=placed, out_specs=P("head", "batch"), check_vma=False
    )
```

```python
import jax
import jax.numpy as jnp
from jax import lax
from jax.experimental import pallas as pl
from jax.experimental.pallas import tpu as pltpu
from jax.sharding import PartitionSpec as P

DH = 128
GROUP = 16
SCALE = DH**-0.5
LOG2E = 1.4426950408889634
BATCH = 32
HEADS = 8
VMEM = pl.BlockSpec(memory_space=pltpu.VMEM)
SMEM = pl.BlockSpec(memory_space=pltpu.SMEM)
F32 = jnp.float32
BF16 = jnp.bfloat16
NT = (((1,), (1,)), ((), ()))
NN = (((1,), (0,)), ((), ()))


ANY = pl.BlockSpec(memory_space=pl.ANY)
HBM = pl.BlockSpec(memory_space=pltpu.HBM)


def params(mib=16):
    return pltpu.CompilerParams(vmem_limit_bytes=mib * 1024 * 1024)


def dot(a, b, dims=NN):
    return lax.dot_general(a, b, dims, preferred_element_type=F32)


def lanes():
    return lax.broadcasted_iota(jnp.int32, (GROUP, DH), 1)


def split_tile(tile, step):
    high = tile.astype(BF16).astype(F32)
    rest = tile - high
    middle = rest.astype(BF16).astype(F32)
    low = rest - middle
    joined = high + pltpu.roll(middle, step, 1) + pltpu.roll(low, 2 * step, 1)
    return joined.astype(BF16)


def join_tile(tile, step):
    wide = tile.astype(F32)
    return (wide + pltpu.roll(wide, DH - step, 1)) + pltpu.roll(wide, DH - 2 * step, 1)


def local_body(
    place, q_in, prompt_in, table_in, length_in, new_in, pool_in, o0, o1, o2, o3,
    q, prompt, table, length, new, pool, wide, scores, weights, slots, sems,
):
    pairs = [
        (q_in, q),
        (prompt_in, prompt),
        (table_in, table),
        (length_in, length),
        (new_in, new),
        (pool_in.at[0], pool.at[0]),
        (pool_in.at[1], pool.at[1]),
    ]
    copies = [pltpu.make_async_copy(a, b, sems.at[i]) for i, (a, b) in enumerate(pairs)]
    for copy in copies:
        copy.start()
    outs = (o0, o1, o2, o3)
    lane = lanes()
    copies[0].wait()
    for h in range(GROUP):
        wide[:, h, :] = q[:, h * DH : (h + 1) * DH].astype(F32)
    copies[1].wait()
    for p in range(8):
        slots[32 + p] = 0
    order = jnp.zeros((GROUP, DH), F32)
    for n in range(32):
        p = prompt[n]
        k = slots[32 + p]
        slots[32 + p] = k + 1
        slots[n] = (4 * p + k) ^ place[0]
        order = jnp.where(lane == n, (4 * p + k).astype(F32), order)
    for copy in copies[2:6]:
        copy.wait()
    base = place[1]
    for n in range(32):
        keys = jnp.concatenate([pool[0, table[j, n] - base] for j in range(8)], axis=0)
        s = dot(wide[n].astype(BF16), keys, NT) * SCALE
        scores[n] = jnp.where(lane < length[n], s, -1e30)
    own_keys = new[0].astype(F32)
    own_values = new[1].astype(F32)
    own = jnp.stack(
        [jnp.sum(wide[n] * own_keys[n : n + 1], axis=1, keepdims=True) for n in range(32)]
    ) * SCALE
    s = scores[...]
    peak = jnp.maximum(jnp.max(s, axis=2, keepdims=True), own)
    w = jnp.exp(s - peak)
    own_weight = jnp.exp(own - peak)
    total = jnp.sum(w, axis=2, keepdims=True) + own_weight
    weights[...] = w.astype(BF16)
    own_weight = own_weight.astype(BF16).astype(F32)
    mass = peak + jnp.log(total)
    inverse = 1.0 / total
    copies[6].wait()
    for n in range(32):
        values = jnp.concatenate([pool[1, table[j, n] - base] for j in range(8)], axis=0)
        mixed = dot(weights[n], values) + own_weight[n] * own_values[n : n + 1]
        scores[slots[n]] = mixed * inverse[n]
    held = [jnp.zeros((GROUP, DH), F32) for _ in range(4)]
    for n in range(32):
        slot = slots[n]
        weights[slot] = wide[n].astype(BF16)
        for i in range(4):
            held[i] = jnp.where(lane + 8 * i == slot, jnp.where(lane < 8, mass[n], 0.0), held[i])
    for i, out in enumerate(outs):
        out[0:8] = weights[8 * i : 8 * i + 8]
        out[8] = order.astype(BF16)
        out[9:17] = scores[8 * i : 8 * i + 8].astype(BF16)
        out[17] = split_tile(jnp.where(lane < 8, held[i], 0.0), 8)


def local_parts(place, q, prompt, table, length, new, pool):
    out = jax.ShapeDtypeStruct((18, GROUP, DH), BF16)
    return pl.pallas_call(
        local_body,
        out_shape=[out] * 4,
        in_specs=[SMEM] + [HBM] * 6,
        out_specs=[VMEM] * 4,
        scratch_shapes=[
            pltpu.VMEM((32, GROUP * DH), BF16),
            pltpu.SMEM((32,), jnp.int32),
            pltpu.SMEM((8, 32), jnp.int32),
            pltpu.SMEM((32,), jnp.int32),
            pltpu.VMEM((2, 32, DH), BF16),
            pltpu.VMEM((2, 256, GROUP, DH), BF16),
            pltpu.VMEM((32, GROUP, DH), F32),
            pltpu.VMEM((32, GROUP, DH), F32),
            pltpu.VMEM((32, GROUP, DH), BF16),
            pltpu.SMEM((40,), jnp.int32),
            pltpu.SemaphoreType.DMA((7,)),
        ],
        compiler_params=params(56),
        name="local_parts",
    )(place, q, prompt, table, length, new, pool)


def regroup_body(place, a0, a1, a2, a3, same, other, across):
    for i, a in enumerate((a0, a1, a2, a3)):
        same[4 * i : 4 * i + 4] = a[0:4]
        other[4 * i : 4 * i + 4] = a[4:8]
        across[4 * i : 4 * i + 4] = a[4:8]
        across[17 + 5 * i : 22 + 5 * i] = a[13:18]

        @pl.when(place[2] ^ (place[4] >> 1) == i)
        def _(a=a):
            same[16] = a[8]
            other[16] = a[8]
            across[16] = a[8]


def regroup(place, parts):
    out = jax.ShapeDtypeStruct((17, GROUP, DH), BF16)
    return pl.pallas_call(
        regroup_body,
        out_shape=[out, out, jax.ShapeDtypeStruct((37, GROUP, DH), BF16)],
        in_specs=[SMEM] + [VMEM] * 4,
        out_specs=[VMEM] * 3,
        compiler_params=params(),
        name="regroup",
    )(place, *parts)


ROWS = 128


def prefix_part(q, kv):
    s = dot(q, kv[0], NT)
    peak = jnp.max(s, axis=1, keepdims=True)
    w = jnp.exp2((s - peak) * (SCALE * LOG2E))
    return dot(w.astype(BF16), kv[1]), peak * SCALE, jnp.sum(w, axis=1, keepdims=True)


def prefix_block(q, kv0, kv1):
    mixed0, peak0, total0 = prefix_part(q, kv0)
    mixed1, peak1, total1 = prefix_part(q, kv1)
    top = jnp.maximum(peak0, peak1)
    f0, f1 = jnp.exp(peak0 - top), jnp.exp(peak1 - top)
    total = total0 * f0 + total1 * f1
    return (mixed0 * f0 + mixed1 * f1) * (1.0 / total), top + jnp.log(total)


COUNT = ROWS // GROUP


def prefix_send_body(qa, qb, kv0, kv1, later, out):
    lane = lanes()
    tile = jnp.zeros((GROUP, DH), F32)
    for half, q in enumerate((qa, qb)):
        for i in range(256 // ROWS):
            rows = q[i * COUNT : (i + 1) * COUNT].reshape(ROWS, DH)
            mixed, mass = prefix_block(rows, kv0, kv1)
            at = half * 16 + i * COUNT
            out[at : at + COUNT] = mixed.reshape(COUNT, GROUP, DH).astype(BF16)
            for n in range(COUNT):
                tile = jnp.where(lane == at + n, mass[n * GROUP : (n + 1) * GROUP], tile)
    out[32] = split_tile(tile, 32)


def prefix_keep_body(q, kv0, kv1, out, masses):
    for i in range(256 // ROWS):
        rows = q[i * COUNT : (i + 1) * COUNT].reshape(ROWS, DH)
        mixed, mass = prefix_block(rows, kv0, kv1)
        at = i * COUNT
        out[at : at + COUNT] = mixed.reshape(COUNT, GROUP, DH)
        masses[at : at + COUNT] = jnp.broadcast_to(mass, (ROWS, DH)).reshape(COUNT, GROUP, DH)


def prefix_first_body(q, kv0_in, kv1_in, out, masses, kv0, kv1, sems):
    copies = [
        pltpu.make_async_copy(kv0_in, kv0, sems.at[0]),
        pltpu.make_async_copy(kv1_in, kv1, sems.at[1]),
    ]
    for copy in copies:
        copy.start()
    for copy in copies:
        copy.wait()
    prefix_keep_body(q, kv0, kv1, out, masses)


def prefix_cost(rows):
    return pl.CostEstimate(
        flops=4 * rows * 4096 * 128, bytes_accessed=2_500_000, transcendentals=rows * 4096
    )


def prefix_send(qa, qb, kv0, kv1, later):
    return pl.pallas_call(
        prefix_send_body,
        out_shape=jax.ShapeDtypeStruct((33, GROUP, DH), BF16),
        in_specs=[VMEM] * 4 + [ANY],
        out_specs=VMEM,
        compiler_params=params(24),
        cost_estimate=prefix_cost(512),
        name="prefix_send",
    )(qa, qb, kv0, kv1, later)


def prefix_keep(q, kv0, kv1):
    out = jax.ShapeDtypeStruct((16, GROUP, DH), F32)
    return pl.pallas_call(
        prefix_keep_body,
        out_shape=[out, out],
        in_specs=[VMEM] * 3,
        out_specs=[VMEM, VMEM],
        compiler_params=params(24),
        cost_estimate=prefix_cost(256),
        name="prefix_keep",
    )(q, kv0, kv1)


def prefix_first(q, kv0, kv1):
    out = jax.ShapeDtypeStruct((16, GROUP, DH), F32)
    held = jax.ShapeDtypeStruct(kv0.shape, BF16)
    return pl.pallas_call(
        prefix_first_body,
        out_shape=[out, out, held, held],
        in_specs=[VMEM, VMEM, VMEM],
        out_specs=[VMEM] * 4,
        scratch_shapes=[pltpu.SemaphoreType.DMA((2,))],
        compiler_params=params(24),
        cost_estimate=prefix_cost(256),
        name="prefix_first",
    )(q, kv0, kv1)


def combine_body(
    place, own, own_masses, cross, cross_masses, message, s0, s1, s2, s3, far, out, held
):
    x, y_high, z = place[2], place[3], place[4]
    theirs = join_tile(message[32], 32)
    near = [join_tile(s[17], 8) for s in (s0, s1, s2, s3)]
    across = [join_tile(far[21 + 5 * i], 8) for i in range(4)]
    for g in range(2):
        for kx in range(4):
            for k in range(4):
                n = g * 16 + kx * 4 + k
                at = kx * 4 + k
                a, la = ((own, own_masses), (cross, cross_masses))[g]
                a, la = a[at], la[at]
                b = message[n].astype(F32)
                lb = jnp.broadcast_to(theirs[:, n : n + 1], (GROUP, DH))
                if g == 0:
                    s = (s0, s1, s2, s3)[kx][9 + k].astype(F32)
                    ls = jnp.broadcast_to(near[kx][:, k : k + 1], (GROUP, DH))
                else:
                    s = far[17 + 5 * kx + k].astype(F32)
                    ls = jnp.broadcast_to(across[kx][:, 4 + k : 5 + k], (GROUP, DH))
                top = jnp.maximum(jnp.maximum(la, lb), ls)
                ea, eb, es = jnp.exp(la - top), jnp.exp(lb - top), jnp.exp(ls - top)
                row = (ea * a + eb * b + es * s) / (ea + eb + es)
                target = (x ^ kx) * 2 + (y_high ^ g)
                held[((target - z) & 7) * 4 + k] = row
    for h in range(GROUP):
        out[:, h * DH : (h + 1) * DH] = held[:, h, :].astype(BF16)


def combine(place, own, cross, message, near, far):
    return pl.pallas_call(
        combine_body,
        out_shape=jax.ShapeDtypeStruct((32, GROUP * DH), BF16),
        in_specs=[SMEM] + [VMEM] * 10,
        out_specs=VMEM,
        scratch_shapes=[pltpu.VMEM((32, GROUP, DH), F32)],
        compiler_params=params(),
        name="combine",
    )(place, *own, *cross, message, *near, far)


def by_target(total):
    low = lax.broadcasted_iota(jnp.int32, (8, total.shape[1]), 0) < 4
    chunks = []
    for g in range(4):
        even, odd = [], []
        for j in (0, 2):
            first = total[j * 32 + g * 8 : j * 32 + g * 8 + 8]
            second = total[(j + 1) * 32 + g * 8 : (j + 1) * 32 + g * 8 + 8]
            even.append(jnp.where(low, first, pltpu.roll(second, 4, 0)))
            odd.append(jnp.where(low, pltpu.roll(first, 4, 0), second))
        chunks += [jnp.concatenate(even, axis=0), jnp.concatenate(odd, axis=0)]
    return chunks


def project_body(sizes, *refs):
    blocks, weights, out = refs[: sum(sizes)], refs[sum(sizes) : sum(sizes) + 2], refs[-1]
    at = 0
    for i, size in enumerate(sizes):
        block = jnp.concatenate([b[...] for b in blocks[at : at + size]], axis=0)
        at += size
        for side, weight in enumerate(weights):
            for d, chunk in enumerate(by_target(dot(block, weight[...]))):
                out[d, i * 16 : i * 16 + 16, side * 512 : side * 512 + 512] = chunk


def project(blocks, weights):
    sizes = [len(block) for block in blocks]
    pieces = [piece for block in blocks for piece in block]
    return pl.pallas_call(
        lambda *refs: project_body(sizes, *refs),
        out_shape=jax.ShapeDtypeStruct((8, 16 * len(sizes), 1024), F32),
        in_specs=[VMEM] * (len(pieces) + 2),
        out_specs=VMEM,
        compiler_params=params(),
        cost_estimate=pl.CostEstimate(
            flops=len(sizes) * 2 * 128 * 2048 * 1024, bytes_accessed=4_500_000, transcendentals=0
        ),
        name="project",
    )(*pieces, *weights)


def last_body(*refs):
    pieces, (w0, w1, first, second, up, down, up4, down4, keep) = refs[:-9], refs[-9:]
    block = jnp.concatenate([piece[...] for piece in pieces], axis=0)
    for side, weight in enumerate((w0, w1)):
        columns = slice(side * 512, side * 512 + 512)
        for d, chunk in enumerate(by_target(dot(block, weight[...]))):
            whole = jnp.concatenate([first[d, :, columns], second[d, :, columns], chunk], axis=0)
            if d in (0, 2, 6):
                keep[(0, 2, 6).index(d), :, columns] = whole
            elif d in (3, 1):
                up[(3, 1).index(d), :, columns] = whole.astype(BF16)
            elif d in (5, 7):
                down[(5, 7).index(d), :, columns] = whole.astype(BF16)
            elif side == 0:
                up4[...] = whole.astype(BF16)
            else:
                down4[...] = whole.astype(BF16)


def project_last(pieces, weights, first, second):
    pair = jax.ShapeDtypeStruct((2, 64, 1024), BF16)
    half = jax.ShapeDtypeStruct((64, 512), BF16)
    return pl.pallas_call(
        last_body,
        out_shape=[pair, pair, half, half, jax.ShapeDtypeStruct((3, 64, 1024), F32)],
        in_specs=[VMEM] * (len(pieces) + 4),
        out_specs=[VMEM] * 5,
        compiler_params=params(),
        name="project_last",
    )(*pieces, *weights, first, second)


def middle_body(keep, below, above, below4, above4, up, down):
    u = keep[1] + below[0].astype(F32)
    up[:, :512] = (u[:, :512] + below4[...].astype(F32)).astype(BF16)
    up[:, 512:] = u[:, 512:].astype(BF16)
    d = keep[2] + above[0].astype(F32)
    down[:, :512] = d[:, :512].astype(BF16)
    down[:, 512:] = (d[:, 512:] + above4[...].astype(F32)).astype(BF16)


def middle(keep, below, above, below4, above4):
    out = jax.ShapeDtypeStruct((64, 1024), BF16)
    return pl.pallas_call(
        middle_body,
        out_shape=[out, out],
        in_specs=[VMEM] * 5,
        out_specs=[VMEM] * 2,
        compiler_params=params(),
        name="middle",
    )(keep, below, above, below4, above4)


def total_body(keep, below, above, below2, above2, own, other):
    near = keep[0] + below[1].astype(F32) + above[1].astype(F32)
    whole = (near + below2[...].astype(F32) + above2[...].astype(F32)).astype(BF16)
    own[...] = whole[:, :512]
    other[...] = whole[:, 512:]


def total(keep, below, above, below2, above2):
    out = jax.ShapeDtypeStruct((64, 512), BF16)
    return pl.pallas_call(
        total_body,
        out_shape=[out, out],
        in_specs=[VMEM] * 5,
        out_specs=[VMEM] * 2,
        compiler_params=params(),
        name="total",
    )(keep, below, above, below2, above2)


def order_body(place, orders, pick):
    x, y, core, z = place[2], place[3] * 2 + place[5], place[6], place[4]
    lane = lanes()
    order = jnp.zeros((GROUP, DH), F32)
    for block in range(4):
        dy = (2 * (z & 1) + block // 2) ^ y
        tile = orders[((block % 2) ^ core) * 4 + dy].astype(F32)
        order = jnp.where(lane >> 5 == block, pltpu.roll(tile, 32 * block, 1), order)
    order = order.astype(jnp.int32)
    prompt, k = order >> 2, order & 3
    block = lane >> 5
    far = block & 1
    dx = (prompt >> 1) ^ x
    dy = (2 * (prompt & 1) + (block >> 1)) ^ y
    first = jnp.where(far == 0, dx, dy)
    second = jnp.where(far == 0, dy, dx)
    second = jnp.where(second >= 2, 5 - second, second)
    source = ((far ^ core) * 16 + second * 4 + first) * 4 + k
    row = lax.broadcasted_iota(jnp.int32, (128, 128), 0)
    pick[...] = (row == source[0:1]).astype(F32).astype(BF16)


def order_rows(place, orders):
    return pl.pallas_call(
        order_body,
        out_shape=jax.ShapeDtypeStruct((128, 128), BF16),
        in_specs=[SMEM, VMEM],
        out_specs=VMEM,
        compiler_params=params(),
        name="order_rows",
    )(place, orders)


def finish_body(own, other, pick, out):
    dims = (((0,), (0,)), ((), ()))
    mixed = dot(pick[0:64], own[...], dims) + dot(pick[64:128], other[...], dims)
    out[...] = mixed.astype(BF16)


def finish(own, other, pick):
    return pl.pallas_call(
        finish_body,
        out_shape=jax.ShapeDtypeStruct((128, 512), BF16),
        in_specs=[VMEM] * 3,
        out_specs=VMEM,
        compiler_params=params(),
        name="finish",
    )(own, other, pick)


def along(value, shift, k):
    return lax.ppermute(value, "batch", [(i, i ^ (k << shift)) for i in range(BATCH)])


def along_x(value, k):
    return along(value, 3, k)


def along_y(value, k):
    return along(value, 1, k)


def other_core(value):
    return along(value, 0, 1)


def turned(value, k, phase):
    pairs = [(i, i ^ (k << (3 if (i & 1) == phase else 1))) for i in range(BATCH)]
    return lax.ppermute(value, "batch", pairs)


def along_z(value, k):
    return lax.ppermute(value, "head", [(i, (i + k) % HEADS) for i in range(HEADS)])


def shards(queries, new_kv, prefix_kv, suffix_kv, page_table, suffix_len, prompt_of, out_weight):
    me = lax.axis_index("batch")
    z = lax.axis_index("head")
    x, y, core = me // 8, (me // 2) % 4, me % 2
    place = [8 * x + 4 * (y // 2), me * 256, x, y // 2, z, y % 2, core]
    place = jnp.stack(place).astype(jnp.int32)

    prefix_other = other_core(prefix_kv)
    weights = [out_weight, other_core(out_weight)]

    sent = local_parts(place, queries, prompt_of, page_table.T, suffix_len, new_kv, suffix_kv)
    by_x = [sent[0]] + [along_x(sent[k], k) for k in (1, 2, 3)]
    same, other, across = regroup(place, by_x)
    from1, from3, from2 = along_y(same, 1), along_y(other, 3), along_y(across, 2)

    *own, kv0, kv1 = prefix_first(same, prefix_kv, prefix_other)
    message = along_y(prefix_send(from1, from3, kv0, kv1, from2), 1)
    cross = prefix_keep(from2, kv0, kv1)
    attended = combine(place, own, cross, message, by_x, from2)

    orders = jnp.stack([same[16], from1[16], from2[16], from3[16]])
    orders = jnp.concatenate([orders, other_core(orders)], axis=0)
    pick = order_rows(place, orders)

    ring0 = jnp.concatenate([attended] + [turned(attended, k, 0) for k in (1, 2, 3)], axis=0)
    ring1, ring3 = turned(ring0, 1, 1), turned(ring0, 3, 1)
    ring2 = [turned(ring3[:64], 1, 1), turned(ring1[64:], 3, 1)]
    first = project([[ring0]], weights)
    second = project([[ring1], [ring3]], weights)
    up, down, up4, down4, keep = project_last(ring2, weights, first, second)

    below4, above4 = along_z(up4, 2), along_z(down4, -2)
    below, above = along_z(up, 1), along_z(down, -1)
    up2, down2 = middle(keep, below, above, below4, above4)
    own, other = total(keep, below, above, along_z(up2, 2), along_z(down2, -2))
    return finish(own, other_core(other), pick)


def solution(mesh):
    placed = (
        P("batch", "head"),
        P(None, "batch", "head"),
        P(None, "batch", "head"),
        P(None, "batch", None, "head"),
        P("batch", None),
        P("batch"),
        P("batch"),
        P("head", "batch"),
    )
    return jax.shard_map(
        shards, mesh=mesh, in_specs=placed, out_specs=P("head", "batch"), check_vma=False
    )
```

```python
import jax
import jax.numpy as jnp
from jax import lax
from jax.experimental import pallas as pl
from jax.experimental.pallas import tpu as pltpu
from jax.sharding import PartitionSpec as P

DH = 128
GROUP = 16
SCALE = DH**-0.5
LOG2E = 1.4426950408889634
BATCH = 32
HEADS = 8
VMEM = pl.BlockSpec(memory_space=pltpu.VMEM)
SMEM = pl.BlockSpec(memory_space=pltpu.SMEM)
F32 = jnp.float32
BF16 = jnp.bfloat16
NT = (((1,), (1,)), ((), ()))
NN = (((1,), (0,)), ((), ()))


ANY = pl.BlockSpec(memory_space=pl.ANY)
HBM = pl.BlockSpec(memory_space=pltpu.HBM)


def params(mib=16):
    return pltpu.CompilerParams(vmem_limit_bytes=mib * 1024 * 1024)


def dot(a, b, dims=NN):
    return lax.dot_general(a, b, dims, preferred_element_type=F32)


def lanes():
    return lax.broadcasted_iota(jnp.int32, (GROUP, DH), 1)


def split_tile(tile, step):
    high = tile.astype(BF16).astype(F32)
    rest = tile - high
    middle = rest.astype(BF16).astype(F32)
    low = rest - middle
    joined = high + pltpu.roll(middle, step, 1) + pltpu.roll(low, 2 * step, 1)
    return joined.astype(BF16)


def join_tile(tile, step):
    wide = tile.astype(F32)
    return (wide + pltpu.roll(wide, DH - step, 1)) + pltpu.roll(wide, DH - 2 * step, 1)


def local_body(
    place, q_in, prompt_in, table_in, length_in, new_in, pool_in, o0, o1, o2, o3,
    q, prompt, table, length, new, pool, wide, scores, weights, slots, sems,
):
    pairs = [
        (q_in, q),
        (prompt_in, prompt),
        (table_in, table),
        (length_in, length),
        (new_in, new),
        (pool_in.at[0], pool.at[0]),
        (pool_in.at[1], pool.at[1]),
    ]
    copies = [pltpu.make_async_copy(a, b, sems.at[i]) for i, (a, b) in enumerate(pairs)]
    for copy in copies:
        copy.start()
    outs = (o0, o1, o2, o3)
    lane = lanes()
    copies[0].wait()
    for h in range(GROUP):
        wide[:, h, :] = q[:, h * DH : (h + 1) * DH].astype(F32)
    copies[1].wait()
    for p in range(8):
        slots[32 + p] = 0
    order = jnp.zeros((GROUP, DH), F32)
    for n in range(32):
        p = prompt[n]
        k = slots[32 + p]
        slots[32 + p] = k + 1
        slots[n] = (4 * p + k) ^ place[0]
        order = jnp.where(lane == n, (4 * p + k).astype(F32), order)
    for copy in copies[2:6]:
        copy.wait()
    base = place[1]
    for n in range(32):
        keys = jnp.concatenate([pool[0, table[j, n] - base] for j in range(8)], axis=0)
        s = dot(wide[n].astype(BF16), keys, NT) * SCALE
        scores[n] = jnp.where(lane < length[n], s, -1e30)
    own_keys = new[0].astype(F32)
    own_values = new[1].astype(F32)
    own = jnp.stack(
        [jnp.sum(wide[n] * own_keys[n : n + 1], axis=1, keepdims=True) for n in range(32)]
    ) * SCALE
    s = scores[...]
    peak = jnp.maximum(jnp.max(s, axis=2, keepdims=True), own)
    w = jnp.exp(s - peak)
    own_weight = jnp.exp(own - peak)
    total = jnp.sum(w, axis=2, keepdims=True) + own_weight
    weights[...] = w.astype(BF16)
    own_weight = own_weight.astype(BF16).astype(F32)
    mass = peak + jnp.log(total)
    inverse = 1.0 / total
    copies[6].wait()
    for n in range(32):
        values = jnp.concatenate([pool[1, table[j, n] - base] for j in range(8)], axis=0)
        mixed = dot(weights[n], values) + own_weight[n] * own_values[n : n + 1]
        scores[slots[n]] = mixed * inverse[n]
    held = [jnp.zeros((GROUP, DH), F32) for _ in range(4)]
    for n in range(32):
        slot = slots[n]
        weights[slot] = wide[n].astype(BF16)
        for i in range(4):
            held[i] = jnp.where(lane + 8 * i == slot, jnp.where(lane < 8, mass[n], 0.0), held[i])
    for i, out in enumerate(outs):
        out[0:8] = weights[8 * i : 8 * i + 8]
        out[8] = order.astype(BF16)
        out[9:17] = scores[8 * i : 8 * i + 8].astype(BF16)
        out[17] = split_tile(jnp.where(lane < 8, held[i], 0.0), 8)


def local_parts(place, q, prompt, table, length, new, pool):
    out = jax.ShapeDtypeStruct((18, GROUP, DH), BF16)
    return pl.pallas_call(
        local_body,
        out_shape=[out] * 4,
        in_specs=[SMEM] + [HBM] * 6,
        out_specs=[VMEM] * 4,
        scratch_shapes=[
            pltpu.VMEM((32, GROUP * DH), BF16),
            pltpu.SMEM((32,), jnp.int32),
            pltpu.SMEM((8, 32), jnp.int32),
            pltpu.SMEM((32,), jnp.int32),
            pltpu.VMEM((2, 32, DH), BF16),
            pltpu.VMEM((2, 256, GROUP, DH), BF16),
            pltpu.VMEM((32, GROUP, DH), F32),
            pltpu.VMEM((32, GROUP, DH), F32),
            pltpu.VMEM((32, GROUP, DH), BF16),
            pltpu.SMEM((40,), jnp.int32),
            pltpu.SemaphoreType.DMA((7,)),
        ],
        compiler_params=params(54),
        name="local_parts",
    )(place, q, prompt, table, length, new, pool)


def regroup_body(place, a0, a1, a2, a3, same, other, across):
    for i, a in enumerate((a0, a1, a2, a3)):
        same[4 * i : 4 * i + 4] = a[0:4]
        other[4 * i : 4 * i + 4] = a[4:8]
        across[4 * i : 4 * i + 4] = a[4:8]
        across[17 + 5 * i : 22 + 5 * i] = a[13:18]

        @pl.when(place[2] ^ (place[4] >> 1) == i)
        def _(a=a):
            same[16] = a[8]
            other[16] = a[8]
            across[16] = a[8]


def regroup(place, parts):
    out = jax.ShapeDtypeStruct((17, GROUP, DH), BF16)
    return pl.pallas_call(
        regroup_body,
        out_shape=[out, out, jax.ShapeDtypeStruct((37, GROUP, DH), BF16)],
        in_specs=[SMEM] + [VMEM] * 4,
        out_specs=[VMEM] * 3,
        compiler_params=params(),
        name="regroup",
    )(place, *parts)


ROWS = 128


def prefix_part(q, kv):
    s = dot(q, kv[0], NT)
    peak = jnp.max(s, axis=1, keepdims=True)
    w = jnp.exp2((s - peak) * (SCALE * LOG2E))
    return dot(w.astype(BF16), kv[1]), peak * SCALE, jnp.sum(w, axis=1, keepdims=True)


def prefix_block(q, kv0, kv1):
    mixed0, peak0, total0 = prefix_part(q, kv0)
    mixed1, peak1, total1 = prefix_part(q, kv1)
    top = jnp.maximum(peak0, peak1)
    f0, f1 = jnp.exp(peak0 - top), jnp.exp(peak1 - top)
    total = total0 * f0 + total1 * f1
    return (mixed0 * f0 + mixed1 * f1) * (1.0 / total), top + jnp.log(total)


COUNT = ROWS // GROUP


def prefix_send_body(qa, qb, kv0, kv1, after, later, out):
    lane = lanes()
    tile = jnp.zeros((GROUP, DH), F32)
    for half, q in enumerate((qa, qb)):
        for i in range(256 // ROWS):
            rows = q[i * COUNT : (i + 1) * COUNT].reshape(ROWS, DH)
            mixed, mass = prefix_block(rows, kv0, kv1)
            at = half * 16 + i * COUNT
            out[at : at + COUNT] = mixed.reshape(COUNT, GROUP, DH).astype(BF16)
            for n in range(COUNT):
                tile = jnp.where(lane == at + n, mass[n * GROUP : (n + 1) * GROUP], tile)
    out[32] = split_tile(tile, 32)


def prefix_keep_body(q, kv0, kv1, out, masses):
    for i in range(256 // ROWS):
        rows = q[i * COUNT : (i + 1) * COUNT].reshape(ROWS, DH)
        mixed, mass = prefix_block(rows, kv0, kv1)
        at = i * COUNT
        out[at : at + COUNT] = mixed.reshape(COUNT, GROUP, DH)
        masses[at : at + COUNT] = jnp.broadcast_to(mass, (ROWS, DH)).reshape(COUNT, GROUP, DH)


def prefix_cost(rows):
    return pl.CostEstimate(
        flops=4 * rows * 4096 * 128, bytes_accessed=2_500_000, transcendentals=rows * 4096
    )


def prefix_send(qa, qb, kv0, kv1, after, later):
    return pl.pallas_call(
        prefix_send_body,
        out_shape=jax.ShapeDtypeStruct((33, GROUP, DH), BF16),
        in_specs=[VMEM] * 4 + [ANY] * 2,
        out_specs=VMEM,
        compiler_params=params(24),
        cost_estimate=prefix_cost(512),
        name="prefix_send",
    )(qa, qb, kv0, kv1, after, later)


def prefix_keep(q, kv0, kv1):
    out = jax.ShapeDtypeStruct((16, GROUP, DH), F32)
    return pl.pallas_call(
        prefix_keep_body,
        out_shape=[out, out],
        in_specs=[VMEM] * 3,
        out_specs=[VMEM, VMEM],
        compiler_params=params(24),
        cost_estimate=prefix_cost(256),
        name="prefix_keep",
    )(q, kv0, kv1)


def combine_body(
    place, own, own_masses, cross, cross_masses, message, s0, s1, s2, s3, far, out, held
):
    x, y_high, z = place[2], place[3], place[4]
    theirs = join_tile(message[32], 32)
    near = [join_tile(s[17], 8) for s in (s0, s1, s2, s3)]
    across = [join_tile(far[21 + 5 * i], 8) for i in range(4)]
    for g in range(2):
        for kx in range(4):
            for k in range(4):
                n = g * 16 + kx * 4 + k
                at = kx * 4 + k
                a, la = ((own, own_masses), (cross, cross_masses))[g]
                a, la = a[at], la[at]
                b = message[n].astype(F32)
                lb = jnp.broadcast_to(theirs[:, n : n + 1], (GROUP, DH))
                if g == 0:
                    s = (s0, s1, s2, s3)[kx][9 + k].astype(F32)
                    ls = jnp.broadcast_to(near[kx][:, k : k + 1], (GROUP, DH))
                else:
                    s = far[17 + 5 * kx + k].astype(F32)
                    ls = jnp.broadcast_to(across[kx][:, 4 + k : 5 + k], (GROUP, DH))
                top = jnp.maximum(jnp.maximum(la, lb), ls)
                ea, eb, es = jnp.exp(la - top), jnp.exp(lb - top), jnp.exp(ls - top)
                row = (ea * a + eb * b + es * s) / (ea + eb + es)
                target = (x ^ kx) * 2 + (y_high ^ g)
                held[((target - z - 2) & 7) * 4 + k] = row
    for h in range(GROUP):
        out[:, h * DH : (h + 1) * DH] = held[:, h, :].astype(BF16)


def combine(place, own, cross, message, near, far):
    return pl.pallas_call(
        combine_body,
        out_shape=jax.ShapeDtypeStruct((32, GROUP * DH), BF16),
        in_specs=[SMEM] + [VMEM] * 10,
        out_specs=VMEM,
        scratch_shapes=[pltpu.VMEM((32, GROUP, DH), F32)],
        compiler_params=params(),
        name="combine",
    )(place, *own, *cross, message, *near, far)


def by_target(total):
    low = lax.broadcasted_iota(jnp.int32, (8, total.shape[1]), 0) < 4
    chunks = []
    for g in range(2):
        even, odd = [], []
        for j in (0, 2):
            first = total[j * 16 + g * 8 : j * 16 + g * 8 + 8]
            second = total[(j + 1) * 16 + g * 8 : (j + 1) * 16 + g * 8 + 8]
            even.append(jnp.where(low, first, pltpu.roll(second, 4, 0)))
            odd.append(jnp.where(low, pltpu.roll(first, 4, 0), second))
        chunks += [jnp.concatenate(even, axis=0), jnp.concatenate(odd, axis=0)]
    return chunks


def project_body(a, b, c, w0, w1, out):
    rows = jnp.concatenate([a[...], b[...], c[...]], axis=0)
    for side, weight in enumerate((w0, w1)):
        total = dot(rows, weight[...])
        for i in range(3):
            for d, chunk in enumerate(by_target(total[64 * i : 64 * i + 64])):
                out[d, i * 16 : i * 16 + 16, side * 512 : side * 512 + 512] = chunk


def project(blocks, weights):
    return pl.pallas_call(
        project_body,
        out_shape=jax.ShapeDtypeStruct((4, 48, 1024), F32),
        in_specs=[VMEM] * 5,
        out_specs=VMEM,
        compiler_params=params(),
        cost_estimate=pl.CostEstimate(
            flops=2 * 192 * 2048 * 1024, bytes_accessed=4_500_000, transcendentals=0
        ),
        name="project",
    )(*blocks, *weights)


def last_chunks(a, b, w0, w1, first):
    rows = jnp.concatenate([a[...], b[...]], axis=0)
    for side, weight in enumerate((w0, w1)):
        columns = slice(side * 512, side * 512 + 512)
        for d, chunk in enumerate(by_target(dot(rows, weight[...]))):
            yield side, columns, d, jnp.concatenate([first[d, :, columns], chunk], axis=0)


def far_body(a, b, w0, w1, first, keep, up, down, up4, down4):
    for side, columns, d, whole in last_chunks(a, b, w0, w1, first):
        if d == 0:
            keep[:, columns] = whole
        elif d == 1:
            up[:, columns] = whole.astype(BF16)
        elif d == 3:
            down[:, columns] = whole.astype(BF16)
        elif side == 0:
            up4[...] = whole.astype(BF16)
        else:
            down4[...] = whole.astype(BF16)


def near_body(a, b, w0, w1, first, keep6, down, keep0, up):
    for _, columns, d, whole in last_chunks(a, b, w0, w1, first):
        if d in (0, 2):
            (keep6, keep0)[d // 2][:, columns] = whole
        else:
            (down, up)[d // 2][:, columns] = whole.astype(BF16)


SUM = jax.ShapeDtypeStruct((64, 1024), F32)
SENT = jax.ShapeDtypeStruct((64, 1024), BF16)
HALF = jax.ShapeDtypeStruct((64, 512), BF16)


def plain(body, out_shape, *args):
    return pl.pallas_call(
        body,
        out_shape=out_shape,
        in_specs=[VMEM] * len(args),
        out_specs=[VMEM] * len(out_shape),
        compiler_params=params(),
        name=body.__name__[:-5],
    )(*args)


def middle_body(keep2, keep6, below, above, below4, above4, up, down):
    up[:, :512] = (keep2[:, :512] + below[:, :512].astype(F32) + below4[...].astype(F32)).astype(BF16)
    up[:, 512:] = (keep2[:, 512:] + below[:, 512:].astype(F32)).astype(BF16)
    down[:, :512] = (keep6[:, :512] + above[:, :512].astype(F32)).astype(BF16)
    down[:, 512:] = (keep6[:, 512:] + above[:, 512:].astype(F32) + above4[...].astype(F32)).astype(BF16)


def total_body(keep, below1, above1, below2, above2, own, other):
    near = keep[...] + below1[...].astype(F32) + above1[...].astype(F32)
    whole = (near + below2[...].astype(F32) + above2[...].astype(F32)).astype(BF16)
    own[...] = whole[:, :512]
    other[...] = whole[:, 512:]


def order_body(place, orders, pick):
    x, y, core, z = place[2], place[3] * 2 + place[5], place[6], place[4]
    lane = lanes()
    order = jnp.zeros((GROUP, DH), F32)
    for block in range(4):
        dy = (2 * (z & 1) + block // 2) ^ y
        tile = orders[((block % 2) ^ core) * 4 + dy].astype(F32)
        order = jnp.where(lane >> 5 == block, pltpu.roll(tile, 32 * block, 1), order)
    order = order.astype(jnp.int32)
    prompt, k = order >> 2, order & 3
    block = lane >> 5
    far = block & 1
    dx = (prompt >> 1) ^ x
    dy = (2 * (prompt & 1) + (block >> 1)) ^ y
    first = jnp.where(far == 0, dx, dy)
    second = jnp.where(far == 0, dy, dx)
    second = jnp.where(second >= 2, 5 - second, second)
    source = ((far ^ core) * 16 + second * 4 + first) * 4 + k
    row = lax.broadcasted_iota(jnp.int32, (128, 128), 0)
    pick[...] = (row == source[0:1]).astype(F32).astype(BF16)


def order_rows(place, orders):
    return pl.pallas_call(
        order_body,
        out_shape=jax.ShapeDtypeStruct((128, 128), BF16),
        in_specs=[SMEM, VMEM],
        out_specs=VMEM,
        compiler_params=params(),
        name="order_rows",
    )(place, orders)


def finish_body(own, other, pick, out):
    dims = (((0,), (0,)), ((), ()))
    mixed = dot(pick[0:64], own[...], dims) + dot(pick[64:128], other[...], dims)
    out[...] = mixed.astype(BF16)


def finish(own, other, pick):
    return pl.pallas_call(
        finish_body,
        out_shape=jax.ShapeDtypeStruct((128, 512), BF16),
        in_specs=[VMEM] * 3,
        out_specs=VMEM,
        compiler_params=params(),
        name="finish",
    )(own, other, pick)


def along(value, shift, k):
    return lax.ppermute(value, "batch", [(i, i ^ (k << shift)) for i in range(BATCH)])


def along_x(value, k):
    return along(value, 3, k)


def along_y(value, k):
    return along(value, 1, k)


def other_core(value):
    return along(value, 0, 1)


def turned(value, k, phase):
    pairs = [(i, i ^ (k << (3 if (i & 1) == phase else 1))) for i in range(BATCH)]
    return lax.ppermute(value, "batch", pairs)


def gathered(parts):
    ring0 = jnp.concatenate(parts, axis=0)
    ring1, ring3 = turned(ring0, 1, 1), turned(ring0, 3, 1)
    return ring0, ring1, ring3, [turned(ring3[:32], 1, 1), turned(ring1[32:], 3, 1)]


def along_z(value, k):
    return lax.ppermute(value, "head", [(i, (i + k) % HEADS) for i in range(HEADS)])


def shards(queries, new_kv, prefix_kv, suffix_kv, page_table, suffix_len, prompt_of, out_weight):
    me = lax.axis_index("batch")
    z = lax.axis_index("head")
    x, y, core = me // 8, (me // 2) % 4, me % 2
    place = [8 * x + 4 * (y // 2), me * 256, x, y // 2, z, y % 2, core]
    place = jnp.stack(place).astype(jnp.int32)

    prefix_other = other_core(prefix_kv)
    weights = [out_weight, other_core(out_weight)]

    sent = local_parts(place, queries, prompt_of, page_table.T, suffix_len, new_kv, suffix_kv)
    by_x = [sent[0]] + [along_x(sent[k], k) for k in (1, 2, 3)]
    same, other, across = regroup(place, by_x)
    from1, from3, from2 = along_y(same, 1), along_y(other, 3), along_y(across, 2)

    own = prefix_keep(same, prefix_kv, prefix_other)
    message = along_y(prefix_send(from1, from3, prefix_kv, prefix_other, own[1], from2), 1)
    cross = prefix_keep(from2, prefix_kv, prefix_other)
    attended = combine(place, own, cross, message, by_x, from2)

    orders = jnp.stack([same[16], from1[16], from2[16], from3[16]])
    orders = jnp.concatenate([orders, other_core(orders)], axis=0)
    pick = order_rows(place, orders)

    parts = [attended] + [turned(attended, k, 0) for k in (1, 2, 3)]
    far, near = [gathered([a[i : i + 16] for a in parts]) for i in (0, 16)]
    first_far, first_near = project(far[:3], weights), project(near[:3], weights)
    keep2, up3, down3, up4, down4 = plain(
        far_body, [SUM, SENT, SENT, HALF, HALF], *far[3], *weights, first_far
    )
    below4, above4 = along_z(up4, 2), along_z(down4, -2)
    below3, above3 = along_z(up3, 1), along_z(down3, -1)
    keep6, down1, keep0, up1 = plain(
        near_body, [SUM, SENT, SUM, SENT], *near[3], *weights, first_near
    )
    below1, above1 = along_z(up1, 1), along_z(down1, -1)
    up2, down2 = plain(middle_body, [SENT, SENT], keep2, keep6, below3, above3, below4, above4)
    below2, above2 = along_z(up2, 2), along_z(down2, -2)
    own, other = plain(total_body, [HALF, HALF], keep0, below1, above1, below2, above2)
    return finish(own, other_core(other), pick)


def solution(mesh):
    placed = (
        P("batch", "head"),
        P(None, "batch", "head"),
        P(None, "batch", "head"),
        P(None, "batch", None, "head"),
        P("batch", None),
        P("batch"),
        P("batch"),
        P("head", "batch"),
    )
    return jax.shard_map(
        shards, mesh=mesh, in_specs=placed, out_specs=P("head", "batch"), check_vma=False
    )
```

```python
import jax
import jax.numpy as jnp
from jax import lax
from jax.experimental import pallas as pl
from jax.experimental.pallas import tpu as pltpu
from jax.sharding import PartitionSpec as P

DH = 128
GROUP = 16
SCALE = DH**-0.5
LOG2E = 1.4426950408889634
BATCH = 32
HEADS = 8
VMEM = pl.BlockSpec(memory_space=pltpu.VMEM)
SMEM = pl.BlockSpec(memory_space=pltpu.SMEM)
F32 = jnp.float32
BF16 = jnp.bfloat16
NT = (((1,), (1,)), ((), ()))
NN = (((1,), (0,)), ((), ()))


ANY = pl.BlockSpec(memory_space=pl.ANY)
HBM = pl.BlockSpec(memory_space=pltpu.HBM)


def params(mib=16):
    return pltpu.CompilerParams(vmem_limit_bytes=mib * 1024 * 1024)


def dot(a, b, dims=NN):
    return lax.dot_general(a, b, dims, preferred_element_type=F32)


def lanes():
    return lax.broadcasted_iota(jnp.int32, (GROUP, DH), 1)


def split_tile(tile, step):
    high = tile.astype(BF16).astype(F32)
    rest = tile - high
    middle = rest.astype(BF16).astype(F32)
    low = rest - middle
    joined = high + pltpu.roll(middle, step, 1) + pltpu.roll(low, 2 * step, 1)
    return joined.astype(BF16)


def join_tile(tile, step):
    wide = tile.astype(F32)
    return (wide + pltpu.roll(wide, DH - step, 1)) + pltpu.roll(wide, DH - 2 * step, 1)


def local_body(
    place, q_in, prompt_in, table_in, length_in, new_in, pool_in, o0, o1, o2, o3,
    q, prompt, table, length, new, pool, wide, scores, weights, slots, sems,
):
    pairs = [
        (q_in, q),
        (prompt_in, prompt),
        (table_in, table),
        (length_in, length),
        (new_in, new),
        (pool_in.at[0], pool.at[0]),
        (pool_in.at[1], pool.at[1]),
    ]
    copies = [pltpu.make_async_copy(a, b, sems.at[i]) for i, (a, b) in enumerate(pairs)]
    for copy in copies:
        copy.start()
    outs = (o0, o1, o2, o3)
    lane = lanes()
    copies[0].wait()
    for h in range(GROUP):
        wide[:, h, :] = q[:, h * DH : (h + 1) * DH].astype(F32)
    copies[1].wait()
    for p in range(8):
        slots[32 + p] = 0
    order = jnp.zeros((GROUP, DH), F32)
    for n in range(32):
        p = prompt[n]
        k = slots[32 + p]
        slots[32 + p] = k + 1
        slots[n] = (4 * p + k) ^ place[0]
        order = jnp.where(lane == n, (4 * p + k).astype(F32), order)
    for copy in copies[2:6]:
        copy.wait()
    base = place[1]
    for n in range(32):
        keys = jnp.concatenate([pool[0, table[j, n] - base] for j in range(8)], axis=0)
        s = dot(wide[n].astype(BF16), keys, NT) * SCALE
        scores[n] = jnp.where(lane < length[n], s, -1e30)
    own_keys = new[0].astype(F32)
    own_values = new[1].astype(F32)
    own = jnp.stack(
        [jnp.sum(wide[n] * own_keys[n : n + 1], axis=1, keepdims=True) for n in range(32)]
    ) * SCALE
    s = scores[...]
    peak = jnp.maximum(jnp.max(s, axis=2, keepdims=True), own)
    w = jnp.exp(s - peak)
    own_weight = jnp.exp(own - peak)
    total = jnp.sum(w, axis=2, keepdims=True) + own_weight
    weights[...] = w.astype(BF16)
    own_weight = own_weight.astype(BF16).astype(F32)
    mass = peak + jnp.log(total)
    inverse = 1.0 / total
    copies[6].wait()
    for n in range(32):
        values = jnp.concatenate([pool[1, table[j, n] - base] for j in range(8)], axis=0)
        mixed = dot(weights[n], values) + own_weight[n] * own_values[n : n + 1]
        scores[slots[n]] = mixed * inverse[n]
    held = [jnp.zeros((GROUP, DH), F32) for _ in range(4)]
    for n in range(32):
        slot = slots[n]
        weights[slot] = wide[n].astype(BF16)
        for i in range(4):
            held[i] = jnp.where(lane + 8 * i == slot, jnp.where(lane < 8, mass[n], 0.0), held[i])
    for i, out in enumerate(outs):
        out[0:8] = weights[8 * i : 8 * i + 8]
        out[8] = order.astype(BF16)
        out[9:17] = scores[8 * i : 8 * i + 8].astype(BF16)
        out[17] = split_tile(jnp.where(lane < 8, held[i], 0.0), 8)


def local_parts(place, q, prompt, table, length, new, pool):
    out = jax.ShapeDtypeStruct((18, GROUP, DH), BF16)
    return pl.pallas_call(
        local_body,
        out_shape=[out] * 4,
        in_specs=[SMEM] + [HBM] * 6,
        out_specs=[VMEM] * 4,
        scratch_shapes=[
            pltpu.VMEM((32, GROUP * DH), BF16),
            pltpu.SMEM((32,), jnp.int32),
            pltpu.SMEM((8, 32), jnp.int32),
            pltpu.SMEM((32,), jnp.int32),
            pltpu.VMEM((2, 32, DH), BF16),
            pltpu.VMEM((2, 256, GROUP, DH), BF16),
            pltpu.VMEM((32, GROUP, DH), F32),
            pltpu.VMEM((32, GROUP, DH), F32),
            pltpu.VMEM((32, GROUP, DH), BF16),
            pltpu.SMEM((40,), jnp.int32),
            pltpu.SemaphoreType.DMA((7,)),
        ],
        compiler_params=params(54),
        name="local_parts",
    )(place, q, prompt, table, length, new, pool)


def regroup_body(place, a0, a1, a2, a3, same, other, across):
    for i, a in enumerate((a0, a1, a2, a3)):
        same[4 * i : 4 * i + 4] = a[0:4]
        other[4 * i : 4 * i + 4] = a[4:8]
        across[4 * i : 4 * i + 4] = a[4:8]
        across[17 + 5 * i : 22 + 5 * i] = a[13:18]

        @pl.when(place[2] ^ (place[4] >> 1) == i)
        def _(a=a):
            same[16] = a[8]
            other[16] = a[8]
            across[16] = a[8]


def regroup(place, parts):
    out = jax.ShapeDtypeStruct((17, GROUP, DH), BF16)
    return pl.pallas_call(
        regroup_body,
        out_shape=[out, out, jax.ShapeDtypeStruct((37, GROUP, DH), BF16)],
        in_specs=[SMEM] + [VMEM] * 4,
        out_specs=[VMEM] * 3,
        compiler_params=params(),
        name="regroup",
    )(place, *parts)


ROWS = 128


def prefix_part(q, kv):
    s = dot(q, kv[0], NT)
    peak = jnp.max(s, axis=1, keepdims=True)
    w = jnp.exp2((s - peak) * (SCALE * LOG2E))
    return dot(w.astype(BF16), kv[1]), peak * SCALE, jnp.sum(w, axis=1, keepdims=True)


def prefix_block(q, kv0, kv1):
    mixed0, peak0, total0 = prefix_part(q, kv0)
    mixed1, peak1, total1 = prefix_part(q, kv1)
    top = jnp.maximum(peak0, peak1)
    f0, f1 = jnp.exp(peak0 - top), jnp.exp(peak1 - top)
    total = total0 * f0 + total1 * f1
    return (mixed0 * f0 + mixed1 * f1) * (1.0 / total), top + jnp.log(total)


COUNT = ROWS // GROUP


def prefix_send_body(qa, qb, kv0, kv1, after, later, out):
    lane = lanes()
    tile = jnp.zeros((GROUP, DH), F32)
    for half, q in enumerate((qa, qb)):
        for i in range(256 // ROWS):
            rows = q[i * COUNT : (i + 1) * COUNT].reshape(ROWS, DH)
            mixed, mass = prefix_block(rows, kv0, kv1)
            at = half * 16 + i * COUNT
            out[at : at + COUNT] = mixed.reshape(COUNT, GROUP, DH).astype(BF16)
            for n in range(COUNT):
                tile = jnp.where(lane == at + n, mass[n * GROUP : (n + 1) * GROUP], tile)
    out[32] = split_tile(tile, 32)


def prefix_keep_body(q, kv0, kv1, out, masses):
    for i in range(256 // ROWS):
        rows = q[i * COUNT : (i + 1) * COUNT].reshape(ROWS, DH)
        mixed, mass = prefix_block(rows, kv0, kv1)
        at = i * COUNT
        out[at : at + COUNT] = mixed.reshape(COUNT, GROUP, DH)
        masses[at : at + COUNT] = jnp.broadcast_to(mass, (ROWS, DH)).reshape(COUNT, GROUP, DH)


def prefix_cost(rows):
    return pl.CostEstimate(
        flops=4 * rows * 4096 * 128, bytes_accessed=2_500_000, transcendentals=rows * 4096
    )


def prefix_send(qa, qb, kv0, kv1, after, later):
    return pl.pallas_call(
        prefix_send_body,
        out_shape=jax.ShapeDtypeStruct((33, GROUP, DH), BF16),
        in_specs=[VMEM] * 4 + [ANY] * 2,
        out_specs=VMEM,
        compiler_params=params(24),
        cost_estimate=prefix_cost(512),
        name="prefix_send",
    )(qa, qb, kv0, kv1, after, later)


def prefix_keep(q, kv0, kv1):
    out = jax.ShapeDtypeStruct((16, GROUP, DH), F32)
    return pl.pallas_call(
        prefix_keep_body,
        out_shape=[out, out],
        in_specs=[VMEM] * 3,
        out_specs=[VMEM, VMEM],
        compiler_params=params(24),
        cost_estimate=prefix_cost(256),
        name="prefix_keep",
    )(q, kv0, kv1)


def combine_body(
    place, own, own_masses, cross, cross_masses, message, s0, s1, s2, s3, far, out, held
):
    x, y_high, z = place[2], place[3], place[4]
    theirs = join_tile(message[32], 32)
    near = [join_tile(s[17], 8) for s in (s0, s1, s2, s3)]
    across = [join_tile(far[21 + 5 * i], 8) for i in range(4)]
    for g in range(2):
        for kx in range(4):
            for k in range(4):
                n = g * 16 + kx * 4 + k
                at = kx * 4 + k
                a, la = ((own, own_masses), (cross, cross_masses))[g]
                a, la = a[at], la[at]
                b = message[n].astype(F32)
                lb = jnp.broadcast_to(theirs[:, n : n + 1], (GROUP, DH))
                if g == 0:
                    s = (s0, s1, s2, s3)[kx][9 + k].astype(F32)
                    ls = jnp.broadcast_to(near[kx][:, k : k + 1], (GROUP, DH))
                else:
                    s = far[17 + 5 * kx + k].astype(F32)
                    ls = jnp.broadcast_to(across[kx][:, 4 + k : 5 + k], (GROUP, DH))
                top = jnp.maximum(jnp.maximum(la, lb), ls)
                ea, eb, es = jnp.exp(la - top), jnp.exp(lb - top), jnp.exp(ls - top)
                row = (ea * a + eb * b + es * s) / (ea + eb + es)
                target = (x ^ kx) * 2 + (y_high ^ g)
                held[((target - z - 2) & 7) * 4 + k] = row
    for h in range(GROUP):
        out[:, h * DH : (h + 1) * DH] = held[:, h, :].astype(BF16)


def combine(place, own, cross, message, near, far):
    return pl.pallas_call(
        combine_body,
        out_shape=jax.ShapeDtypeStruct((32, GROUP * DH), BF16),
        in_specs=[SMEM] + [VMEM] * 10,
        out_specs=VMEM,
        scratch_shapes=[pltpu.VMEM((32, GROUP, DH), F32)],
        compiler_params=params(),
        name="combine",
    )(place, *own, *cross, message, *near, far)


def by_target(total):
    low = lax.broadcasted_iota(jnp.int32, (8, total.shape[1]), 0) < 4
    chunks = []
    for g in range(2):
        even, odd = [], []
        for j in (0, 2):
            first = total[j * 16 + g * 8 : j * 16 + g * 8 + 8]
            second = total[(j + 1) * 16 + g * 8 : (j + 1) * 16 + g * 8 + 8]
            even.append(jnp.where(low, first, pltpu.roll(second, 4, 0)))
            odd.append(jnp.where(low, pltpu.roll(first, 4, 0), second))
        chunks += [jnp.concatenate(even, axis=0), jnp.concatenate(odd, axis=0)]
    return chunks


def project_body(a, b, c, w0, w1, out):
    rows = jnp.concatenate([a[...], b[...], c[...]], axis=0)
    for side, weight in enumerate((w0, w1)):
        total = dot(rows, weight[...])
        for i in range(3):
            for d, chunk in enumerate(by_target(total[64 * i : 64 * i + 64])):
                out[d, i * 16 : i * 16 + 16, side * 512 : side * 512 + 512] = chunk


def project(blocks, weights):
    return pl.pallas_call(
        project_body,
        out_shape=jax.ShapeDtypeStruct((4, 48, 1024), F32),
        in_specs=[VMEM] * 5,
        out_specs=VMEM,
        compiler_params=params(),
        cost_estimate=pl.CostEstimate(
            flops=2 * 192 * 2048 * 1024, bytes_accessed=4_500_000, transcendentals=0
        ),
        name="project",
    )(*blocks, *weights)


def last_chunks(a, b, w0, w1, first):
    rows = jnp.concatenate([a[...], b[...]], axis=0)
    for side, weight in enumerate((w0, w1)):
        columns = slice(side * 512, side * 512 + 512)
        for d, chunk in enumerate(by_target(dot(rows, weight[...]))):
            yield side, columns, d, jnp.concatenate([first[d, :, columns], chunk], axis=0)


def far_body(a, b, w0, w1, first, keep, up, down):
    for side, columns, d, whole in last_chunks(a, b, w0, w1, first):
        if d == 0:
            keep[:, columns] = whole
        elif d == 1:
            up[side] = whole.astype(BF16)
        elif d == 3:
            down[side] = whole.astype(BF16)
        else:
            (up, down)[side][2] = whole.astype(BF16)


def near_body(a, b, w0, w1, first, out):
    for _, columns, d, whole in last_chunks(a, b, w0, w1, first):
        out[d, :, columns] = whole


def join_body(near, below, above, keep2, up1, down1, up2, down2):
    for side in range(2):
        columns = slice(side * 512, side * 512 + 512)
        up1[:, columns] = (near[3, :, columns] + below[side].astype(F32)).astype(BF16)
        down1[:, columns] = (near[1, :, columns] + above[side].astype(F32)).astype(BF16)
        low, high = keep2[:, columns], near[0, :, columns]
        if side == 0:
            low = low + below[2].astype(F32)
        else:
            high = high + above[2].astype(F32)
        up2[:, columns] = low.astype(BF16)
        down2[:, columns] = high.astype(BF16)


SUM = jax.ShapeDtypeStruct((64, 1024), F32)
SENT = jax.ShapeDtypeStruct((64, 1024), BF16)
HALF = jax.ShapeDtypeStruct((64, 512), BF16)
THREE = jax.ShapeDtypeStruct((3, 64, 512), BF16)


def plain(body, out_shape, *args):
    return pl.pallas_call(
        body,
        out_shape=out_shape,
        in_specs=[VMEM] * len(args),
        out_specs=[VMEM] * len(out_shape),
        compiler_params=params(),
        name=body.__name__[:-5],
    )(*args)


def total_body(near, below1, above1, below2, above2, own, other):
    whole = near[2] + below1[...].astype(F32) + above1[...].astype(F32)
    whole = (whole + below2[...].astype(F32) + above2[...].astype(F32)).astype(BF16)
    own[...] = whole[:, :512]
    other[...] = whole[:, 512:]


def order_body(place, orders, pick):
    x, y, core, z = place[2], place[3] * 2 + place[5], place[6], place[4]
    lane = lanes()
    order = jnp.zeros((GROUP, DH), F32)
    for block in range(4):
        dy = (2 * (z & 1) + block // 2) ^ y
        tile = orders[((block % 2) ^ core) * 4 + dy].astype(F32)
        order = jnp.where(lane >> 5 == block, pltpu.roll(tile, 32 * block, 1), order)
    order = order.astype(jnp.int32)
    prompt, k = order >> 2, order & 3
    block = lane >> 5
    far = block & 1
    dx = (prompt >> 1) ^ x
    dy = (2 * (prompt & 1) + (block >> 1)) ^ y
    first = jnp.where(far == 0, dx, dy)
    second = jnp.where(far == 0, dy, dx)
    second = jnp.where(second >= 2, 5 - second, second)
    source = ((far ^ core) * 16 + second * 4 + first) * 4 + k
    row = lax.broadcasted_iota(jnp.int32, (128, 128), 0)
    pick[...] = (row == source[0:1]).astype(F32).astype(BF16)


def order_rows(place, orders):
    return pl.pallas_call(
        order_body,
        out_shape=jax.ShapeDtypeStruct((128, 128), BF16),
        in_specs=[SMEM, VMEM],
        out_specs=VMEM,
        compiler_params=params(),
        name="order_rows",
    )(place, orders)


def finish_body(own, other, pick, out):
    dims = (((0,), (0,)), ((), ()))
    mixed = dot(pick[0:64], own[...], dims) + dot(pick[64:128], other[...], dims)
    out[...] = mixed.astype(BF16)


def finish(own, other, pick):
    return pl.pallas_call(
        finish_body,
        out_shape=jax.ShapeDtypeStruct((128, 512), BF16),
        in_specs=[VMEM] * 3,
        out_specs=VMEM,
        compiler_params=params(),
        name="finish",
    )(own, other, pick)


def along(value, shift, k):
    return lax.ppermute(value, "batch", [(i, i ^ (k << shift)) for i in range(BATCH)])


def along_x(value, k):
    return along(value, 3, k)


def along_y(value, k):
    return along(value, 1, k)


def other_core(value):
    return along(value, 0, 1)


def turned(value, k, phase):
    pairs = [(i, i ^ (k << (3 if (i & 1) == phase else 1))) for i in range(BATCH)]
    return lax.ppermute(value, "batch", pairs)


def gathered(parts):
    ring0 = jnp.concatenate(parts, axis=0)
    ring1, ring3 = turned(ring0, 1, 1), turned(ring0, 3, 1)
    return ring0, ring1, ring3, [turned(ring3[:32], 1, 1), turned(ring1[32:], 3, 1)]


def along_z(value, k):
    return lax.ppermute(value, "head", [(i, (i + k) % HEADS) for i in range(HEADS)])


def shards(queries, new_kv, prefix_kv, suffix_kv, page_table, suffix_len, prompt_of, out_weight):
    me = lax.axis_index("batch")
    z = lax.axis_index("head")
    x, y, core = me // 8, (me // 2) % 4, me % 2
    place = [8 * x + 4 * (y // 2), me * 256, x, y // 2, z, y % 2, core]
    place = jnp.stack(place).astype(jnp.int32)

    prefix_other = other_core(prefix_kv)
    weights = [out_weight, other_core(out_weight)]

    sent = local_parts(place, queries, prompt_of, page_table.T, suffix_len, new_kv, suffix_kv)
    by_x = [sent[0]] + [along_x(sent[k], k) for k in (1, 2, 3)]
    same, other, across = regroup(place, by_x)
    from1, from3, from2 = along_y(same, 1), along_y(other, 3), along_y(across, 2)

    own = prefix_keep(same, prefix_kv, prefix_other)
    message = along_y(prefix_send(from1, from3, prefix_kv, prefix_other, own[1], from2), 1)
    cross = prefix_keep(from2, prefix_kv, prefix_other)
    attended = combine(place, own, cross, message, by_x, from2)

    orders = jnp.stack([same[16], from1[16], from2[16], from3[16]])
    orders = jnp.concatenate([orders, other_core(orders)], axis=0)
    pick = order_rows(place, orders)

    parts = [attended] + [turned(attended, k, 0) for k in (1, 2, 3)]
    far = gathered([a[:16] for a in parts])
    late = lax.optimization_barrier((tuple(a[16:] for a in parts), far[1], far[2]))[0]
    near = gathered(list(late))
    first_far, first_near = project(far[:3], weights), project(near[:3], weights)
    keep2, up, down = plain(far_body, [SUM, THREE, THREE], *far[3], *weights, first_far)
    below, above = along_z(up, 2), along_z(down, -2)
    sums = jax.ShapeDtypeStruct((4, 64, 1024), F32)
    (sums,) = plain(near_body, [sums], *near[3], *weights, first_near)
    up1, down1, up2, down2 = plain(join_body, [SENT] * 4, sums, below, above, keep2)
    below1, above1 = along_z(up1, 1), along_z(down1, -1)
    below2, above2 = along_z(up2, 2), along_z(down2, -2)
    own, other = plain(total_body, [HALF, HALF], sums, below1, above1, below2, above2)
    return finish(own, other_core(other), pick)


def solution(mesh):
    placed = (
        P("batch", "head"),
        P(None, "batch", "head"),
        P(None, "batch", "head"),
        P(None, "batch", None, "head"),
        P("batch", None),
        P("batch"),
        P("batch"),
        P("head", "batch"),
    )
    return jax.shard_map(
        shards, mesh=mesh, in_specs=placed, out_specs=P("head", "batch"), check_vma=False
    )
```

```python
import jax
import jax.numpy as jnp
from jax import lax
from jax.experimental import pallas as pl
from jax.experimental.pallas import tpu as pltpu
from jax.sharding import PartitionSpec as P

DH = 128
GROUP = 16
SCALE = DH**-0.5
LOG2E = 1.4426950408889634
BATCH = 32
HEADS = 8
VMEM = pl.BlockSpec(memory_space=pltpu.VMEM)
SMEM = pl.BlockSpec(memory_space=pltpu.SMEM)
F32 = jnp.float32
BF16 = jnp.bfloat16
NT = (((1,), (1,)), ((), ()))
NN = (((1,), (0,)), ((), ()))


ANY = pl.BlockSpec(memory_space=pl.ANY)
HBM = pl.BlockSpec(memory_space=pltpu.HBM)


def params(mib=16):
    return pltpu.CompilerParams(vmem_limit_bytes=mib * 1024 * 1024)


def dot(a, b, dims=NN):
    return lax.dot_general(a, b, dims, preferred_element_type=F32)


def lanes():
    return lax.broadcasted_iota(jnp.int32, (GROUP, DH), 1)


def split_tile(tile, step):
    high = tile.astype(BF16).astype(F32)
    rest = tile - high
    middle = rest.astype(BF16).astype(F32)
    low = rest - middle
    joined = high + pltpu.roll(middle, step, 1) + pltpu.roll(low, 2 * step, 1)
    return joined.astype(BF16)


def join_tile(tile, step):
    wide = tile.astype(F32)
    return (wide + pltpu.roll(wide, DH - step, 1)) + pltpu.roll(wide, DH - 2 * step, 1)


def local_body(
    place, q_in, prompt_in, table_in, length_in, new_in, pool_in, o0, o1, o2, o3,
    q, prompt, table, length, new, pool, wide, scores, weights, slots, sems,
):
    pairs = [
        (q_in, q),
        (prompt_in, prompt),
        (table_in, table),
        (length_in, length),
        (new_in, new),
        (pool_in.at[0], pool.at[0]),
        (pool_in.at[1], pool.at[1]),
    ]
    copies = [pltpu.make_async_copy(a, b, sems.at[i]) for i, (a, b) in enumerate(pairs)]
    for copy in copies:
        copy.start()
    outs = (o0, o1, o2, o3)
    lane = lanes()
    copies[0].wait()
    for h in range(GROUP):
        wide[:, h, :] = q[:, h * DH : (h + 1) * DH].astype(F32)
    copies[1].wait()
    for p in range(8):
        slots[32 + p] = 0
    order = jnp.zeros((GROUP, DH), F32)
    for n in range(32):
        p = prompt[n]
        k = slots[32 + p]
        slots[32 + p] = k + 1
        slots[n] = (4 * p + k) ^ place[0]
        order = jnp.where(lane == n, (4 * p + k).astype(F32), order)
    for copy in copies[2:6]:
        copy.wait()
    base = place[1]
    for n in range(32):
        keys = jnp.concatenate([pool[0, table[j, n] - base] for j in range(8)], axis=0)
        s = dot(wide[n].astype(BF16), keys, NT) * SCALE
        scores[n] = jnp.where(lane < length[n], s, -1e30)
    own_keys = new[0].astype(F32)
    own_values = new[1].astype(F32)
    own = jnp.stack(
        [jnp.sum(wide[n] * own_keys[n : n + 1], axis=1, keepdims=True) for n in range(32)]
    ) * SCALE
    s = scores[...]
    peak = jnp.maximum(jnp.max(s, axis=2, keepdims=True), own)
    w = jnp.exp(s - peak)
    own_weight = jnp.exp(own - peak)
    total = jnp.sum(w, axis=2, keepdims=True) + own_weight
    weights[...] = w.astype(BF16)
    own_weight = own_weight.astype(BF16).astype(F32)
    mass = peak + jnp.log(total)
    inverse = 1.0 / total
    copies[6].wait()
    for n in range(32):
        values = jnp.concatenate([pool[1, table[j, n] - base] for j in range(8)], axis=0)
        mixed = dot(weights[n], values) + own_weight[n] * own_values[n : n + 1]
        scores[slots[n]] = mixed * inverse[n]
    held = [jnp.zeros((GROUP, DH), F32) for _ in range(4)]
    for n in range(32):
        slot = slots[n]
        weights[slot] = wide[n].astype(BF16)
        for i in range(4):
            held[i] = jnp.where(lane + 8 * i == slot, jnp.where(lane < 8, mass[n], 0.0), held[i])
    for i, out in enumerate(outs):
        out[0:8] = weights[8 * i : 8 * i + 8]
        out[8] = order.astype(BF16)
        out[9:17] = scores[8 * i : 8 * i + 8].astype(BF16)
        out[17] = split_tile(jnp.where(lane < 8, held[i], 0.0), 8)


def local_parts(place, q, prompt, table, length, new, pool):
    out = jax.ShapeDtypeStruct((18, GROUP, DH), BF16)
    return pl.pallas_call(
        local_body,
        out_shape=[out] * 4,
        in_specs=[SMEM] + [HBM] * 6,
        out_specs=[VMEM] * 4,
        scratch_shapes=[
            pltpu.VMEM((32, GROUP * DH), BF16),
            pltpu.SMEM((32,), jnp.int32),
            pltpu.SMEM((8, 32), jnp.int32),
            pltpu.SMEM((32,), jnp.int32),
            pltpu.VMEM((2, 32, DH), BF16),
            pltpu.VMEM((2, 256, GROUP, DH), BF16),
            pltpu.VMEM((32, GROUP, DH), F32),
            pltpu.VMEM((32, GROUP, DH), F32),
            pltpu.VMEM((32, GROUP, DH), BF16),
            pltpu.SMEM((40,), jnp.int32),
            pltpu.SemaphoreType.DMA((7,)),
        ],
        compiler_params=params(54),
        name="local_parts",
    )(place, q, prompt, table, length, new, pool)


def regroup_body(place, a0, a1, a2, a3, same, other, across):
    for i, a in enumerate((a0, a1, a2, a3)):
        same[4 * i : 4 * i + 4] = a[0:4]
        other[4 * i : 4 * i + 4] = a[4:8]
        across[4 * i : 4 * i + 4] = a[4:8]
        across[17 + 5 * i : 22 + 5 * i] = a[13:18]

        @pl.when(place[2] ^ (place[4] >> 1) == i)
        def _(a=a):
            same[16] = a[8]
            other[16] = a[8]
            across[16] = a[8]


def regroup(place, parts):
    out = jax.ShapeDtypeStruct((17, GROUP, DH), BF16)
    return pl.pallas_call(
        regroup_body,
        out_shape=[out, out, jax.ShapeDtypeStruct((37, GROUP, DH), BF16)],
        in_specs=[SMEM] + [VMEM] * 4,
        out_specs=[VMEM] * 3,
        compiler_params=params(),
        name="regroup",
    )(place, *parts)


ROWS = 128


def prefix_part(q, kv):
    s = dot(q, kv[0], NT)
    peak = jnp.max(s, axis=1, keepdims=True)
    w = jnp.exp2((s - peak) * (SCALE * LOG2E))
    return dot(w.astype(BF16), kv[1]), peak * SCALE, jnp.sum(w, axis=1, keepdims=True)


def prefix_block(q, kv0, kv1):
    mixed0, peak0, total0 = prefix_part(q, kv0)
    mixed1, peak1, total1 = prefix_part(q, kv1)
    top = jnp.maximum(peak0, peak1)
    f0, f1 = jnp.exp(peak0 - top), jnp.exp(peak1 - top)
    total = total0 * f0 + total1 * f1
    return (mixed0 * f0 + mixed1 * f1) * (1.0 / total), top + jnp.log(total)


COUNT = ROWS // GROUP


def prefix_send_body(qa, qb, kv0, kv1, after, later, out):
    lane = lanes()
    tile = jnp.zeros((GROUP, DH), F32)
    for half, q in enumerate((qa, qb)):
        for i in range(256 // ROWS):
            rows = q[i * COUNT : (i + 1) * COUNT].reshape(ROWS, DH)
            mixed, mass = prefix_block(rows, kv0, kv1)
            at = half * 16 + i * COUNT
            out[at : at + COUNT] = mixed.reshape(COUNT, GROUP, DH).astype(BF16)
            for n in range(COUNT):
                tile = jnp.where(lane == at + n, mass[n * GROUP : (n + 1) * GROUP], tile)
    out[32] = split_tile(tile, 32)


def prefix_keep_body(q, kv0, kv1, out, masses):
    for i in range(256 // ROWS):
        rows = q[i * COUNT : (i + 1) * COUNT].reshape(ROWS, DH)
        mixed, mass = prefix_block(rows, kv0, kv1)
        at = i * COUNT
        out[at : at + COUNT] = mixed.reshape(COUNT, GROUP, DH)
        masses[at : at + COUNT] = jnp.broadcast_to(mass, (ROWS, DH)).reshape(COUNT, GROUP, DH)


def prefix_cost(rows):
    return pl.CostEstimate(
        flops=4 * rows * 4096 * 128, bytes_accessed=2_500_000, transcendentals=rows * 4096
    )


def prefix_send(qa, qb, kv0, kv1, after, later):
    return pl.pallas_call(
        prefix_send_body,
        out_shape=jax.ShapeDtypeStruct((33, GROUP, DH), BF16),
        in_specs=[VMEM] * 4 + [ANY] * 2,
        out_specs=VMEM,
        compiler_params=params(24),
        cost_estimate=prefix_cost(512),
        name="prefix_send",
    )(qa, qb, kv0, kv1, after, later)


def prefix_keep(q, kv0, kv1):
    out = jax.ShapeDtypeStruct((16, GROUP, DH), F32)
    return pl.pallas_call(
        prefix_keep_body,
        out_shape=[out, out],
        in_specs=[VMEM] * 3,
        out_specs=[VMEM, VMEM],
        compiler_params=params(24),
        cost_estimate=prefix_cost(256),
        name="prefix_keep",
    )(q, kv0, kv1)


def combine_body(
    place, own, own_masses, cross, cross_masses, message, s0, s1, s2, s3, far, out, held
):
    x, y_high, z = place[2], place[3], place[4]
    theirs = join_tile(message[32], 32)
    near = [join_tile(s[17], 8) for s in (s0, s1, s2, s3)]
    across = [join_tile(far[21 + 5 * i], 8) for i in range(4)]
    for g in range(2):
        for kx in range(4):
            for k in range(4):
                n = g * 16 + kx * 4 + k
                at = kx * 4 + k
                a, la = ((own, own_masses), (cross, cross_masses))[g]
                a, la = a[at], la[at]
                b = message[n].astype(F32)
                lb = jnp.broadcast_to(theirs[:, n : n + 1], (GROUP, DH))
                if g == 0:
                    s = (s0, s1, s2, s3)[kx][9 + k].astype(F32)
                    ls = jnp.broadcast_to(near[kx][:, k : k + 1], (GROUP, DH))
                else:
                    s = far[17 + 5 * kx + k].astype(F32)
                    ls = jnp.broadcast_to(across[kx][:, 4 + k : 5 + k], (GROUP, DH))
                top = jnp.maximum(jnp.maximum(la, lb), ls)
                ea, eb, es = jnp.exp(la - top), jnp.exp(lb - top), jnp.exp(ls - top)
                row = (ea * a + eb * b + es * s) / (ea + eb + es)
                target = (x ^ kx) * 2 + (y_high ^ g)
                held[((target - z - 2) & 7) * 4 + k] = row
    for h in range(GROUP):
        out[:, h * DH : (h + 1) * DH] = held[:, h, :].astype(BF16)


def combine(place, own, cross, message, near, far):
    return pl.pallas_call(
        combine_body,
        out_shape=jax.ShapeDtypeStruct((32, GROUP * DH), BF16),
        in_specs=[SMEM] + [VMEM] * 10,
        out_specs=VMEM,
        scratch_shapes=[pltpu.VMEM((32, GROUP, DH), F32)],
        compiler_params=params(),
        name="combine",
    )(place, *own, *cross, message, *near, far)


def by_target(total):
    low = lax.broadcasted_iota(jnp.int32, (8, total.shape[1]), 0) < 4
    chunks = []
    for g in range(2):
        even, odd = [], []
        for j in (0, 2):
            first = total[j * 16 + g * 8 : j * 16 + g * 8 + 8]
            second = total[(j + 1) * 16 + g * 8 : (j + 1) * 16 + g * 8 + 8]
            even.append(jnp.where(low, first, pltpu.roll(second, 4, 0)))
            odd.append(jnp.where(low, pltpu.roll(first, 4, 0), second))
        chunks += [jnp.concatenate(even, axis=0), jnp.concatenate(odd, axis=0)]
    return chunks


def project_body(a, b, c, w0, w1, out):
    rows = jnp.concatenate([a[...], b[...], c[...]], axis=0)
    for side, weight in enumerate((w0, w1)):
        total = dot(rows, weight[...])
        for i in range(3):
            for d, chunk in enumerate(by_target(total[64 * i : 64 * i + 64])):
                out[d, i * 16 : i * 16 + 16, side * 512 : side * 512 + 512] = chunk


def project(blocks, weights):
    return pl.pallas_call(
        project_body,
        out_shape=jax.ShapeDtypeStruct((4, 48, 1024), F32),
        in_specs=[VMEM] * 5,
        out_specs=VMEM,
        compiler_params=params(),
        cost_estimate=pl.CostEstimate(
            flops=2 * 192 * 2048 * 1024, bytes_accessed=4_500_000, transcendentals=0
        ),
        name="project",
    )(*blocks, *weights)


def last_chunks(a, b, w0, w1, first):
    rows = jnp.concatenate([a[...], b[...]], axis=0)
    for side, weight in enumerate((w0, w1)):
        columns = slice(side * 512, side * 512 + 512)
        for d, chunk in enumerate(by_target(dot(rows, weight[...]))):
            yield side, columns, d, jnp.concatenate([first[d, :, columns], chunk], axis=0)


def far_body(a, b, w0, w1, first, keep, up, down, direct):
    for _, columns, d, whole in last_chunks(a, b, w0, w1, first):
        if d == 0:
            keep[:, columns] = whole
        else:
            (up, direct, down)[d - 1][:, columns] = whole.astype(BF16)


def near_body(a, b, w0, w1, first, keep6, down, keep0, up):
    for _, columns, d, whole in last_chunks(a, b, w0, w1, first):
        if d in (0, 2):
            (keep6, keep0)[d // 2][:, columns] = whole
        else:
            (down, up)[d // 2][:, columns] = whole.astype(BF16)


SUM = jax.ShapeDtypeStruct((64, 1024), F32)
SENT = jax.ShapeDtypeStruct((64, 1024), BF16)
HALF = jax.ShapeDtypeStruct((64, 512), BF16)


def plain(body, out_shape, *args):
    return pl.pallas_call(
        body,
        out_shape=out_shape,
        in_specs=[VMEM] * len(args),
        out_specs=[VMEM] * len(out_shape),
        compiler_params=params(),
        name=body.__name__[:-5],
    )(*args)


def middle_body(keep2, keep6, below, above, up, down):
    up[...] = (keep2[...] + below[...].astype(F32)).astype(BF16)
    down[...] = (keep6[...] + above[...].astype(F32)).astype(BF16)


def total_body(keep, below1, above1, below2, above2, opposite, own, other):
    near = keep[...] + below1[...].astype(F32) + above1[...].astype(F32)
    whole = near + below2[...].astype(F32) + above2[...].astype(F32)
    whole = (whole + opposite[...].astype(F32)).astype(BF16)
    own[...] = whole[:, :512]
    other[...] = whole[:, 512:]


def order_body(place, orders, pick):
    x, y, core, z = place[2], place[3] * 2 + place[5], place[6], place[4]
    lane = lanes()
    order = jnp.zeros((GROUP, DH), F32)
    for block in range(4):
        dy = (2 * (z & 1) + block // 2) ^ y
        tile = orders[((block % 2) ^ core) * 4 + dy].astype(F32)
        order = jnp.where(lane >> 5 == block, pltpu.roll(tile, 32 * block, 1), order)
    order = order.astype(jnp.int32)
    prompt, k = order >> 2, order & 3
    block = lane >> 5
    far = block & 1
    dx = (prompt >> 1) ^ x
    dy = (2 * (prompt & 1) + (block >> 1)) ^ y
    first = jnp.where(far == 0, dx, dy)
    second = jnp.where(far == 0, dy, dx)
    second = jnp.where(second >= 2, 5 - second, second)
    source = ((far ^ core) * 16 + second * 4 + first) * 4 + k
    row = lax.broadcasted_iota(jnp.int32, (128, 128), 0)
    pick[...] = (row == source[0:1]).astype(F32).astype(BF16)


def order_rows(place, orders):
    return pl.pallas_call(
        order_body,
        out_shape=jax.ShapeDtypeStruct((128, 128), BF16),
        in_specs=[SMEM, VMEM],
        out_specs=VMEM,
        compiler_params=params(),
        name="order_rows",
    )(place, orders)


def finish_body(own, other, pick, out):
    dims = (((0,), (0,)), ((), ()))
    mixed = dot(pick[0:64], own[...], dims) + dot(pick[64:128], other[...], dims)
    out[...] = mixed.astype(BF16)


def finish(own, other, pick):
    return pl.pallas_call(
        finish_body,
        out_shape=jax.ShapeDtypeStruct((128, 512), BF16),
        in_specs=[VMEM] * 3,
        out_specs=VMEM,
        compiler_params=params(),
        name="finish",
    )(own, other, pick)


def along(value, shift, k):
    return lax.ppermute(value, "batch", [(i, i ^ (k << shift)) for i in range(BATCH)])


def along_x(value, k):
    return along(value, 3, k)


def along_y(value, k):
    return along(value, 1, k)


def other_core(value):
    return along(value, 0, 1)


def turned(value, k, phase):
    pairs = [(i, i ^ (k << (3 if (i & 1) == phase else 1))) for i in range(BATCH)]
    return lax.ppermute(value, "batch", pairs)


def gathered(parts):
    ring0 = jnp.concatenate(parts, axis=0)
    ring1, ring3 = turned(ring0, 1, 1), turned(ring0, 3, 1)
    return ring0, ring1, ring3, [turned(ring3[:32], 1, 1), turned(ring1[32:], 3, 1)]


def along_z(value, k):
    return lax.ppermute(value, "head", [(i, (i + k) % HEADS) for i in range(HEADS)])


def shards(queries, new_kv, prefix_kv, suffix_kv, page_table, suffix_len, prompt_of, out_weight):
    me = lax.axis_index("batch")
    z = lax.axis_index("head")
    x, y, core = me // 8, (me // 2) % 4, me % 2
    place = [8 * x + 4 * (y // 2), me * 256, x, y // 2, z, y % 2, core]
    place = jnp.stack(place).astype(jnp.int32)

    prefix_other = other_core(prefix_kv)
    weights = [out_weight, other_core(out_weight)]

    sent = local_parts(place, queries, prompt_of, page_table.T, suffix_len, new_kv, suffix_kv)
    by_x = [sent[0]] + [along_x(sent[k], k) for k in (1, 2, 3)]
    same, other, across = regroup(place, by_x)
    from1, from3, from2 = along_y(same, 1), along_y(other, 3), along_y(across, 2)

    own = prefix_keep(same, prefix_kv, prefix_other)
    message = along_y(prefix_send(from1, from3, prefix_kv, prefix_other, own[1], from2), 1)
    cross = prefix_keep(from2, prefix_kv, prefix_other)
    attended = combine(place, own, cross, message, by_x, from2)

    orders = jnp.stack([same[16], from1[16], from2[16], from3[16]])
    orders = jnp.concatenate([orders, other_core(orders)], axis=0)
    pick = order_rows(place, orders)

    parts = [attended] + [turned(attended, k, 0) for k in (1, 2, 3)]
    far, near = [gathered([a[i : i + 16] for a in parts]) for i in (0, 16)]
    first_far, first_near = project(far[:3], weights), project(near[:3], weights)
    keep2, up3, down3, up4 = plain(
        far_body, [SUM, SENT, SENT, SENT], *far[3], *weights, first_far
    )
    below3, above3 = along_z(up3, 1), along_z(down3, -1)
    opposite = along_z(up4, 4)
    keep6, down1, keep0, up1 = plain(
        near_body, [SUM, SENT, SUM, SENT], *near[3], *weights, first_near
    )
    below1, above1 = along_z(up1, 1), along_z(down1, -1)
    up2, down2 = plain(middle_body, [SENT, SENT], keep2, keep6, below3, above3)
    below2, above2 = along_z(up2, 2), along_z(down2, -2)
    own, other = plain(total_body, [HALF, HALF], keep0, below1, above1, below2, above2, opposite)
    return finish(own, other_core(other), pick)


def solution(mesh):
    placed = (
        P("batch", "head"),
        P(None, "batch", "head"),
        P(None, "batch", "head"),
        P(None, "batch", None, "head"),
        P("batch", None),
        P("batch"),
        P("batch"),
        P("head", "batch"),
    )
    return jax.shard_map(
        shards, mesh=mesh, in_specs=placed, out_specs=P("head", "batch"), check_vma=False
    )
```

```python
import jax
import jax.numpy as jnp
from jax import lax
from jax.experimental import pallas as pl
from jax.experimental.pallas import tpu as pltpu
from jax.sharding import PartitionSpec as P

DH = 128
GROUP = 16
SCALE = DH**-0.5
LOG2E = 1.4426950408889634
BATCH = 32
HEADS = 8
VMEM = pl.BlockSpec(memory_space=pltpu.VMEM)
SMEM = pl.BlockSpec(memory_space=pltpu.SMEM)
F32 = jnp.float32
BF16 = jnp.bfloat16
NT = (((1,), (1,)), ((), ()))
NN = (((1,), (0,)), ((), ()))


ANY = pl.BlockSpec(memory_space=pl.ANY)
HBM = pl.BlockSpec(memory_space=pltpu.HBM)


def params(mib=16):
    return pltpu.CompilerParams(vmem_limit_bytes=mib * 1024 * 1024)


def dot(a, b, dims=NN):
    return lax.dot_general(a, b, dims, preferred_element_type=F32)


def lanes():
    return lax.broadcasted_iota(jnp.int32, (GROUP, DH), 1)


def split_tile(tile, step):
    high = tile.astype(BF16).astype(F32)
    rest = tile - high
    middle = rest.astype(BF16).astype(F32)
    low = rest - middle
    joined = high + pltpu.roll(middle, step, 1) + pltpu.roll(low, 2 * step, 1)
    return joined.astype(BF16)


def join_tile(tile, step):
    wide = tile.astype(F32)
    return (wide + pltpu.roll(wide, DH - step, 1)) + pltpu.roll(wide, DH - 2 * step, 1)


def local_body(
    place, q_in, prompt_in, table_in, length_in, new_in, pool_in, o0, o1, o2, o3,
    q, prompt, table, length, new, pool, wide, scores, weights, slots, sems,
):
    pairs = [
        (q_in, q),
        (prompt_in, prompt),
        (table_in, table),
        (length_in, length),
        (new_in, new),
        (pool_in.at[0], pool.at[0]),
        (pool_in.at[1], pool.at[1]),
    ]
    copies = [pltpu.make_async_copy(a, b, sems.at[i]) for i, (a, b) in enumerate(pairs)]
    for copy in copies:
        copy.start()
    outs = (o0, o1, o2, o3)
    lane = lanes()
    copies[0].wait()
    for h in range(GROUP):
        wide[:, h, :] = q[:, h * DH : (h + 1) * DH].astype(F32)
    copies[1].wait()
    for p in range(8):
        slots[32 + p] = 0
    order = jnp.zeros((GROUP, DH), F32)
    for n in range(32):
        p = prompt[n]
        k = slots[32 + p]
        slots[32 + p] = k + 1
        slots[n] = (4 * p + k) ^ place[0]
        order = jnp.where(lane == n, (4 * p + k).astype(F32), order)
    for copy in copies[2:6]:
        copy.wait()
    base = place[1]
    for n in range(32):
        keys = jnp.concatenate([pool[0, table[j, n] - base] for j in range(8)], axis=0)
        s = dot(wide[n].astype(BF16), keys, NT) * SCALE
        scores[n] = jnp.where(lane < length[n], s, -1e30)
    own_keys = new[0].astype(F32)
    own_values = new[1].astype(F32)
    own = jnp.stack(
        [jnp.sum(wide[n] * own_keys[n : n + 1], axis=1, keepdims=True) for n in range(32)]
    ) * SCALE
    s = scores[...]
    peak = jnp.maximum(jnp.max(s, axis=2, keepdims=True), own)
    w = jnp.exp(s - peak)
    own_weight = jnp.exp(own - peak)
    total = jnp.sum(w, axis=2, keepdims=True) + own_weight
    weights[...] = w.astype(BF16)
    own_weight = own_weight.astype(BF16).astype(F32)
    mass = peak + jnp.log(total)
    inverse = 1.0 / total
    copies[6].wait()
    for n in range(32):
        values = jnp.concatenate([pool[1, table[j, n] - base] for j in range(8)], axis=0)
        mixed = dot(weights[n], values) + own_weight[n] * own_values[n : n + 1]
        scores[slots[n]] = mixed * inverse[n]
    held = [jnp.zeros((GROUP, DH), F32) for _ in range(4)]
    for n in range(32):
        slot = slots[n]
        weights[slot] = wide[n].astype(BF16)
        for i in range(4):
            held[i] = jnp.where(lane + 8 * i == slot, jnp.where(lane < 8, mass[n], 0.0), held[i])
    for i, out in enumerate(outs):
        out[0:8] = weights[8 * i : 8 * i + 8]
        out[8] = order.astype(BF16)
        out[9:17] = scores[8 * i : 8 * i + 8].astype(BF16)
        out[17] = split_tile(jnp.where(lane < 8, held[i], 0.0), 8)


def local_parts(place, q, prompt, table, length, new, pool):
    out = jax.ShapeDtypeStruct((18, GROUP, DH), BF16)
    return pl.pallas_call(
        local_body,
        out_shape=[out] * 4,
        in_specs=[SMEM] + [HBM] * 6,
        out_specs=[VMEM] * 4,
        scratch_shapes=[
            pltpu.VMEM((32, GROUP * DH), BF16),
            pltpu.SMEM((32,), jnp.int32),
            pltpu.SMEM((8, 32), jnp.int32),
            pltpu.SMEM((32,), jnp.int32),
            pltpu.VMEM((2, 32, DH), BF16),
            pltpu.VMEM((2, 256, GROUP, DH), BF16),
            pltpu.VMEM((32, GROUP, DH), F32),
            pltpu.VMEM((32, GROUP, DH), F32),
            pltpu.VMEM((32, GROUP, DH), BF16),
            pltpu.SMEM((40,), jnp.int32),
            pltpu.SemaphoreType.DMA((7,)),
        ],
        compiler_params=params(54),
        name="local_parts",
    )(place, q, prompt, table, length, new, pool)


def regroup_body(place, a0, a1, a2, a3, same, across):
    for i, a in enumerate((a0, a1, a2, a3)):
        same[4 * i : 4 * i + 4] = a[0:4]
        across[4 * i : 4 * i + 4] = a[4:8]
        across[17 + 5 * i : 22 + 5 * i] = a[13:18]

        @pl.when(place[2] ^ (place[4] >> 1) == i)
        def _(a=a):
            same[16] = a[8]
            across[16] = a[8]


def regroup(place, parts):
    return pl.pallas_call(
        regroup_body,
        out_shape=[
            jax.ShapeDtypeStruct((17, GROUP, DH), BF16),
            jax.ShapeDtypeStruct((37, GROUP, DH), BF16),
        ],
        in_specs=[SMEM] + [VMEM] * 4,
        out_specs=[VMEM] * 2,
        compiler_params=params(),
        name="regroup",
    )(place, *parts)


ROWS = 128


def prefix_part(q, kv):
    s = dot(q, kv[0], NT)
    peak = jnp.max(s, axis=1, keepdims=True)
    w = jnp.exp2((s - peak) * (SCALE * LOG2E))
    return dot(w.astype(BF16), kv[1]), peak * SCALE, jnp.sum(w, axis=1, keepdims=True)


def prefix_block(q, kv0, kv1):
    mixed0, peak0, total0 = prefix_part(q, kv0)
    mixed1, peak1, total1 = prefix_part(q, kv1)
    top = jnp.maximum(peak0, peak1)
    f0, f1 = jnp.exp(peak0 - top), jnp.exp(peak1 - top)
    total = total0 * f0 + total1 * f1
    return (mixed0 * f0 + mixed1 * f1) * (1.0 / total), top + jnp.log(total)


COUNT = ROWS // GROUP


def prefix_send_body(qa, qb, kv0, kv1, after, out):
    lane = lanes()
    tile = jnp.zeros((GROUP, DH), F32)
    for half, q in enumerate((qa, qb)):
        for i in range(256 // ROWS):
            rows = q[i * COUNT : (i + 1) * COUNT].reshape(ROWS, DH)
            mixed, mass = prefix_block(rows, kv0, kv1)
            at = half * 16 + i * COUNT
            out[at : at + COUNT] = mixed.reshape(COUNT, GROUP, DH).astype(BF16)
            for n in range(COUNT):
                tile = jnp.where(lane == at + n, mass[n * GROUP : (n + 1) * GROUP], tile)
    out[32] = split_tile(tile, 32)


def prefix_keep_body(q, kv0, kv1, out, masses):
    for i in range(256 // ROWS):
        rows = q[i * COUNT : (i + 1) * COUNT].reshape(ROWS, DH)
        mixed, mass = prefix_block(rows, kv0, kv1)
        at = i * COUNT
        out[at : at + COUNT] = mixed.reshape(COUNT, GROUP, DH)
        masses[at : at + COUNT] = jnp.broadcast_to(mass, (ROWS, DH)).reshape(COUNT, GROUP, DH)


def prefix_cost(rows):
    return pl.CostEstimate(
        flops=4 * rows * 4096 * 128, bytes_accessed=2_500_000, transcendentals=rows * 4096
    )


def prefix_send(qa, qb, kv0, kv1, after):
    return pl.pallas_call(
        prefix_send_body,
        out_shape=jax.ShapeDtypeStruct((33, GROUP, DH), BF16),
        in_specs=[VMEM] * 4 + [ANY],
        out_specs=VMEM,
        compiler_params=params(24),
        cost_estimate=prefix_cost(512),
        name="prefix_send",
    )(qa, qb, kv0, kv1, after)


def prefix_keep(q, kv0, kv1):
    out = jax.ShapeDtypeStruct((16, GROUP, DH), F32)
    return pl.pallas_call(
        prefix_keep_body,
        out_shape=[out, out],
        in_specs=[VMEM] * 3,
        out_specs=[VMEM, VMEM],
        compiler_params=params(24),
        cost_estimate=prefix_cost(256),
        name="prefix_keep",
    )(q, kv0, kv1)


def combine_body(
    place, own, own_masses, cross, cross_masses, message, s0, s1, s2, s3, far, out, held
):
    x, y_high, z = place[2], place[3], place[4]
    theirs = join_tile(message[32], 32)
    near = [join_tile(s[17], 8) for s in (s0, s1, s2, s3)]
    across = [join_tile(far[21 + 5 * i], 8) for i in range(4)]
    for g in range(2):
        for kx in range(4):
            for k in range(4):
                n = g * 16 + kx * 4 + k
                at = kx * 4 + k
                a, la = ((own, own_masses), (cross, cross_masses))[g]
                a, la = a[at], la[at]
                b = message[n].astype(F32)
                lb = jnp.broadcast_to(theirs[:, n : n + 1], (GROUP, DH))
                if g == 0:
                    s = (s0, s1, s2, s3)[kx][9 + k].astype(F32)
                    ls = jnp.broadcast_to(near[kx][:, k : k + 1], (GROUP, DH))
                else:
                    s = far[17 + 5 * kx + k].astype(F32)
                    ls = jnp.broadcast_to(across[kx][:, 4 + k : 5 + k], (GROUP, DH))
                top = jnp.maximum(jnp.maximum(la, lb), ls)
                ea, eb, es = jnp.exp(la - top), jnp.exp(lb - top), jnp.exp(ls - top)
                row = (ea * a + eb * b + es * s) / (ea + eb + es)
                target = (x ^ kx) * 2 + (y_high ^ g)
                held[((target - z - 2) & 7) * 4 + k] = row
    for h in range(GROUP):
        out[:, h * DH : (h + 1) * DH] = held[:, h, :].astype(BF16)


def combine(place, own, cross, message, near, far):
    return pl.pallas_call(
        combine_body,
        out_shape=jax.ShapeDtypeStruct((32, GROUP * DH), BF16),
        in_specs=[SMEM] + [VMEM] * 10,
        out_specs=VMEM,
        scratch_shapes=[pltpu.VMEM((32, GROUP, DH), F32)],
        compiler_params=params(),
        name="combine",
    )(place, *own, *cross, message, *near, far)


def by_target(total):
    low = lax.broadcasted_iota(jnp.int32, (8, total.shape[1]), 0) < 4
    chunks = []
    for g in range(2):
        even, odd = [], []
        for j in (0, 2):
            first = total[j * 16 + g * 8 : j * 16 + g * 8 + 8]
            second = total[(j + 1) * 16 + g * 8 : (j + 1) * 16 + g * 8 + 8]
            even.append(jnp.where(low, first, pltpu.roll(second, 4, 0)))
            odd.append(jnp.where(low, pltpu.roll(first, 4, 0), second))
        chunks += [jnp.concatenate(even, axis=0), jnp.concatenate(odd, axis=0)]
    return chunks


def project_body(a, b, c, w0, w1, out):
    rows = jnp.concatenate([a[...], b[...], c[...]], axis=0)
    for side, weight in enumerate((w0, w1)):
        total = dot(rows, weight[...])
        for i in range(3):
            for d, chunk in enumerate(by_target(total[64 * i : 64 * i + 64])):
                out[d, i * 16 : i * 16 + 16, side * 512 : side * 512 + 512] = chunk


def project(blocks, weights):
    return pl.pallas_call(
        project_body,
        out_shape=jax.ShapeDtypeStruct((4, 48, 1024), F32),
        in_specs=[VMEM] * 5,
        out_specs=VMEM,
        compiler_params=params(),
        cost_estimate=pl.CostEstimate(
            flops=2 * 192 * 2048 * 1024, bytes_accessed=4_500_000, transcendentals=0
        ),
        name="project",
    )(*blocks, *weights)


def last_chunks(a, b, w0, w1, first):
    rows = jnp.concatenate([a[...], b[...]], axis=0)
    for side, weight in enumerate((w0, w1)):
        columns = slice(side * 512, side * 512 + 512)
        for d, chunk in enumerate(by_target(dot(rows, weight[...]))):
            yield side, columns, d, jnp.concatenate([first[d, :, columns], chunk], axis=0)


def far_body(a, b, w0, w1, first, keep, up, down, direct):
    for _, columns, d, whole in last_chunks(a, b, w0, w1, first):
        if d == 0:
            keep[:, columns] = whole
        else:
            (up, direct, down)[d - 1][:, columns] = whole.astype(BF16)


def near_body(a, b, w0, w1, first, keep6, down, keep0, up):
    for _, columns, d, whole in last_chunks(a, b, w0, w1, first):
        if d in (0, 2):
            (keep6, keep0)[d // 2][:, columns] = whole
        else:
            (down, up)[d // 2][:, columns] = whole.astype(BF16)


SUM = jax.ShapeDtypeStruct((64, 1024), F32)
SENT = jax.ShapeDtypeStruct((64, 1024), BF16)
HALF = jax.ShapeDtypeStruct((64, 512), BF16)


def plain(body, out_shape, *args):
    return pl.pallas_call(
        body,
        out_shape=out_shape,
        in_specs=[VMEM] * len(args),
        out_specs=[VMEM] * len(out_shape),
        compiler_params=params(),
        name=body.__name__[:-5],
    )(*args)


def middle_body(keep2, keep6, below, above, up, down):
    up[...] = (keep2[...] + below[...].astype(F32)).astype(BF16)
    down[...] = (keep6[...] + above[...].astype(F32)).astype(BF16)


def total_body(keep, below1, above1, below2, above2, opposite, own, other):
    near = keep[...] + below1[...].astype(F32) + above1[...].astype(F32)
    whole = near + below2[...].astype(F32) + above2[...].astype(F32)
    whole = (whole + opposite[...].astype(F32)).astype(BF16)
    own[...] = whole[:, :512]
    other[...] = whole[:, 512:]


def order_body(place, orders, pick):
    x, y, core, z = place[2], place[3] * 2 + place[5], place[6], place[4]
    lane = lanes()
    order = jnp.zeros((GROUP, DH), F32)
    for block in range(4):
        dy = (2 * (z & 1) + block // 2) ^ y
        tile = orders[((block % 2) ^ core) * 4 + dy].astype(F32)
        order = jnp.where(lane >> 5 == block, pltpu.roll(tile, 32 * block, 1), order)
    order = order.astype(jnp.int32)
    prompt, k = order >> 2, order & 3
    block = lane >> 5
    far = block & 1
    dx = (prompt >> 1) ^ x
    dy = (2 * (prompt & 1) + (block >> 1)) ^ y
    first = jnp.where(far == 0, dx, dy)
    second = jnp.where(far == 0, dy, dx)
    second = jnp.where(second >= 2, 5 - second, second)
    source = ((far ^ core) * 16 + second * 4 + first) * 4 + k
    row = lax.broadcasted_iota(jnp.int32, (128, 128), 0)
    pick[...] = (row == source[0:1]).astype(F32).astype(BF16)


def order_rows(place, orders):
    return pl.pallas_call(
        order_body,
        out_shape=jax.ShapeDtypeStruct((128, 128), BF16),
        in_specs=[SMEM, VMEM],
        out_specs=VMEM,
        compiler_params=params(),
        name="order_rows",
    )(place, orders)


def finish_body(own, other, pick, out):
    dims = (((0,), (0,)), ((), ()))
    mixed = dot(pick[0:64], own[...], dims) + dot(pick[64:128], other[...], dims)
    out[...] = mixed.astype(BF16)


def finish(own, other, pick):
    return pl.pallas_call(
        finish_body,
        out_shape=jax.ShapeDtypeStruct((128, 512), BF16),
        in_specs=[VMEM] * 3,
        out_specs=VMEM,
        compiler_params=params(),
        name="finish",
    )(own, other, pick)


def along(value, shift, k):
    return lax.ppermute(value, "batch", [(i, i ^ (k << shift)) for i in range(BATCH)])


def along_x(value, k):
    return along(value, 3, k)


def along_y(value, k):
    return along(value, 1, k)


def other_core(value):
    return along(value, 0, 1)


def turned(value, k, phase):
    pairs = [(i, i ^ (k << (3 if (i & 1) == phase else 1))) for i in range(BATCH)]
    return lax.ppermute(value, "batch", pairs)


def gathered(parts):
    ring0 = jnp.concatenate(parts, axis=0)
    ring1, ring3 = turned(ring0, 1, 1), turned(ring0, 3, 1)
    return ring0, ring1, ring3, [turned(ring3[:32], 1, 1), turned(ring1[32:], 3, 1)]


def along_z(value, k):
    return lax.ppermute(value, "head", [(i, (i + k) % HEADS) for i in range(HEADS)])


def shards(queries, new_kv, prefix_kv, suffix_kv, page_table, suffix_len, prompt_of, out_weight):
    me = lax.axis_index("batch")
    z = lax.axis_index("head")
    x, y, core = me // 8, (me // 2) % 4, me % 2
    place = [8 * x + 4 * (y // 2), me * 256, x, y // 2, z, y % 2, core]
    place = jnp.stack(place).astype(jnp.int32)

    prefix_other = other_core(prefix_kv)
    weights = [out_weight, other_core(out_weight)]

    sent = local_parts(place, queries, prompt_of, page_table.T, suffix_len, new_kv, suffix_kv)
    by_x = [sent[0]] + [along_x(sent[k], k) for k in (1, 2, 3)]
    same, across = regroup(place, by_x)
    from1, from3 = along_y(same, 1), along_y(across, 3)

    own = prefix_keep(same, prefix_kv, prefix_other)
    passed, own = lax.optimization_barrier((from3, own))
    from2 = along_y(passed, 1)
    message = prefix_send(from1, from3, prefix_kv, prefix_other, own[1])
    message, from2 = lax.optimization_barrier((message, from2))
    message = along_y(message, 1)
    cross = prefix_keep(from2, prefix_kv, prefix_other)
    attended = combine(place, own, cross, message, by_x, from2)

    orders = jnp.stack([same[16], from1[16], from2[16], from3[16]])
    orders = jnp.concatenate([orders, other_core(orders)], axis=0)
    pick = order_rows(place, orders)

    parts = [attended] + [turned(attended, k, 0) for k in (1, 2, 3)]
    far, near = [gathered([a[i : i + 16] for a in parts]) for i in (0, 16)]
    first_far, first_near = project(far[:3], weights), project(near[:3], weights)
    keep2, up3, down3, up4 = plain(
        far_body, [SUM, SENT, SENT, SENT], *far[3], *weights, first_far
    )
    below3, above3 = along_z(up3, 1), along_z(down3, -1)
    opposite = along_z(up4, 4)
    keep6, down1, keep0, up1 = plain(
        near_body, [SUM, SENT, SUM, SENT], *near[3], *weights, first_near
    )
    below1, above1 = along_z(up1, 1), along_z(down1, -1)
    up2, down2 = plain(middle_body, [SENT, SENT], keep2, keep6, below3, above3)
    below2, above2 = along_z(up2, 2), along_z(down2, -2)
    own, other = plain(total_body, [HALF, HALF], keep0, below1, above1, below2, above2, opposite)
    return finish(own, other_core(other), pick)


def solution(mesh):
    placed = (
        P("batch", "head"),
        P(None, "batch", "head"),
        P(None, "batch", "head"),
        P(None, "batch", None, "head"),
        P("batch", None),
        P("batch"),
        P("batch"),
        P("head", "batch"),
    )
    return jax.shard_map(
        shards, mesh=mesh, in_specs=placed, out_specs=P("head", "batch"), check_vma=False
    )
```

```python
import jax
import jax.numpy as jnp
from jax import lax
from jax.experimental import pallas as pl
from jax.experimental.pallas import tpu as pltpu
from jax.sharding import PartitionSpec as P

DH = 128
GROUP = 16
SCALE = DH**-0.5
LOG2E = 1.4426950408889634
BATCH = 32
HEADS = 8
VMEM = pl.BlockSpec(memory_space=pltpu.VMEM)
SMEM = pl.BlockSpec(memory_space=pltpu.SMEM)
F32 = jnp.float32
BF16 = jnp.bfloat16
NT = (((1,), (1,)), ((), ()))
NN = (((1,), (0,)), ((), ()))


ANY = pl.BlockSpec(memory_space=pl.ANY)
HBM = pl.BlockSpec(memory_space=pltpu.HBM)


def params(mib=16):
    return pltpu.CompilerParams(vmem_limit_bytes=mib * 1024 * 1024)


def dot(a, b, dims=NN):
    return lax.dot_general(a, b, dims, preferred_element_type=F32)


def lanes():
    return lax.broadcasted_iota(jnp.int32, (GROUP, DH), 1)


def split_tile(tile, step):
    high = tile.astype(BF16).astype(F32)
    rest = tile - high
    middle = rest.astype(BF16).astype(F32)
    low = rest - middle
    joined = high + pltpu.roll(middle, step, 1) + pltpu.roll(low, 2 * step, 1)
    return joined.astype(BF16)


def join_tile(tile, step):
    wide = tile.astype(F32)
    return (wide + pltpu.roll(wide, DH - step, 1)) + pltpu.roll(wide, DH - 2 * step, 1)


def local_body(
    place, q_in, prompt_in, table_in, length_in, new_in, pool_in, o0, o1, o2, o3,
    q, prompt, table, length, new, pool, wide, scores, weights, slots, sems,
):
    pairs = [
        (q_in, q),
        (prompt_in, prompt),
        (table_in, table),
        (length_in, length),
        (new_in, new),
        (pool_in.at[0], pool.at[0]),
        (pool_in.at[1], pool.at[1]),
    ]
    copies = [pltpu.make_async_copy(a, b, sems.at[i]) for i, (a, b) in enumerate(pairs)]
    for copy in copies:
        copy.start()
    outs = (o0, o1, o2, o3)
    lane = lanes()
    copies[0].wait()
    for h in range(GROUP):
        wide[:, h, :] = q[:, h * DH : (h + 1) * DH].astype(F32)
    copies[1].wait()
    for p in range(8):
        slots[32 + p] = 0
    order = jnp.zeros((GROUP, DH), F32)
    for n in range(32):
        p = prompt[n]
        k = slots[32 + p]
        slots[32 + p] = k + 1
        slots[n] = (4 * p + k) ^ place[0]
        order = jnp.where(lane == n, (4 * p + k).astype(F32), order)
    for copy in copies[2:6]:
        copy.wait()
    base = place[1]
    for n in range(32):
        keys = jnp.concatenate([pool[0, table[j, n] - base] for j in range(8)], axis=0)
        s = dot(wide[n].astype(BF16), keys, NT) * SCALE
        scores[n] = jnp.where(lane < length[n], s, -1e30)
    own_keys = new[0].astype(F32)
    own_values = new[1].astype(F32)
    own = jnp.stack(
        [jnp.sum(wide[n] * own_keys[n : n + 1], axis=1, keepdims=True) for n in range(32)]
    ) * SCALE
    s = scores[...]
    peak = jnp.maximum(jnp.max(s, axis=2, keepdims=True), own)
    w = jnp.exp(s - peak)
    own_weight = jnp.exp(own - peak)
    total = jnp.sum(w, axis=2, keepdims=True) + own_weight
    weights[...] = w.astype(BF16)
    own_weight = own_weight.astype(BF16).astype(F32)
    mass = peak + jnp.log(total)
    inverse = 1.0 / total
    copies[6].wait()
    for n in range(32):
        values = jnp.concatenate([pool[1, table[j, n] - base] for j in range(8)], axis=0)
        mixed = dot(weights[n], values) + own_weight[n] * own_values[n : n + 1]
        scores[slots[n]] = mixed * inverse[n]
    held = [jnp.zeros((GROUP, DH), F32) for _ in range(4)]
    for n in range(32):
        slot = slots[n]
        weights[slot] = wide[n].astype(BF16)
        for i in range(4):
            held[i] = jnp.where(lane + 8 * i == slot, jnp.where(lane < 8, mass[n], 0.0), held[i])
    for i, out in enumerate(outs):
        out[0:8] = weights[8 * i : 8 * i + 8]
        out[8] = order.astype(BF16)
        out[9:17] = scores[8 * i : 8 * i + 8].astype(BF16)
        out[17] = split_tile(jnp.where(lane < 8, held[i], 0.0), 8)


def local_parts(place, q, prompt, table, length, new, pool):
    out = jax.ShapeDtypeStruct((18, GROUP, DH), BF16)
    return pl.pallas_call(
        local_body,
        out_shape=[out] * 4,
        in_specs=[SMEM] + [HBM] * 6,
        out_specs=[VMEM] * 4,
        scratch_shapes=[
            pltpu.VMEM((32, GROUP * DH), BF16),
            pltpu.SMEM((32,), jnp.int32),
            pltpu.SMEM((8, 32), jnp.int32),
            pltpu.SMEM((32,), jnp.int32),
            pltpu.VMEM((2, 32, DH), BF16),
            pltpu.VMEM((2, 256, GROUP, DH), BF16),
            pltpu.VMEM((32, GROUP, DH), F32),
            pltpu.VMEM((32, GROUP, DH), F32),
            pltpu.VMEM((32, GROUP, DH), BF16),
            pltpu.SMEM((40,), jnp.int32),
            pltpu.SemaphoreType.DMA((7,)),
        ],
        compiler_params=params(54),
        name="local_parts",
    )(place, q, prompt, table, length, new, pool)


def regroup_body(place, a0, a1, a2, a3, same, across):
    for i, a in enumerate((a0, a1, a2, a3)):
        same[4 * i : 4 * i + 4] = a[0:4]
        across[4 * i : 4 * i + 4] = a[4:8]
        across[17 + 5 * i : 22 + 5 * i] = a[13:18]

        @pl.when(place[2] ^ (place[4] >> 1) == i)
        def _(a=a):
            same[16] = a[8]
            across[16] = a[8]


def regroup(place, parts):
    return pl.pallas_call(
        regroup_body,
        out_shape=[
            jax.ShapeDtypeStruct((17, GROUP, DH), BF16),
            jax.ShapeDtypeStruct((37, GROUP, DH), BF16),
        ],
        in_specs=[SMEM] + [VMEM] * 4,
        out_specs=[VMEM] * 2,
        compiler_params=params(),
        name="regroup",
    )(place, *parts)


ROWS = 256


def prefix_part(q, kv):
    s = dot(q, kv[0], NT)
    peak = jnp.max(s, axis=1, keepdims=True)
    w = jnp.exp2((s - peak) * (SCALE * LOG2E))
    return dot(w.astype(BF16), kv[1]), peak * SCALE, jnp.sum(w, axis=1, keepdims=True)


def prefix_block(q, kv0, kv1):
    mixed0, peak0, total0 = prefix_part(q, kv0)
    mixed1, peak1, total1 = prefix_part(q, kv1)
    top = jnp.maximum(peak0, peak1)
    f0, f1 = jnp.exp(peak0 - top), jnp.exp(peak1 - top)
    total = total0 * f0 + total1 * f1
    return (mixed0 * f0 + mixed1 * f1) * (1.0 / total), top + jnp.log(total)


COUNT = ROWS // GROUP


def prefix_send_body(qa, qb, kv0, kv1, after, out):
    lane = lanes()
    tile = jnp.zeros((GROUP, DH), F32)
    for half, q in enumerate((qa, qb)):
        for i in range(256 // ROWS):
            rows = q[i * COUNT : (i + 1) * COUNT].reshape(ROWS, DH)
            mixed, mass = prefix_block(rows, kv0, kv1)
            at = half * 16 + i * COUNT
            out[at : at + COUNT] = mixed.reshape(COUNT, GROUP, DH).astype(BF16)
            for n in range(COUNT):
                tile = jnp.where(lane == at + n, mass[n * GROUP : (n + 1) * GROUP], tile)
    out[32] = split_tile(tile, 32)


def prefix_keep_body(q, kv0, kv1, out, masses):
    for i in range(256 // ROWS):
        rows = q[i * COUNT : (i + 1) * COUNT].reshape(ROWS, DH)
        mixed, mass = prefix_block(rows, kv0, kv1)
        at = i * COUNT
        out[at : at + COUNT] = mixed.reshape(COUNT, GROUP, DH)
        masses[at : at + COUNT] = jnp.broadcast_to(mass, (ROWS, DH)).reshape(COUNT, GROUP, DH)


def prefix_cost(rows):
    return pl.CostEstimate(
        flops=4 * rows * 4096 * 128, bytes_accessed=2_500_000, transcendentals=rows * 4096
    )


def prefix_send(qa, qb, kv0, kv1, after):
    return pl.pallas_call(
        prefix_send_body,
        out_shape=jax.ShapeDtypeStruct((33, GROUP, DH), BF16),
        in_specs=[VMEM] * 4 + [ANY],
        out_specs=VMEM,
        compiler_params=params(24),
        cost_estimate=prefix_cost(512),
        name="prefix_send",
    )(qa, qb, kv0, kv1, after)


def prefix_keep(q, kv0, kv1):
    out = jax.ShapeDtypeStruct((16, GROUP, DH), F32)
    return pl.pallas_call(
        prefix_keep_body,
        out_shape=[out, out],
        in_specs=[VMEM] * 3,
        out_specs=[VMEM, VMEM],
        compiler_params=params(24),
        cost_estimate=prefix_cost(256),
        name="prefix_keep",
    )(q, kv0, kv1)


def combine_body(
    place, own, own_masses, cross, cross_masses, message, s0, s1, s2, s3, far, out, held
):
    x, y_high, z = place[2], place[3], place[4]
    theirs = join_tile(message[32], 32)
    near = [join_tile(s[17], 8) for s in (s0, s1, s2, s3)]
    across = [join_tile(far[21 + 5 * i], 8) for i in range(4)]
    for g in range(2):
        for kx in range(4):
            for k in range(4):
                n = g * 16 + kx * 4 + k
                at = kx * 4 + k
                a, la = ((own, own_masses), (cross, cross_masses))[g]
                a, la = a[at], la[at]
                b = message[n].astype(F32)
                lb = jnp.broadcast_to(theirs[:, n : n + 1], (GROUP, DH))
                if g == 0:
                    s = (s0, s1, s2, s3)[kx][9 + k].astype(F32)
                    ls = jnp.broadcast_to(near[kx][:, k : k + 1], (GROUP, DH))
                else:
                    s = far[17 + 5 * kx + k].astype(F32)
                    ls = jnp.broadcast_to(across[kx][:, 4 + k : 5 + k], (GROUP, DH))
                top = jnp.maximum(jnp.maximum(la, lb), ls)
                ea, eb, es = jnp.exp(la - top), jnp.exp(lb - top), jnp.exp(ls - top)
                row = (ea * a + eb * b + es * s) / (ea + eb + es)
                target = (x ^ kx) * 2 + (y_high ^ g)
                held[((target - z - 2) & 7) * 4 + k] = row
    for h in range(GROUP):
        out[:, h * DH : (h + 1) * DH] = held[:, h, :].astype(BF16)


def combine(place, own, cross, message, near, far):
    return pl.pallas_call(
        combine_body,
        out_shape=jax.ShapeDtypeStruct((32, GROUP * DH), BF16),
        in_specs=[SMEM] + [VMEM] * 10,
        out_specs=VMEM,
        scratch_shapes=[pltpu.VMEM((32, GROUP, DH), F32)],
        compiler_params=params(),
        name="combine",
    )(place, *own, *cross, message, *near, far)


def by_target(total):
    low = lax.broadcasted_iota(jnp.int32, (8, total.shape[1]), 0) < 4
    chunks = []
    for g in range(2):
        even, odd = [], []
        for j in (0, 2):
            first = total[j * 16 + g * 8 : j * 16 + g * 8 + 8]
            second = total[(j + 1) * 16 + g * 8 : (j + 1) * 16 + g * 8 + 8]
            even.append(jnp.where(low, first, pltpu.roll(second, 4, 0)))
            odd.append(jnp.where(low, pltpu.roll(first, 4, 0), second))
        chunks += [jnp.concatenate(even, axis=0), jnp.concatenate(odd, axis=0)]
    return chunks


def project_body(a, b, c, w0, w1, out):
    rows = jnp.concatenate([a[...], b[...], c[...]], axis=0)
    for side, weight in enumerate((w0, w1)):
        total = dot(rows, weight[...])
        for i in range(3):
            for d, chunk in enumerate(by_target(total[64 * i : 64 * i + 64])):
                out[d, i * 16 : i * 16 + 16, side * 512 : side * 512 + 512] = chunk


def project(blocks, weights):
    return pl.pallas_call(
        project_body,
        out_shape=jax.ShapeDtypeStruct((4, 48, 1024), F32),
        in_specs=[VMEM] * 5,
        out_specs=VMEM,
        compiler_params=params(),
        cost_estimate=pl.CostEstimate(
            flops=2 * 192 * 2048 * 1024, bytes_accessed=4_500_000, transcendentals=0
        ),
        name="project",
    )(*blocks, *weights)


def last_chunks(a, b, w0, w1, first):
    rows = jnp.concatenate([a[...], b[...]], axis=0)
    for side, weight in enumerate((w0, w1)):
        columns = slice(side * 512, side * 512 + 512)
        for d, chunk in enumerate(by_target(dot(rows, weight[...]))):
            yield side, columns, d, jnp.concatenate([first[d, :, columns], chunk], axis=0)


def far_body(a, b, w0, w1, first, keep, up, down, direct):
    for _, columns, d, whole in last_chunks(a, b, w0, w1, first):
        if d == 0:
            keep[:, columns] = whole
        else:
            (up, direct, down)[d - 1][:, columns] = whole.astype(BF16)


def near_body(a, b, w0, w1, first, keep6, down, keep0, up):
    for _, columns, d, whole in last_chunks(a, b, w0, w1, first):
        if d in (0, 2):
            (keep6, keep0)[d // 2][:, columns] = whole
        else:
            (down, up)[d // 2][:, columns] = whole.astype(BF16)


SUM = jax.ShapeDtypeStruct((64, 1024), F32)
SENT = jax.ShapeDtypeStruct((64, 1024), BF16)
HALF = jax.ShapeDtypeStruct((64, 512), BF16)


def plain(body, out_shape, *args):
    return pl.pallas_call(
        body,
        out_shape=out_shape,
        in_specs=[VMEM] * len(args),
        out_specs=[VMEM] * len(out_shape),
        compiler_params=params(),
        name=body.__name__[:-5],
    )(*args)


def middle_body(keep2, keep6, below, above, up, down):
    up[...] = (keep2[...] + below[...].astype(F32)).astype(BF16)
    down[...] = (keep6[...] + above[...].astype(F32)).astype(BF16)


def total_body(keep, below1, above1, below2, above2, opposite, own, other):
    near = keep[...] + below1[...].astype(F32) + above1[...].astype(F32)
    whole = near + below2[...].astype(F32) + above2[...].astype(F32)
    whole = (whole + opposite[...].astype(F32)).astype(BF16)
    own[...] = whole[:, :512]
    other[...] = whole[:, 512:]


def order_body(place, orders, pick):
    x, y, core, z = place[2], place[3] * 2 + place[5], place[6], place[4]
    lane = lanes()
    order = jnp.zeros((GROUP, DH), F32)
    for block in range(4):
        dy = (2 * (z & 1) + block // 2) ^ y
        tile = orders[((block % 2) ^ core) * 4 + dy].astype(F32)
        order = jnp.where(lane >> 5 == block, pltpu.roll(tile, 32 * block, 1), order)
    order = order.astype(jnp.int32)
    prompt, k = order >> 2, order & 3
    block = lane >> 5
    far = block & 1
    dx = (prompt >> 1) ^ x
    dy = (2 * (prompt & 1) + (block >> 1)) ^ y
    first = jnp.where(far == 0, dx, dy)
    second = jnp.where(far == 0, dy, dx)
    second = jnp.where(second >= 2, 5 - second, second)
    source = ((far ^ core) * 16 + second * 4 + first) * 4 + k
    row = lax.broadcasted_iota(jnp.int32, (128, 128), 0)
    pick[...] = (row == source[0:1]).astype(F32).astype(BF16)


def order_rows(place, orders):
    return pl.pallas_call(
        order_body,
        out_shape=jax.ShapeDtypeStruct((128, 128), BF16),
        in_specs=[SMEM, VMEM],
        out_specs=VMEM,
        compiler_params=params(),
        name="order_rows",
    )(place, orders)


def finish_body(own, other, pick, out):
    dims = (((0,), (0,)), ((), ()))
    mixed = dot(pick[0:64], own[...], dims) + dot(pick[64:128], other[...], dims)
    out[...] = mixed.astype(BF16)


def finish(own, other, pick):
    return pl.pallas_call(
        finish_body,
        out_shape=jax.ShapeDtypeStruct((128, 512), BF16),
        in_specs=[VMEM] * 3,
        out_specs=VMEM,
        compiler_params=params(),
        name="finish",
    )(own, other, pick)


def along(value, shift, k):
    return lax.ppermute(value, "batch", [(i, i ^ (k << shift)) for i in range(BATCH)])


def along_x(value, k):
    return along(value, 3, k)


def along_y(value, k):
    return along(value, 1, k)


def other_core(value):
    return along(value, 0, 1)


def turned(value, k, phase):
    pairs = [(i, i ^ (k << (3 if (i & 1) == phase else 1))) for i in range(BATCH)]
    return lax.ppermute(value, "batch", pairs)


def gathered(parts):
    ring0 = jnp.concatenate(parts, axis=0)
    ring1, ring3 = turned(ring0, 1, 1), turned(ring0, 3, 1)
    return ring0, ring1, ring3, [turned(ring3[:32], 1, 1), turned(ring1[32:], 3, 1)]


def along_z(value, k):
    return lax.ppermute(value, "head", [(i, (i + k) % HEADS) for i in range(HEADS)])


def shards(queries, new_kv, prefix_kv, suffix_kv, page_table, suffix_len, prompt_of, out_weight):
    me = lax.axis_index("batch")
    z = lax.axis_index("head")
    x, y, core = me // 8, (me // 2) % 4, me % 2
    place = [8 * x + 4 * (y // 2), me * 256, x, y // 2, z, y % 2, core]
    place = jnp.stack(place).astype(jnp.int32)

    prefix_other = other_core(prefix_kv)
    weights = [out_weight, other_core(out_weight)]

    sent = local_parts(place, queries, prompt_of, page_table.T, suffix_len, new_kv, suffix_kv)
    by_x = [sent[0]] + [along_x(sent[k], k) for k in (1, 2, 3)]
    same, across = regroup(place, by_x)
    from1, from3 = along_y(same, 1), along_y(across, 3)

    own = prefix_keep(same, prefix_kv, prefix_other)
    passed, own = lax.optimization_barrier((from3, own))
    from2 = along_y(passed, 1)
    message = prefix_send(from1, from3, prefix_kv, prefix_other, own[1])
    message, from2 = lax.optimization_barrier((message, from2))
    message = along_y(message, 1)
    cross = prefix_keep(from2, prefix_kv, prefix_other)
    attended = combine(place, own, cross, message, by_x, from2)

    orders = jnp.stack([same[16], from1[16], from2[16], from3[16]])
    orders = jnp.concatenate([orders, other_core(orders)], axis=0)
    pick = order_rows(place, orders)

    parts = [attended] + [turned(attended, k, 0) for k in (1, 2, 3)]
    far = gathered([a[:16] for a in parts])
    first_far = project(far[:3], weights)
    late, last_far = lax.optimization_barrier(([a[16:] for a in parts], far[3]))
    near = gathered(late)
    first_near = project(near[:3], weights)
    keep2, up3, down3, up4 = plain(
        far_body, [SUM, SENT, SENT, SENT], *last_far, *weights, first_far
    )
    below3, above3 = along_z(up3, 1), along_z(down3, -1)
    opposite = along_z(up4, 4)
    keep6, down1, keep0, up1 = plain(
        near_body, [SUM, SENT, SUM, SENT], *near[3], *weights, first_near
    )
    below1, above1 = along_z(up1, 1), along_z(down1, -1)
    up2, down2 = plain(middle_body, [SENT, SENT], keep2, keep6, below3, above3)
    below2, above2 = along_z(up2, 2), along_z(down2, -2)
    own, other = plain(total_body, [HALF, HALF], keep0, below1, above1, below2, above2, opposite)
    return finish(own, other_core(other), pick)


def solution(mesh):
    placed = (
        P("batch", "head"),
        P(None, "batch", "head"),
        P(None, "batch", "head"),
        P(None, "batch", None, "head"),
        P("batch", None),
        P("batch"),
        P("batch"),
        P("head", "batch"),
    )
    return jax.shard_map(
        shards, mesh=mesh, in_specs=placed, out_specs=P("head", "batch"), check_vma=False
    )
```

```python
import jax
import jax.numpy as jnp
from jax import lax
from jax.experimental import pallas as pl
from jax.experimental.pallas import tpu as pltpu
from jax.sharding import PartitionSpec as P

DH = 128
GROUP = 16
SCALE = DH**-0.5
LOG2E = 1.4426950408889634
BATCH = 32
HEADS = 8
VMEM = pl.BlockSpec(memory_space=pltpu.VMEM)
SMEM = pl.BlockSpec(memory_space=pltpu.SMEM)
F32 = jnp.float32
BF16 = jnp.bfloat16
NT = (((1,), (1,)), ((), ()))
NN = (((1,), (0,)), ((), ()))


ANY = pl.BlockSpec(memory_space=pl.ANY)
HBM = pl.BlockSpec(memory_space=pltpu.HBM)


def params(mib=16):
    return pltpu.CompilerParams(vmem_limit_bytes=mib * 1024 * 1024)


def dot(a, b, dims=NN):
    return lax.dot_general(a, b, dims, preferred_element_type=F32)


def position():
    index = lax.axis_index("batch")
    return index >> 3, (index >> 1) & 3, index & 1, lax.axis_index("head")


def lanes():
    return lax.broadcasted_iota(jnp.int32, (GROUP, DH), 1)


def split_tile(tile, step):
    high = tile.astype(BF16).astype(F32)
    rest = tile - high
    middle = rest.astype(BF16).astype(F32)
    low = rest - middle
    joined = high + pltpu.roll(middle, step, 1) + pltpu.roll(low, 2 * step, 1)
    return joined.astype(BF16)


def join_tile(tile, step):
    wide = tile.astype(F32)
    return (wide + pltpu.roll(wide, DH - step, 1)) + pltpu.roll(wide, DH - 2 * step, 1)


def local_body(
    q_in, prompt_in, table_in, length_in, new_in, pool_in, o0, o1, o2, o3,
    q, prompt, table, length, new, pool, wide, scores, weights, slots, sems,
):
    pairs = [
        (q_in, q),
        (prompt_in, prompt),
        (table_in, table),
        (length_in, length),
        (new_in, new),
        (pool_in.at[0], pool.at[0]),
        (pool_in.at[1], pool.at[1]),
    ]
    copies = [pltpu.make_async_copy(a, b, sems.at[i]) for i, (a, b) in enumerate(pairs)]
    for copy in copies:
        copy.start()
    outs = (o0, o1, o2, o3)
    lane = lanes()
    x, y, _, _ = position()
    mask = 8 * x + 4 * (y >> 1)
    copies[0].wait()
    for h in range(GROUP):
        wide[:, h, :] = q[:, h * DH : (h + 1) * DH].astype(F32)
    copies[1].wait()
    for p in range(8):
        slots[32 + p] = 0
    order = jnp.zeros((GROUP, DH), F32)
    for n in range(32):
        p = prompt[n]
        k = slots[32 + p]
        slots[32 + p] = k + 1
        slots[n] = (4 * p + k) ^ mask
        order = jnp.where(lane == n, (4 * p + k).astype(F32), order)
    for copy in copies[2:6]:
        copy.wait()
    base = lax.axis_index("batch") * 256
    for n in range(32):
        keys = jnp.concatenate([pool[0, table[j, n] - base] for j in range(8)], axis=0)
        s = dot(wide[n].astype(BF16), keys, NT) * SCALE
        scores[n] = jnp.where(lane < length[n], s, -1e30)
    own_keys = new[0].astype(F32)
    own_values = new[1].astype(F32)
    own = jnp.stack(
        [jnp.sum(wide[n] * own_keys[n : n + 1], axis=1, keepdims=True) for n in range(32)]
    ) * SCALE
    s = scores[...]
    peak = jnp.maximum(jnp.max(s, axis=2, keepdims=True), own)
    w = jnp.exp(s - peak)
    own_weight = jnp.exp(own - peak)
    total = jnp.sum(w, axis=2, keepdims=True) + own_weight
    weights[...] = w.astype(BF16)
    own_weight = own_weight.astype(BF16).astype(F32)
    mass = peak + jnp.log(total)
    inverse = 1.0 / total
    copies[6].wait()
    for n in range(32):
        values = jnp.concatenate([pool[1, table[j, n] - base] for j in range(8)], axis=0)
        mixed = dot(weights[n], values) + own_weight[n] * own_values[n : n + 1]
        scores[slots[n]] = mixed * inverse[n]
    held = [jnp.zeros((GROUP, DH), F32) for _ in range(4)]
    for n in range(32):
        slot = slots[n]
        weights[slot] = wide[n].astype(BF16)
        for i in range(4):
            held[i] = jnp.where(lane + 8 * i == slot, jnp.where(lane < 8, mass[n], 0.0), held[i])
    for i, out in enumerate(outs):
        out[0:8] = weights[8 * i : 8 * i + 8]
        out[8] = order.astype(BF16)
        out[9:17] = scores[8 * i : 8 * i + 8].astype(BF16)
        out[17] = split_tile(jnp.where(lane < 8, held[i], 0.0), 8)


def local_parts(q, prompt, table, length, new, pool):
    out = jax.ShapeDtypeStruct((18, GROUP, DH), BF16)
    return pl.pallas_call(
        local_body,
        out_shape=[out] * 4,
        in_specs=[HBM] * 6,
        out_specs=[VMEM] * 4,
        scratch_shapes=[
            pltpu.VMEM((32, GROUP * DH), BF16),
            pltpu.SMEM((32,), jnp.int32),
            pltpu.SMEM((8, 32), jnp.int32),
            pltpu.SMEM((32,), jnp.int32),
            pltpu.VMEM((2, 32, DH), BF16),
            pltpu.VMEM((2, 256, GROUP, DH), BF16),
            pltpu.VMEM((32, GROUP, DH), F32),
            pltpu.VMEM((32, GROUP, DH), F32),
            pltpu.VMEM((32, GROUP, DH), BF16),
            pltpu.SMEM((40,), jnp.int32),
            pltpu.SemaphoreType.DMA((7,)),
        ],
        compiler_params=params(54),
        name="local_parts",
    )(q, prompt, table, length, new, pool)


def regroup_body(a0, a1, a2, a3, same, across):
    x, _, _, z = position()
    for i, a in enumerate((a0, a1, a2, a3)):
        same[4 * i : 4 * i + 4] = a[0:4]
        across[4 * i : 4 * i + 4] = a[4:8]
        across[17 + 5 * i : 22 + 5 * i] = a[13:18]

        @pl.when(x ^ (z >> 1) == i)
        def _(a=a):
            same[16] = a[8]
            across[16] = a[8]


def regroup(parts):
    return pl.pallas_call(
        regroup_body,
        out_shape=[
            jax.ShapeDtypeStruct((17, GROUP, DH), BF16),
            jax.ShapeDtypeStruct((37, GROUP, DH), BF16),
        ],
        in_specs=[VMEM] * 4,
        out_specs=[VMEM] * 2,
        compiler_params=params(),
        name="regroup",
    )(*parts)


ROWS = 256


def prefix_part(q, kv):
    s = dot(q, kv[0], NT)
    peak = jnp.max(s, axis=1, keepdims=True)
    w = jnp.exp2((s - peak) * (SCALE * LOG2E))
    return dot(w.astype(BF16), kv[1]), peak * SCALE, jnp.sum(w, axis=1, keepdims=True)


def prefix_block(q, kv0, kv1):
    mixed0, peak0, total0 = prefix_part(q, kv0)
    mixed1, peak1, total1 = prefix_part(q, kv1)
    top = jnp.maximum(peak0, peak1)
    f0, f1 = jnp.exp(peak0 - top), jnp.exp(peak1 - top)
    total = total0 * f0 + total1 * f1
    return (mixed0 * f0 + mixed1 * f1) * (1.0 / total), top + jnp.log(total)


COUNT = ROWS // GROUP


def prefix_send_body(qa, qb, kv0, kv1, after, out):
    lane = lanes()
    tile = jnp.zeros((GROUP, DH), F32)
    for half, q in enumerate((qa, qb)):
        for i in range(256 // ROWS):
            rows = q[i * COUNT : (i + 1) * COUNT].reshape(ROWS, DH)
            mixed, mass = prefix_block(rows, kv0, kv1)
            at = half * 16 + i * COUNT
            out[at : at + COUNT] = mixed.reshape(COUNT, GROUP, DH).astype(BF16)
            for n in range(COUNT):
                tile = jnp.where(lane == at + n, mass[n * GROUP : (n + 1) * GROUP], tile)
    out[32] = split_tile(tile, 32)


def prefix_keep_body(q, kv0, kv1, out, masses):
    for i in range(256 // ROWS):
        rows = q[i * COUNT : (i + 1) * COUNT].reshape(ROWS, DH)
        mixed, mass = prefix_block(rows, kv0, kv1)
        at = i * COUNT
        out[at : at + COUNT] = mixed.reshape(COUNT, GROUP, DH)
        masses[at : at + COUNT] = jnp.broadcast_to(mass, (ROWS, DH)).reshape(COUNT, GROUP, DH)


def prefix_cost(rows):
    return pl.CostEstimate(
        flops=4 * rows * 4096 * 128, bytes_accessed=2_500_000, transcendentals=rows * 4096
    )


def prefix_send(qa, qb, kv0, kv1, after):
    return pl.pallas_call(
        prefix_send_body,
        out_shape=jax.ShapeDtypeStruct((33, GROUP, DH), BF16),
        in_specs=[VMEM] * 4 + [ANY],
        out_specs=VMEM,
        compiler_params=params(24),
        cost_estimate=prefix_cost(512),
        name="prefix_send",
    )(qa, qb, kv0, kv1, after)


def prefix_keep(q, kv0, kv1):
    out = jax.ShapeDtypeStruct((16, GROUP, DH), F32)
    return pl.pallas_call(
        prefix_keep_body,
        out_shape=[out, out],
        in_specs=[VMEM] * 3,
        out_specs=[VMEM, VMEM],
        compiler_params=params(24),
        cost_estimate=prefix_cost(256),
        name="prefix_keep",
    )(q, kv0, kv1)


PLACES = 0x47210635


def combine_body(
    own, own_masses, cross, cross_masses, message, s0, s1, s2, s3, far, after, out, held
):
    x, y, _, z = position()
    y_high = y >> 1
    theirs = join_tile(message[32], 32)
    near = [join_tile(s[17], 8) for s in (s0, s1, s2, s3)]
    across = [join_tile(far[21 + 5 * i], 8) for i in range(4)]
    for g in range(2):
        for kx in range(4):
            for k in range(4):
                n = g * 16 + kx * 4 + k
                at = kx * 4 + k
                a, la = ((own, own_masses), (cross, cross_masses))[g]
                a, la = a[at], la[at]
                b = message[n].astype(F32)
                lb = jnp.broadcast_to(theirs[:, n : n + 1], (GROUP, DH))
                if g == 0:
                    s = (s0, s1, s2, s3)[kx][9 + k].astype(F32)
                    ls = jnp.broadcast_to(near[kx][:, k : k + 1], (GROUP, DH))
                else:
                    s = far[17 + 5 * kx + k].astype(F32)
                    ls = jnp.broadcast_to(across[kx][:, 4 + k : 5 + k], (GROUP, DH))
                top = jnp.maximum(jnp.maximum(la, lb), ls)
                ea, eb, es = jnp.exp(la - top), jnp.exp(lb - top), jnp.exp(ls - top)
                row = (ea * a + eb * b + es * s) / (ea + eb + es)
                target = (x ^ kx) * 2 + (y_high ^ g)
                held[((PLACES >> (4 * ((target - z) & 7))) & 7) * 4 + k] = row
    for h in range(GROUP):
        out[:, h * DH : (h + 1) * DH] = held[:, h, :].astype(BF16)


def combine(own, cross, message, near, far, after):
    return pl.pallas_call(
        combine_body,
        out_shape=jax.ShapeDtypeStruct((32, GROUP * DH), BF16),
        in_specs=[VMEM] * 10 + [ANY],
        out_specs=VMEM,
        scratch_shapes=[pltpu.VMEM((32, GROUP, DH), F32)],
        compiler_params=params(),
        name="combine",
    )(*own, *cross, message, *near, far, after)


def by_target(total, count):
    low = lax.broadcasted_iota(jnp.int32, (8, total.shape[1]), 0) < 4
    chunks = []
    for g in range(count // 2):
        even, odd = [], []
        for j in (0, 2):
            at = j * 4 * count + g * 8
            first, second = total[at : at + 8], total[at + 4 * count : at + 4 * count + 8]
            even.append(jnp.where(low, first, pltpu.roll(second, 4, 0)))
            odd.append(jnp.where(low, pltpu.roll(first, 4, 0), second))
        chunks += [jnp.concatenate(even, axis=0), jnp.concatenate(odd, axis=0)]
    return chunks


def project_body(a, b, c, w0, w1, out):
    count, size = out.shape[0], a.shape[0]
    rows = jnp.concatenate([a[...], b[...], c[...]], axis=0)
    for side, weight in enumerate((w0, w1)):
        total = dot(rows, weight[...])
        for i in range(3):
            for d, chunk in enumerate(by_target(total[size * i : size * i + size], count)):
                out[d, i * 16 : i * 16 + 16, side * 512 : side * 512 + 512] = chunk


def project(blocks, weights):
    size = blocks[0].shape[0]
    return pl.pallas_call(
        project_body,
        out_shape=jax.ShapeDtypeStruct((size // 16, 48, 1024), F32),
        in_specs=[VMEM] * 5,
        out_specs=VMEM,
        compiler_params=params(),
        cost_estimate=pl.CostEstimate(
            flops=2 * 3 * size * 2048 * 1024, bytes_accessed=4_500_000, transcendentals=0
        ),
        name="project",
    )(*blocks, *weights)


def last_chunks(a, b, w0, w1, first):
    rows = jnp.concatenate([a[...], b[...]], axis=0)
    for side, weight in enumerate((w0, w1)):
        columns = slice(side * 512, side * 512 + 512)
        for d, chunk in enumerate(by_target(dot(rows, weight[...]), first.shape[0])):
            yield columns, d, jnp.concatenate([first[d, :, columns], chunk], axis=0)


def far_body(a, b, w0, w1, first, keep, up, down, direct):
    for columns, d, whole in last_chunks(a, b, w0, w1, first):
        if d == 5:
            keep[:, columns] = whole
        elif d == 1:
            direct[:, columns] = whole.astype(BF16)
        else:
            out = up if d in (0, 3) else down
            out[d // 3, :, columns] = whole.astype(BF16)


def near_body(a, b, w0, w1, first, keep2, keep6):
    for columns, d, whole in last_chunks(a, b, w0, w1, first):
        (keep2, keep6)[d][:, columns] = whole


SUM = jax.ShapeDtypeStruct((64, 1024), F32)
SENT = jax.ShapeDtypeStruct((64, 1024), BF16)
HALF = jax.ShapeDtypeStruct((64, 512), BF16)
TWO = jax.ShapeDtypeStruct((2, 64, 1024), BF16)


def plain(body, out_shape, *args):
    return pl.pallas_call(
        body,
        out_shape=out_shape,
        in_specs=[VMEM] * len(args),
        out_specs=[VMEM] * len(out_shape),
        compiler_params=params(),
        name=body.__name__[:-5],
    )(*args)


def middle_body(keep2, keep6, below, above, up, down):
    up[...] = (keep2[...] + below[0].astype(F32)).astype(BF16)
    down[...] = (keep6[...] + above[0].astype(F32)).astype(BF16)


def total_body(keep, below, above, below2, above2, opposite, own, other):
    near = keep[...] + below[1].astype(F32) + above[1].astype(F32)
    whole = near + below2[...].astype(F32) + above2[...].astype(F32)
    whole = (whole + opposite[...].astype(F32)).astype(BF16)
    own[...] = whole[:, :512]
    other[...] = whole[:, 512:]


def order_body(orders, pick):
    x, y, core, z = position()
    lane = lanes()
    order = jnp.zeros((GROUP, DH), F32)
    for block in range(4):
        dy = (2 * (z & 1) + block // 2) ^ y
        tile = orders[((block % 2) ^ core) * 4 + dy].astype(F32)
        order = jnp.where(lane >> 5 == block, pltpu.roll(tile, 32 * block, 1), order)
    order = order.astype(jnp.int32)
    prompt, k = order >> 2, order & 3
    block = lane >> 5
    far = block & 1
    dx = (prompt >> 1) ^ x
    dy = (2 * (prompt & 1) + (block >> 1)) ^ y
    first = jnp.where(far == 0, dx, dy)
    second = jnp.where(far == 0, dy, dx)
    second = jnp.where(second >= 2, 5 - second, second)
    source = ((far ^ core) * 16 + second * 4 + first) * 4 + k
    row = lax.broadcasted_iota(jnp.int32, (128, 128), 0)
    pick[...] = (row == source[0:1]).astype(F32).astype(BF16)


def order_rows(orders):
    return pl.pallas_call(
        order_body,
        out_shape=jax.ShapeDtypeStruct((128, 128), BF16),
        in_specs=[VMEM],
        out_specs=VMEM,
        compiler_params=params(),
        name="order_rows",
    )(orders)


def finish_body(own, other, pick, out):
    dims = (((0,), (0,)), ((), ()))
    mixed = dot(pick[0:64], own[...], dims) + dot(pick[64:128], other[...], dims)
    out[...] = mixed.astype(BF16)


def finish(own, other, pick):
    return pl.pallas_call(
        finish_body,
        out_shape=jax.ShapeDtypeStruct((128, 512), BF16),
        in_specs=[VMEM] * 3,
        out_specs=VMEM,
        compiler_params=params(),
        name="finish",
    )(own, other, pick)


def along(value, shift, k):
    return lax.ppermute(value, "batch", [(i, i ^ (k << shift)) for i in range(BATCH)])


def along_x(value, k):
    return along(value, 3, k)


def along_y(value, k):
    return along(value, 1, k)


def other_core(value):
    return along(value, 0, 1)


def turned(value, k, phase):
    pairs = [(i, i ^ (k << (3 if (i & 1) == phase else 1))) for i in range(BATCH)]
    return lax.ppermute(value, "batch", pairs)


def gathered(parts):
    ring0 = jnp.concatenate(parts, axis=0)
    ring1, ring3 = turned(ring0, 1, 1), turned(ring0, 3, 1)
    half = ring0.shape[0] // 2
    return ring0, ring1, ring3, [turned(ring3[:half], 1, 1), turned(ring1[half:], 3, 1)]


def along_z(value, k):
    return lax.ppermute(value, "head", [(i, (i + k) % HEADS) for i in range(HEADS)])


def shards(queries, new_kv, prefix_kv, suffix_kv, page_table, suffix_len, prompt_of, out_weight):
    prefix_other = other_core(prefix_kv)
    weights = [out_weight, other_core(out_weight)]

    sent = local_parts(queries, prompt_of, page_table.T, suffix_len, new_kv, suffix_kv)
    by_x = [sent[0]] + [along_x(sent[k], k) for k in (1, 2, 3)]
    same, across = regroup(by_x)
    from1, from3 = along_y(same, 1), along_y(across, 3)

    own = prefix_keep(same, prefix_kv, prefix_other)
    passed, own = lax.optimization_barrier((from3, own))
    from2 = along_y(passed, 1)
    message = prefix_send(from1, from3, prefix_kv, prefix_other, own[1])
    message, from2 = lax.optimization_barrier((message, from2))
    message = along_y(message, 1)
    cross = prefix_keep(from2, prefix_kv, prefix_other)
    orders = jnp.stack([same[16], from1[16], from2[16], from3[16]])
    orders = jnp.concatenate([orders, other_core(orders)], axis=0)
    pick = order_rows(orders)
    attended = combine(own, cross, message, by_x, from2, pick)

    parts = [attended] + [turned(attended, k, 0) for k in (1, 2, 3)]
    far, near = gathered([a[:24] for a in parts]), gathered([a[24:] for a in parts])
    first_far, first_near = project(far[:3], weights), project(near[:3], weights)
    keep0, up, down, direct = plain(
        far_body, [SUM, TWO, TWO, SENT], *far[3], *weights, first_far
    )
    below, above = along_z(up, 1), along_z(down, -1)
    opposite = along_z(direct, 4)
    keep2, keep6 = plain(near_body, [SUM, SUM], *near[3], *weights, first_near)
    up2, down2 = plain(middle_body, [SENT, SENT], keep2, keep6, below, above)
    below2, above2 = along_z(up2, 2), along_z(down2, -2)
    own, other = plain(total_body, [HALF, HALF], keep0, below, above, below2, above2, opposite)
    return finish(own, other_core(other), pick)


def solution(mesh):
    placed = (
        P("batch", "head"),
        P(None, "batch", "head"),
        P(None, "batch", "head"),
        P(None, "batch", None, "head"),
        P("batch", None),
        P("batch"),
        P("batch"),
        P("head", "batch"),
    )
    return jax.shard_map(
        shards, mesh=mesh, in_specs=placed, out_specs=P("head", "batch"), check_vma=False
    )
```

```python
import jax
import jax.numpy as jnp
from jax import lax
from jax.experimental import pallas as pl
from jax.experimental.pallas import tpu as pltpu
from jax.sharding import PartitionSpec as P

DH = 128
GROUP = 16
SCALE = DH**-0.5
LOG2E = 1.4426950408889634
BATCH = 32
HEADS = 8
VMEM = pl.BlockSpec(memory_space=pltpu.VMEM)
SMEM = pl.BlockSpec(memory_space=pltpu.SMEM)
F32 = jnp.float32
BF16 = jnp.bfloat16
NT = (((1,), (1,)), ((), ()))
NN = (((1,), (0,)), ((), ()))


ANY = pl.BlockSpec(memory_space=pl.ANY)
HBM = pl.BlockSpec(memory_space=pltpu.HBM)


def params(mib=16):
    return pltpu.CompilerParams(vmem_limit_bytes=mib * 1024 * 1024)


def dot(a, b, dims=NN):
    return lax.dot_general(a, b, dims, preferred_element_type=F32)


def position():
    index = lax.axis_index("batch")
    return index >> 3, (index >> 1) & 3, index & 1, lax.axis_index("head")


def lanes():
    return lax.broadcasted_iota(jnp.int32, (GROUP, DH), 1)


def split_tile(tile, step):
    high = tile.astype(BF16).astype(F32)
    rest = tile - high
    middle = rest.astype(BF16).astype(F32)
    low = rest - middle
    joined = high + pltpu.roll(middle, step, 1) + pltpu.roll(low, 2 * step, 1)
    return joined.astype(BF16)


def join_tile(tile, step):
    wide = tile.astype(F32)
    return (wide + pltpu.roll(wide, DH - step, 1)) + pltpu.roll(wide, DH - 2 * step, 1)


def local_body(
    q_in, prompt_in, table_in, length_in, new_in, pool_in, o0, o1, o2, o3,
    q, prompt, table, length, new, pool, wide, scores, weights, slots, sems,
):
    pairs = [
        (q_in, q),
        (prompt_in, prompt),
        (table_in, table),
        (length_in, length),
        (new_in, new),
        (pool_in.at[0], pool.at[0]),
        (pool_in.at[1], pool.at[1]),
    ]
    copies = [pltpu.make_async_copy(a, b, sems.at[i]) for i, (a, b) in enumerate(pairs)]
    for copy in copies:
        copy.start()
    outs = (o0, o1, o2, o3)
    lane = lanes()
    x, y, _, _ = position()
    mask = 8 * x + 4 * (y >> 1)
    copies[0].wait()
    for h in range(GROUP):
        wide[:, h, :] = q[:, h * DH : (h + 1) * DH].astype(F32)
    copies[1].wait()
    for p in range(8):
        slots[32 + p] = 0
    order = jnp.zeros((GROUP, DH), F32)
    for n in range(32):
        p = prompt[n]
        k = slots[32 + p]
        slots[32 + p] = k + 1
        slots[n] = (4 * p + k) ^ mask
        order = jnp.where(lane == n, (4 * p + k).astype(F32), order)
    for copy in copies[2:6]:
        copy.wait()
    base = lax.axis_index("batch") * 256
    for n in range(32):
        keys = jnp.concatenate([pool[0, table[j, n] - base] for j in range(8)], axis=0)
        s = dot(wide[n].astype(BF16), keys, NT) * SCALE
        scores[n] = jnp.where(lane < length[n], s, -1e30)
    own_keys = new[0].astype(F32)
    own_values = new[1].astype(F32)
    own = jnp.stack(
        [jnp.sum(wide[n] * own_keys[n : n + 1], axis=1, keepdims=True) for n in range(32)]
    ) * SCALE
    s = scores[...]
    peak = jnp.maximum(jnp.max(s, axis=2, keepdims=True), own)
    w = jnp.exp(s - peak)
    own_weight = jnp.exp(own - peak)
    total = jnp.sum(w, axis=2, keepdims=True) + own_weight
    weights[...] = w.astype(BF16)
    own_weight = own_weight.astype(BF16).astype(F32)
    mass = peak + jnp.log(total)
    inverse = 1.0 / total
    copies[6].wait()
    for n in range(32):
        values = jnp.concatenate([pool[1, table[j, n] - base] for j in range(8)], axis=0)
        mixed = dot(weights[n], values) + own_weight[n] * own_values[n : n + 1]
        scores[slots[n]] = mixed * inverse[n]
    held = [jnp.zeros((GROUP, DH), F32) for _ in range(4)]
    for n in range(32):
        slot = slots[n]
        weights[slot] = wide[n].astype(BF16)
        for i in range(4):
            held[i] = jnp.where(lane + 8 * i == slot, jnp.where(lane < 8, mass[n], 0.0), held[i])
    for i, out in enumerate(outs):
        out[0:8] = weights[8 * i : 8 * i + 8]
        out[8] = order.astype(BF16)
        out[9:17] = scores[8 * i : 8 * i + 8].astype(BF16)
        out[17] = split_tile(jnp.where(lane < 8, held[i], 0.0), 8)


def local_parts(q, prompt, table, length, new, pool):
    out = jax.ShapeDtypeStruct((18, GROUP, DH), BF16)
    return pl.pallas_call(
        local_body,
        out_shape=[out] * 4,
        in_specs=[HBM] * 6,
        out_specs=[VMEM] * 4,
        scratch_shapes=[
            pltpu.VMEM((32, GROUP * DH), BF16),
            pltpu.SMEM((32,), jnp.int32),
            pltpu.SMEM((8, 32), jnp.int32),
            pltpu.SMEM((32,), jnp.int32),
            pltpu.VMEM((2, 32, DH), BF16),
            pltpu.VMEM((2, 256, GROUP, DH), BF16),
            pltpu.VMEM((32, GROUP, DH), F32),
            pltpu.VMEM((32, GROUP, DH), F32),
            pltpu.VMEM((32, GROUP, DH), BF16),
            pltpu.SMEM((40,), jnp.int32),
            pltpu.SemaphoreType.DMA((7,)),
        ],
        compiler_params=params(54),
        name="local_parts",
    )(q, prompt, table, length, new, pool)


def regroup_body(a0, a1, a2, a3, same, across):
    x, _, _, z = position()
    for i, a in enumerate((a0, a1, a2, a3)):
        same[4 * i : 4 * i + 4] = a[0:4]
        across[4 * i : 4 * i + 4] = a[4:8]
        across[17 + 5 * i : 22 + 5 * i] = a[13:18]

        @pl.when(x ^ (z >> 1) == i)
        def _(a=a):
            same[16] = a[8]
            across[16] = a[8]


def regroup(parts):
    return pl.pallas_call(
        regroup_body,
        out_shape=[
            jax.ShapeDtypeStruct((17, GROUP, DH), BF16),
            jax.ShapeDtypeStruct((37, GROUP, DH), BF16),
        ],
        in_specs=[VMEM] * 4,
        out_specs=[VMEM] * 2,
        compiler_params=params(),
        name="regroup",
    )(*parts)


ROWS = 256


def prefix_part(q, kv):
    s = dot(q, kv[0], NT)
    peak = jnp.max(s, axis=1, keepdims=True)
    w = jnp.exp2((s - peak) * (SCALE * LOG2E))
    return dot(w.astype(BF16), kv[1]), peak * SCALE, jnp.sum(w, axis=1, keepdims=True)


def prefix_block(q, kv0, kv1):
    mixed0, peak0, total0 = prefix_part(q, kv0)
    mixed1, peak1, total1 = prefix_part(q, kv1)
    top = jnp.maximum(peak0, peak1)
    f0, f1 = jnp.exp(peak0 - top), jnp.exp(peak1 - top)
    total = total0 * f0 + total1 * f1
    return (mixed0 * f0 + mixed1 * f1) * (1.0 / total), top + jnp.log(total)


COUNT = ROWS // GROUP


def prefix_send_body(qa, qb, kv0, kv1, after, out):
    lane = lanes()
    tile = jnp.zeros((GROUP, DH), F32)
    for half, q in enumerate((qa, qb)):
        for i in range(256 // ROWS):
            rows = q[i * COUNT : (i + 1) * COUNT].reshape(ROWS, DH)
            mixed, mass = prefix_block(rows, kv0, kv1)
            at = half * 16 + i * COUNT
            out[at : at + COUNT] = mixed.reshape(COUNT, GROUP, DH).astype(BF16)
            for n in range(COUNT):
                tile = jnp.where(lane == at + n, mass[n * GROUP : (n + 1) * GROUP], tile)
    out[32] = split_tile(tile, 32)


def prefix_keep_body(q, kv0, kv1, out, masses):
    for i in range(256 // ROWS):
        rows = q[i * COUNT : (i + 1) * COUNT].reshape(ROWS, DH)
        mixed, mass = prefix_block(rows, kv0, kv1)
        at = i * COUNT
        out[at : at + COUNT] = mixed.reshape(COUNT, GROUP, DH)
        masses[at : at + COUNT] = jnp.broadcast_to(mass, (ROWS, DH)).reshape(COUNT, GROUP, DH)


def prefix_cost(rows):
    return pl.CostEstimate(
        flops=4 * rows * 4096 * 128, bytes_accessed=2_500_000, transcendentals=rows * 4096
    )


def prefix_send(qa, qb, kv0, kv1, after):
    return pl.pallas_call(
        prefix_send_body,
        out_shape=jax.ShapeDtypeStruct((33, GROUP, DH), BF16),
        in_specs=[VMEM] * 4 + [ANY],
        out_specs=VMEM,
        compiler_params=params(24),
        cost_estimate=prefix_cost(512),
        name="prefix_send",
    )(qa, qb, kv0, kv1, after)


def prefix_keep(q, kv0, kv1):
    out = jax.ShapeDtypeStruct((16, GROUP, DH), F32)
    return pl.pallas_call(
        prefix_keep_body,
        out_shape=[out, out],
        in_specs=[VMEM] * 3,
        out_specs=[VMEM, VMEM],
        compiler_params=params(24),
        cost_estimate=prefix_cost(256),
        name="prefix_keep",
    )(q, kv0, kv1)


PLACES = 0x47210635


def combine_body(
    own, own_masses, cross, cross_masses, message, s0, s1, s2, s3, far, out, held
):
    x, y, _, z = position()
    y_high = y >> 1
    theirs = join_tile(message[32], 32)
    near = [join_tile(s[17], 8) for s in (s0, s1, s2, s3)]
    across = [join_tile(far[21 + 5 * i], 8) for i in range(4)]
    for g in range(2):
        for kx in range(4):
            for k in range(4):
                n = g * 16 + kx * 4 + k
                at = kx * 4 + k
                a, la = ((own, own_masses), (cross, cross_masses))[g]
                a, la = a[at], la[at]
                b = message[n].astype(F32)
                lb = jnp.broadcast_to(theirs[:, n : n + 1], (GROUP, DH))
                if g == 0:
                    s = (s0, s1, s2, s3)[kx][9 + k].astype(F32)
                    ls = jnp.broadcast_to(near[kx][:, k : k + 1], (GROUP, DH))
                else:
                    s = far[17 + 5 * kx + k].astype(F32)
                    ls = jnp.broadcast_to(across[kx][:, 4 + k : 5 + k], (GROUP, DH))
                top = jnp.maximum(jnp.maximum(la, lb), ls)
                ea, eb, es = jnp.exp(la - top), jnp.exp(lb - top), jnp.exp(ls - top)
                row = (ea * a + eb * b + es * s) / (ea + eb + es)
                target = (x ^ kx) * 2 + (y_high ^ g)
                held[((PLACES >> (4 * ((target - z) & 7))) & 7) * 4 + k] = row
    for h in range(GROUP):
        out[:, h * DH : (h + 1) * DH] = held[:, h, :].astype(BF16)


def combine(own, cross, message, near, far):
    return pl.pallas_call(
        combine_body,
        out_shape=jax.ShapeDtypeStruct((32, GROUP * DH), BF16),
        in_specs=[VMEM] * 10,
        out_specs=VMEM,
        scratch_shapes=[pltpu.VMEM((32, GROUP, DH), F32)],
        compiler_params=params(),
        name="combine",
    )(*own, *cross, message, *near, far)


def by_target(total, count):
    low = lax.broadcasted_iota(jnp.int32, (8, total.shape[1]), 0) < 4
    chunks = []
    for g in range(count // 2):
        even, odd = [], []
        for j in (0, 2):
            at = j * 4 * count + g * 8
            first, second = total[at : at + 8], total[at + 4 * count : at + 4 * count + 8]
            even.append(jnp.where(low, first, pltpu.roll(second, 4, 0)))
            odd.append(jnp.where(low, pltpu.roll(first, 4, 0), second))
        chunks += [jnp.concatenate(even, axis=0), jnp.concatenate(odd, axis=0)]
    return chunks


def project_body(a, b, c, w0, w1, out):
    count, size = out.shape[0], a.shape[0]
    rows = jnp.concatenate([a[...], b[...], c[...]], axis=0)
    for side, weight in enumerate((w0, w1)):
        total = dot(rows, weight[...])
        for i in range(3):
            for d, chunk in enumerate(by_target(total[size * i : size * i + size], count)):
                out[d, i * 16 : i * 16 + 16, side * 512 : side * 512 + 512] = chunk


def project(blocks, weights):
    size = blocks[0].shape[0]
    return pl.pallas_call(
        project_body,
        out_shape=jax.ShapeDtypeStruct((size // 16, 48, 1024), F32),
        in_specs=[VMEM] * 5,
        out_specs=VMEM,
        compiler_params=params(),
        cost_estimate=pl.CostEstimate(
            flops=2 * 3 * size * 2048 * 1024, bytes_accessed=4_500_000, transcendentals=0
        ),
        name="project",
    )(*blocks, *weights)


def last_chunks(a, b, w0, w1, first):
    rows = jnp.concatenate([a[...], b[...]], axis=0)
    for side, weight in enumerate((w0, w1)):
        columns = slice(side * 512, side * 512 + 512)
        for d, chunk in enumerate(by_target(dot(rows, weight[...]), first.shape[0])):
            yield columns, d, jnp.concatenate([first[d, :, columns], chunk], axis=0)


def far_body(a, b, w0, w1, first, keep, up, down, direct):
    for columns, d, whole in last_chunks(a, b, w0, w1, first):
        if d == 5:
            keep[:, columns] = whole
        elif d == 1:
            direct[:, columns] = whole.astype(BF16)
        else:
            out = up if d in (0, 3) else down
            out[d // 3, :, columns] = whole.astype(BF16)


def near_body(a, b, w0, w1, first, keep2, keep6):
    for columns, d, whole in last_chunks(a, b, w0, w1, first):
        (keep2, keep6)[d][:, columns] = whole


SUM = jax.ShapeDtypeStruct((64, 1024), F32)
SENT = jax.ShapeDtypeStruct((64, 1024), BF16)
HALF = jax.ShapeDtypeStruct((64, 512), BF16)
TWO = jax.ShapeDtypeStruct((2, 64, 1024), BF16)


def plain(body, out_shape, *args):
    return pl.pallas_call(
        body,
        out_shape=out_shape,
        in_specs=[VMEM] * len(args),
        out_specs=[VMEM] * len(out_shape),
        compiler_params=params(),
        name=body.__name__[:-5],
    )(*args)


def middle_body(keep2, keep6, below, above, up, down):
    up[...] = (keep2[...] + below[0].astype(F32)).astype(BF16)
    down[...] = (keep6[...] + above[0].astype(F32)).astype(BF16)


def total_body(keep, below, above, below2, above2, opposite, own, other):
    near = keep[...] + below[1].astype(F32) + above[1].astype(F32)
    whole = near + below2[...].astype(F32) + above2[...].astype(F32)
    whole = (whole + opposite[...].astype(F32)).astype(BF16)
    own[...] = whole[:, :512]
    other[...] = whole[:, 512:]


def order_body(orders, pick):
    x, y, core, z = position()
    lane = lanes()
    order = jnp.zeros((GROUP, DH), F32)
    for block in range(4):
        dy = (2 * (z & 1) + block // 2) ^ y
        tile = orders[((block % 2) ^ core) * 4 + dy].astype(F32)
        order = jnp.where(lane >> 5 == block, pltpu.roll(tile, 32 * block, 1), order)
    order = order.astype(jnp.int32)
    prompt, k = order >> 2, order & 3
    block = lane >> 5
    far = block & 1
    dx = (prompt >> 1) ^ x
    dy = (2 * (prompt & 1) + (block >> 1)) ^ y
    first = jnp.where(far == 0, dx, dy)
    second = jnp.where(far == 0, dy, dx)
    second = jnp.where(second >= 2, 5 - second, second)
    source = ((far ^ core) * 16 + second * 4 + first) * 4 + k
    row = lax.broadcasted_iota(jnp.int32, (128, 128), 0)
    pick[...] = (row == source[0:1]).astype(F32).astype(BF16)


def order_rows(orders):
    return pl.pallas_call(
        order_body,
        out_shape=jax.ShapeDtypeStruct((128, 128), BF16),
        in_specs=[VMEM],
        out_specs=VMEM,
        compiler_params=params(),
        name="order_rows",
    )(orders)


def finish_body(own, other, pick, out):
    dims = (((0,), (0,)), ((), ()))
    mixed = dot(pick[0:64], own[...], dims) + dot(pick[64:128], other[...], dims)
    out[...] = mixed.astype(BF16)


def finish(own, other, pick):
    return pl.pallas_call(
        finish_body,
        out_shape=jax.ShapeDtypeStruct((128, 512), BF16),
        in_specs=[VMEM] * 3,
        out_specs=VMEM,
        compiler_params=params(),
        name="finish",
    )(own, other, pick)


def along(value, shift, k):
    return lax.ppermute(value, "batch", [(i, i ^ (k << shift)) for i in range(BATCH)])


def along_x(value, k):
    return along(value, 3, k)


def along_y(value, k):
    return along(value, 1, k)


def other_core(value):
    return along(value, 0, 1)


def turned(value, k, phase):
    pairs = [(i, i ^ (k << (3 if (i & 1) == phase else 1))) for i in range(BATCH)]
    return lax.ppermute(value, "batch", pairs)


def gathered(parts):
    ring0 = jnp.concatenate(parts, axis=0)
    ring1, ring3 = turned(ring0, 1, 1), turned(ring0, 3, 1)
    half = ring0.shape[0] // 2
    return ring0, ring1, ring3, [turned(ring3[:half], 1, 1), turned(ring1[half:], 3, 1)]


def along_z(value, k):
    return lax.ppermute(value, "head", [(i, (i + k) % HEADS) for i in range(HEADS)])


def shards(queries, new_kv, prefix_kv, suffix_kv, page_table, suffix_len, prompt_of, out_weight):
    prefix_other = other_core(prefix_kv)
    weights = [out_weight, other_core(out_weight)]

    sent = local_parts(queries, prompt_of, page_table.T, suffix_len, new_kv, suffix_kv)
    by_x = [sent[0]] + [along_x(sent[k], k) for k in (1, 2, 3)]
    same, across = regroup(by_x)
    from1, from3 = along_y(same, 1), along_y(across, 3)

    own = prefix_keep(same, prefix_kv, prefix_other)
    passed, own = lax.optimization_barrier((from3, own))
    from2 = along_y(passed, 1)
    message = prefix_send(from1, from3, prefix_kv, prefix_other, own[1])
    message, from2 = lax.optimization_barrier((message, from2))
    message = along_y(message, 1)
    cross = prefix_keep(from2, prefix_kv, prefix_other)
    attended = combine(own, cross, message, by_x, from2)
    orders = jnp.stack([same[16], from1[16], from2[16], from3[16]])
    orders = jnp.concatenate([orders, other_core(orders)], axis=0)
    pick = order_rows(orders)

    parts = [attended] + [turned(attended, k, 0) for k in (1, 2, 3)]
    far, near = gathered([a[:24] for a in parts]), gathered([a[24:] for a in parts])
    first_far = project(far[:3], weights)
    three, first_far = lax.optimization_barrier((near[:3], first_far))
    first_near = project(three, weights)
    last_far, first_near = lax.optimization_barrier((far[3], first_near))
    keep0, up, down, direct = plain(
        far_body, [SUM, TWO, TWO, SENT], *last_far, *weights, first_far
    )
    below, above = along_z(up, 1), along_z(down, -1)
    opposite = along_z(direct, 4)
    keep2, keep6 = plain(near_body, [SUM, SUM], *near[3], *weights, first_near)
    up2, down2 = plain(middle_body, [SENT, SENT], keep2, keep6, below, above)
    below2, above2 = along_z(up2, 2), along_z(down2, -2)
    own, other = plain(total_body, [HALF, HALF], keep0, below, above, below2, above2, opposite)
    return finish(own, other_core(other), pick)


def solution(mesh):
    placed = (
        P("batch", "head"),
        P(None, "batch", "head"),
        P(None, "batch", "head"),
        P(None, "batch", None, "head"),
        P("batch", None),
        P("batch"),
        P("batch"),
        P("head", "batch"),
    )
    return jax.shard_map(
        shards, mesh=mesh, in_specs=placed, out_specs=P("head", "batch"), check_vma=False
    )
```

```python
import jax
import jax.numpy as jnp
from jax import lax
from jax.experimental import pallas as pl
from jax.experimental.pallas import tpu as pltpu
from jax.sharding import PartitionSpec as P

DH = 128
GROUP = 16
SCALE = DH**-0.5
LOG2E = 1.4426950408889634
BATCH = 32
HEADS = 8
VMEM = pl.BlockSpec(memory_space=pltpu.VMEM)
SMEM = pl.BlockSpec(memory_space=pltpu.SMEM)
F32 = jnp.float32
BF16 = jnp.bfloat16
NT = (((1,), (1,)), ((), ()))
NN = (((1,), (0,)), ((), ()))


ANY = pl.BlockSpec(memory_space=pl.ANY)
HBM = pl.BlockSpec(memory_space=pltpu.HBM)


def params(mib=16):
    return pltpu.CompilerParams(vmem_limit_bytes=mib * 1024 * 1024)


def dot(a, b, dims=NN):
    return lax.dot_general(a, b, dims, preferred_element_type=F32)


def position():
    index = lax.axis_index("batch")
    return index >> 3, (index >> 1) & 3, index & 1, lax.axis_index("head")


def lanes():
    return lax.broadcasted_iota(jnp.int32, (GROUP, DH), 1)


def split_tile(tile, step):
    high = tile.astype(BF16).astype(F32)
    rest = tile - high
    middle = rest.astype(BF16).astype(F32)
    low = rest - middle
    joined = high + pltpu.roll(middle, step, 1) + pltpu.roll(low, 2 * step, 1)
    return joined.astype(BF16)


def join_tile(tile, step):
    wide = tile.astype(F32)
    return (wide + pltpu.roll(wide, DH - step, 1)) + pltpu.roll(wide, DH - 2 * step, 1)


def local_body(
    q_in, prompt_in, table_in, length_in, new_in, pool_in, o0, o1, o2, o3,
    q, prompt, table, length, new, pool, wide, scores, weights, slots, sems,
):
    pairs = [
        (q_in, q),
        (prompt_in, prompt),
        (table_in, table),
        (length_in, length),
        (new_in, new),
        (pool_in.at[0], pool.at[0]),
        (pool_in.at[1], pool.at[1]),
    ]
    copies = [pltpu.make_async_copy(a, b, sems.at[i]) for i, (a, b) in enumerate(pairs)]
    for copy in copies:
        copy.start()
    outs = (o0, o1, o2, o3)
    lane = lanes()
    x, y, _, _ = position()
    mask = 8 * x + 4 * (y >> 1)
    copies[0].wait()
    for h in range(GROUP):
        wide[:, h, :] = q[:, h * DH : (h + 1) * DH].astype(F32)
    copies[1].wait()
    for p in range(8):
        slots[32 + p] = 0
    order = jnp.zeros((GROUP, DH), F32)
    for n in range(32):
        p = prompt[n]
        k = slots[32 + p]
        slots[32 + p] = k + 1
        slots[n] = (4 * p + k) ^ mask
        order = jnp.where(lane == n, (4 * p + k).astype(F32), order)
    for copy in copies[2:6]:
        copy.wait()
    base = lax.axis_index("batch") * 256
    for n in range(32):
        keys = jnp.concatenate([pool[0, table[j, n] - base] for j in range(8)], axis=0)
        s = dot(wide[n].astype(BF16), keys, NT) * SCALE
        scores[n] = jnp.where(lane < length[n], s, -1e30)
    own_keys = new[0].astype(F32)
    own_values = new[1].astype(F32)
    own = jnp.stack(
        [jnp.sum(wide[n] * own_keys[n : n + 1], axis=1, keepdims=True) for n in range(32)]
    ) * SCALE
    s = scores[...]
    peak = jnp.maximum(jnp.max(s, axis=2, keepdims=True), own)
    w = jnp.exp(s - peak)
    own_weight = jnp.exp(own - peak)
    total = jnp.sum(w, axis=2, keepdims=True) + own_weight
    weights[...] = w.astype(BF16)
    own_weight = own_weight.astype(BF16).astype(F32)
    mass = peak + jnp.log(total)
    inverse = 1.0 / total
    copies[6].wait()
    for n in range(32):
        values = jnp.concatenate([pool[1, table[j, n] - base] for j in range(8)], axis=0)
        mixed = dot(weights[n], values) + own_weight[n] * own_values[n : n + 1]
        scores[slots[n]] = mixed * inverse[n]
    held = [jnp.zeros((GROUP, DH), F32) for _ in range(4)]
    for n in range(32):
        slot = slots[n]
        weights[slot] = wide[n].astype(BF16)
        for i in range(4):
            held[i] = jnp.where(lane + 8 * i == slot, jnp.where(lane < 8, mass[n], 0.0), held[i])
    for i, out in enumerate(outs):
        out[0:8] = weights[8 * i : 8 * i + 8]
        out[8] = order.astype(BF16)
        out[9:17] = scores[8 * i : 8 * i + 8].astype(BF16)
        out[17] = split_tile(jnp.where(lane < 8, held[i], 0.0), 8)


def local_parts(q, prompt, table, length, new, pool):
    out = jax.ShapeDtypeStruct((18, GROUP, DH), BF16)
    return pl.pallas_call(
        local_body,
        out_shape=[out] * 4,
        in_specs=[HBM] * 6,
        out_specs=[VMEM] * 4,
        scratch_shapes=[
            pltpu.VMEM((32, GROUP * DH), BF16),
            pltpu.SMEM((32,), jnp.int32),
            pltpu.SMEM((8, 32), jnp.int32),
            pltpu.SMEM((32,), jnp.int32),
            pltpu.VMEM((2, 32, DH), BF16),
            pltpu.VMEM((2, 256, GROUP, DH), BF16),
            pltpu.VMEM((32, GROUP, DH), F32),
            pltpu.VMEM((32, GROUP, DH), F32),
            pltpu.VMEM((32, GROUP, DH), BF16),
            pltpu.SMEM((40,), jnp.int32),
            pltpu.SemaphoreType.DMA((7,)),
        ],
        compiler_params=params(54),
        name="local_parts",
    )(q, prompt, table, length, new, pool)


def regroup_body(a0, a1, a2, a3, same, across):
    x, _, _, z = position()
    for i, a in enumerate((a0, a1, a2, a3)):
        same[4 * i : 4 * i + 4] = a[0:4]
        across[4 * i : 4 * i + 4] = a[4:8]
        across[17 + 5 * i : 22 + 5 * i] = a[13:18]

        @pl.when(x ^ (z >> 1) == i)
        def _(a=a):
            same[16] = a[8]
            across[16] = a[8]


def regroup(parts):
    return pl.pallas_call(
        regroup_body,
        out_shape=[
            jax.ShapeDtypeStruct((17, GROUP, DH), BF16),
            jax.ShapeDtypeStruct((37, GROUP, DH), BF16),
        ],
        in_specs=[VMEM] * 4,
        out_specs=[VMEM] * 2,
        compiler_params=params(),
        name="regroup",
    )(*parts)


ROWS = 256


def prefix_part(q, kv):
    s = dot(q, kv[0], NT)
    peak = jnp.max(s, axis=1, keepdims=True)
    w = jnp.exp2((s - peak) * (SCALE * LOG2E))
    return dot(w.astype(BF16), kv[1]), peak * SCALE, jnp.sum(w, axis=1, keepdims=True)


def prefix_block(q, kv0, kv1):
    mixed0, peak0, total0 = prefix_part(q, kv0)
    mixed1, peak1, total1 = prefix_part(q, kv1)
    top = jnp.maximum(peak0, peak1)
    f0, f1 = jnp.exp(peak0 - top), jnp.exp(peak1 - top)
    total = total0 * f0 + total1 * f1
    return (mixed0 * f0 + mixed1 * f1) * (1.0 / total), top + jnp.log(total)


COUNT = ROWS // GROUP


def prefix_send_body(qa, qb, kv0, kv1, after, out):
    lane = lanes()
    tile = jnp.zeros((GROUP, DH), F32)
    for half, q in enumerate((qa, qb)):
        for i in range(256 // ROWS):
            rows = q[i * COUNT : (i + 1) * COUNT].reshape(ROWS, DH)
            mixed, mass = prefix_block(rows, kv0, kv1)
            at = half * 16 + i * COUNT
            out[at : at + COUNT] = mixed.reshape(COUNT, GROUP, DH).astype(BF16)
            for n in range(COUNT):
                tile = jnp.where(lane == at + n, mass[n * GROUP : (n + 1) * GROUP], tile)
    out[32] = split_tile(tile, 32)


def prefix_keep_body(q, kv0, kv1, out, masses):
    for i in range(256 // ROWS):
        rows = q[i * COUNT : (i + 1) * COUNT].reshape(ROWS, DH)
        mixed, mass = prefix_block(rows, kv0, kv1)
        at = i * COUNT
        out[at : at + COUNT] = mixed.reshape(COUNT, GROUP, DH)
        masses[at : at + COUNT] = jnp.broadcast_to(mass, (ROWS, DH)).reshape(COUNT, GROUP, DH)


def prefix_cost(rows):
    return pl.CostEstimate(
        flops=4 * rows * 4096 * 128, bytes_accessed=2_500_000, transcendentals=rows * 4096
    )


def prefix_send(qa, qb, kv0, kv1, after):
    return pl.pallas_call(
        prefix_send_body,
        out_shape=jax.ShapeDtypeStruct((33, GROUP, DH), BF16),
        in_specs=[VMEM] * 4 + [ANY],
        out_specs=VMEM,
        compiler_params=params(24),
        cost_estimate=prefix_cost(512),
        name="prefix_send",
    )(qa, qb, kv0, kv1, after)


def prefix_keep(q, kv0, kv1):
    out = jax.ShapeDtypeStruct((16, GROUP, DH), F32)
    return pl.pallas_call(
        prefix_keep_body,
        out_shape=[out, out],
        in_specs=[VMEM] * 3,
        out_specs=[VMEM, VMEM],
        compiler_params=params(24),
        cost_estimate=prefix_cost(256),
        name="prefix_keep",
    )(q, kv0, kv1)


def combine_body(
    own, own_masses, cross, cross_masses, message, s0, s1, s2, s3, far, out, held
):
    x, y, _, z = position()
    y_high = y >> 1
    theirs = join_tile(message[32], 32)
    near = [join_tile(s[17], 8) for s in (s0, s1, s2, s3)]
    across = [join_tile(far[21 + 5 * i], 8) for i in range(4)]
    for g in range(2):
        for kx in range(4):
            for k in range(4):
                n = g * 16 + kx * 4 + k
                at = kx * 4 + k
                a, la = ((own, own_masses), (cross, cross_masses))[g]
                a, la = a[at], la[at]
                b = message[n].astype(F32)
                lb = jnp.broadcast_to(theirs[:, n : n + 1], (GROUP, DH))
                if g == 0:
                    s = (s0, s1, s2, s3)[kx][9 + k].astype(F32)
                    ls = jnp.broadcast_to(near[kx][:, k : k + 1], (GROUP, DH))
                else:
                    s = far[17 + 5 * kx + k].astype(F32)
                    ls = jnp.broadcast_to(across[kx][:, 4 + k : 5 + k], (GROUP, DH))
                top = jnp.maximum(jnp.maximum(la, lb), ls)
                ea, eb, es = jnp.exp(la - top), jnp.exp(lb - top), jnp.exp(ls - top)
                row = (ea * a + eb * b + es * s) / (ea + eb + es)
                target = (x ^ kx) * 2 + (y_high ^ g)
                held[((target - z - 2) & 7) * 4 + k] = row
    for h in range(GROUP):
        out[:, h * DH : (h + 1) * DH] = held[:, h, :].astype(BF16)


def combine(own, cross, message, near, far):
    return pl.pallas_call(
        combine_body,
        out_shape=jax.ShapeDtypeStruct((32, GROUP * DH), BF16),
        in_specs=[VMEM] * 10,
        out_specs=VMEM,
        scratch_shapes=[pltpu.VMEM((32, GROUP, DH), F32)],
        compiler_params=params(),
        name="combine",
    )(*own, *cross, message, *near, far)


def by_target(total):
    low = lax.broadcasted_iota(jnp.int32, (8, total.shape[1]), 0) < 4
    chunks = []
    for g in range(2):
        even, odd = [], []
        for j in (0, 2):
            first = total[j * 16 + g * 8 : j * 16 + g * 8 + 8]
            second = total[(j + 1) * 16 + g * 8 : (j + 1) * 16 + g * 8 + 8]
            even.append(jnp.where(low, first, pltpu.roll(second, 4, 0)))
            odd.append(jnp.where(low, pltpu.roll(first, 4, 0), second))
        chunks += [jnp.concatenate(even, axis=0), jnp.concatenate(odd, axis=0)]
    return chunks


def project_body(a, b, c, w0, w1, out):
    rows = jnp.concatenate([a[...], b[...], c[...]], axis=0)
    for side, weight in enumerate((w0, w1)):
        total = dot(rows, weight[...])
        for i in range(3):
            for d, chunk in enumerate(by_target(total[64 * i : 64 * i + 64])):
                out[d, i * 16 : i * 16 + 16, side * 512 : side * 512 + 512] = chunk


def project(blocks, weights):
    return pl.pallas_call(
        project_body,
        out_shape=jax.ShapeDtypeStruct((4, 48, 1024), F32),
        in_specs=[VMEM] * 5,
        out_specs=VMEM,
        compiler_params=params(),
        cost_estimate=pl.CostEstimate(
            flops=2 * 192 * 2048 * 1024, bytes_accessed=4_500_000, transcendentals=0
        ),
        name="project",
    )(*blocks, *weights)


def last_chunks(a, b, w0, w1, first):
    rows = jnp.concatenate([a[...], b[...]], axis=0)
    for side, weight in enumerate((w0, w1)):
        columns = slice(side * 512, side * 512 + 512)
        for d, chunk in enumerate(by_target(dot(rows, weight[...]))):
            yield side, columns, d, jnp.concatenate([first[d, :, columns], chunk], axis=0)


def far_body(a, b, w0, w1, first, keep, up, down, direct):
    for _, columns, d, whole in last_chunks(a, b, w0, w1, first):
        if d == 0:
            keep[:, columns] = whole
        else:
            (up, direct, down)[d - 1][:, columns] = whole.astype(BF16)


def near_body(a, b, w0, w1, first, keep6, down, keep0, up):
    for _, columns, d, whole in last_chunks(a, b, w0, w1, first):
        if d in (0, 2):
            (keep6, keep0)[d // 2][:, columns] = whole
        else:
            (down, up)[d // 2][:, columns] = whole.astype(BF16)


SUM = jax.ShapeDtypeStruct((64, 1024), F32)
SENT = jax.ShapeDtypeStruct((64, 1024), BF16)
HALF = jax.ShapeDtypeStruct((64, 512), BF16)


def plain(body, out_shape, *args):
    return pl.pallas_call(
        body,
        out_shape=out_shape,
        in_specs=[VMEM] * len(args),
        out_specs=[VMEM] * len(out_shape),
        compiler_params=params(),
        name=body.__name__[:-5],
    )(*args)


def middle_body(keep2, keep6, below, above, up, down):
    up[...] = (keep2[...] + below[...].astype(F32)).astype(BF16)
    down[...] = (keep6[...] + above[...].astype(F32)).astype(BF16)


def total_body(keep, below1, above1, below2, above2, opposite, own, other):
    near = keep[...] + below1[...].astype(F32) + above1[...].astype(F32)
    whole = near + below2[...].astype(F32) + above2[...].astype(F32)
    whole = (whole + opposite[...].astype(F32)).astype(BF16)
    own[...] = whole[:, :512]
    other[...] = whole[:, 512:]


def order_body(orders, pick):
    x, y, core, z = position()
    lane = lanes()
    order = jnp.zeros((GROUP, DH), F32)
    for block in range(4):
        dy = (2 * (z & 1) + block // 2) ^ y
        tile = orders[((block % 2) ^ core) * 4 + dy].astype(F32)
        order = jnp.where(lane >> 5 == block, pltpu.roll(tile, 32 * block, 1), order)
    order = order.astype(jnp.int32)
    prompt, k = order >> 2, order & 3
    block = lane >> 5
    far = block & 1
    dx = (prompt >> 1) ^ x
    dy = (2 * (prompt & 1) + (block >> 1)) ^ y
    first = jnp.where(far == 0, dx, dy)
    second = jnp.where(far == 0, dy, dx)
    second = jnp.where(second >= 2, 5 - second, second)
    source = ((far ^ core) * 16 + second * 4 + first) * 4 + k
    row = lax.broadcasted_iota(jnp.int32, (128, 128), 0)
    pick[...] = (row == source[0:1]).astype(F32).astype(BF16)


def order_rows(orders):
    return pl.pallas_call(
        order_body,
        out_shape=jax.ShapeDtypeStruct((128, 128), BF16),
        in_specs=[VMEM],
        out_specs=VMEM,
        compiler_params=params(),
        name="order_rows",
    )(orders)


def finish_body(own, other, pick, out):
    dims = (((0,), (0,)), ((), ()))
    mixed = dot(pick[0:64], own[...], dims) + dot(pick[64:128], other[...], dims)
    out[...] = mixed.astype(BF16)


def finish(own, other, pick):
    return pl.pallas_call(
        finish_body,
        out_shape=jax.ShapeDtypeStruct((128, 512), BF16),
        in_specs=[VMEM] * 3,
        out_specs=VMEM,
        compiler_params=params(),
        name="finish",
    )(own, other, pick)


def along(value, shift, k):
    return lax.ppermute(value, "batch", [(i, i ^ (k << shift)) for i in range(BATCH)])


def along_x(value, k):
    return along(value, 3, k)


def along_y(value, k):
    return along(value, 1, k)


def other_core(value):
    return along(value, 0, 1)


def turned(value, k, phase):
    pairs = [(i, i ^ (k << (3 if (i & 1) == phase else 1))) for i in range(BATCH)]
    return lax.ppermute(value, "batch", pairs)


def gathered(parts):
    ring0 = jnp.concatenate(parts, axis=0)
    ring1, ring3 = turned(ring0, 1, 1), turned(ring0, 3, 1)
    return ring0, ring1, ring3, [turned(ring3[:32], 1, 1), turned(ring1[32:], 3, 1)]


def along_z(value, k):
    return lax.ppermute(value, "head", [(i, (i + k) % HEADS) for i in range(HEADS)])


def shards(queries, new_kv, prefix_kv, suffix_kv, page_table, suffix_len, prompt_of, out_weight):
    prefix_other = other_core(prefix_kv)
    weights = [out_weight, other_core(out_weight)]

    sent = local_parts(queries, prompt_of, page_table.T, suffix_len, new_kv, suffix_kv)
    by_x = [sent[0]] + [along_x(sent[k], k) for k in (1, 2, 3)]
    same, across = regroup(by_x)
    from1, from3 = along_y(same, 1), along_y(across, 3)

    own = prefix_keep(same, prefix_kv, prefix_other)
    passed, own = lax.optimization_barrier((from3, own))
    from2 = along_y(passed, 1)
    message = prefix_send(from1, from3, prefix_kv, prefix_other, own[1])
    message, from2 = lax.optimization_barrier((message, from2))
    message = along_y(message, 1)
    cross = prefix_keep(from2, prefix_kv, prefix_other)
    attended = combine(own, cross, message, by_x, from2)

    orders = jnp.stack([same[16], from1[16], from2[16], from3[16]])
    orders = jnp.concatenate([orders, other_core(orders)], axis=0)
    pick = order_rows(orders)

    parts = [attended] + [turned(attended, k, 0) for k in (1, 2, 3)]
    far, near = [gathered([a[i : i + 16] for a in parts]) for i in (0, 16)]
    first_far, first_near = project(far[:3], weights), project(near[:3], weights)
    keep2, up3, down3, up4 = plain(
        far_body, [SUM, SENT, SENT, SENT], *far[3], *weights, first_far
    )
    below3, above3 = along_z(up3, 1), along_z(down3, -1)
    opposite = along_z(up4, 4)
    keep6, down1, keep0, up1 = plain(
        near_body, [SUM, SENT, SUM, SENT], *near[3], *weights, first_near
    )
    below1, above1 = along_z(up1, 1), along_z(down1, -1)
    up2, down2 = plain(middle_body, [SENT, SENT], keep2, keep6, below3, above3)
    below2, above2 = along_z(up2, 2), along_z(down2, -2)
    own, other = plain(total_body, [HALF, HALF], keep0, below1, above1, below2, above2, opposite)
    return finish(own, other_core(other), pick)


def solution(mesh):
    placed = (
        P("batch", "head"),
        P(None, "batch", "head"),
        P(None, "batch", "head"),
        P(None, "batch", None, "head"),
        P("batch", None),
        P("batch"),
        P("batch"),
        P("head", "batch"),
    )
    return jax.shard_map(
        shards, mesh=mesh, in_specs=placed, out_specs=P("head", "batch"), check_vma=False
    )
```

```python
import jax
import jax.numpy as jnp
from jax import lax
from jax.experimental import pallas as pl
from jax.experimental.pallas import tpu as pltpu
from jax.sharding import PartitionSpec as P

DH = 128
GROUP = 16
SCALE = DH**-0.5
LOG2E = 1.4426950408889634
BATCH = 32
HEADS = 8
VMEM = pl.BlockSpec(memory_space=pltpu.VMEM)
SMEM = pl.BlockSpec(memory_space=pltpu.SMEM)
F32 = jnp.float32
BF16 = jnp.bfloat16
NT = (((1,), (1,)), ((), ()))
NN = (((1,), (0,)), ((), ()))


ANY = pl.BlockSpec(memory_space=pl.ANY)
HBM = pl.BlockSpec(memory_space=pltpu.HBM)


def params(mib=16):
    return pltpu.CompilerParams(vmem_limit_bytes=mib * 1024 * 1024)


def dot(a, b, dims=NN):
    return lax.dot_general(a, b, dims, preferred_element_type=F32)


def position():
    index = lax.axis_index("batch")
    return index >> 3, (index >> 1) & 3, index & 1, lax.axis_index("head")


def lanes():
    return lax.broadcasted_iota(jnp.int32, (GROUP, DH), 1)


def split_tile(tile, step):
    high = tile.astype(BF16).astype(F32)
    rest = tile - high
    middle = rest.astype(BF16).astype(F32)
    low = rest - middle
    joined = high + pltpu.roll(middle, step, 1) + pltpu.roll(low, 2 * step, 1)
    return joined.astype(BF16)


def join_tile(tile, step):
    wide = tile.astype(F32)
    return (wide + pltpu.roll(wide, DH - step, 1)) + pltpu.roll(wide, DH - 2 * step, 1)


def local_body(
    q_in, prompt_in, table_in, length_in, new_in, pool_in, o0, o1, o2, o3,
    q, prompt, table, length, new, pool, wide, scores, weights, slots, sems,
):
    pairs = [
        (q_in, q),
        (prompt_in, prompt),
        (table_in, table),
        (length_in, length),
        (new_in, new),
        (pool_in.at[0], pool.at[0]),
        (pool_in.at[1], pool.at[1]),
    ]
    copies = [pltpu.make_async_copy(a, b, sems.at[i]) for i, (a, b) in enumerate(pairs)]
    for copy in copies:
        copy.start()
    outs = (o0, o1, o2, o3)
    lane = lanes()
    x, y, _, _ = position()
    mask = 8 * x + 4 * (y >> 1)
    copies[0].wait()
    for h in range(GROUP):
        wide[:, h, :] = q[:, h * DH : (h + 1) * DH].astype(F32)
    copies[1].wait()
    for p in range(8):
        slots[32 + p] = 0
    order = jnp.zeros((GROUP, DH), F32)
    for n in range(32):
        p = prompt[n]
        k = slots[32 + p]
        slots[32 + p] = k + 1
        slots[n] = (4 * p + k) ^ mask
        order = jnp.where(lane == n, (4 * p + k).astype(F32), order)
    for copy in copies[2:6]:
        copy.wait()
    base = lax.axis_index("batch") * 256
    for n in range(32):
        keys = jnp.concatenate([pool[0, table[j, n] - base] for j in range(8)], axis=0)
        s = dot(wide[n].astype(BF16), keys, NT) * SCALE
        scores[n] = jnp.where(lane < length[n], s, -1e30)
    own_keys = new[0].astype(F32)
    own_values = new[1].astype(F32)
    own = jnp.stack(
        [jnp.sum(wide[n] * own_keys[n : n + 1], axis=1, keepdims=True) for n in range(32)]
    ) * SCALE
    s = scores[...]
    peak = jnp.maximum(jnp.max(s, axis=2, keepdims=True), own)
    w = jnp.exp(s - peak)
    own_weight = jnp.exp(own - peak)
    total = jnp.sum(w, axis=2, keepdims=True) + own_weight
    weights[...] = w.astype(BF16)
    own_weight = own_weight.astype(BF16).astype(F32)
    mass = peak + jnp.log(total)
    inverse = 1.0 / total
    copies[6].wait()
    for n in range(32):
        values = jnp.concatenate([pool[1, table[j, n] - base] for j in range(8)], axis=0)
        mixed = dot(weights[n], values) + own_weight[n] * own_values[n : n + 1]
        scores[slots[n]] = mixed * inverse[n]
    held = [jnp.zeros((GROUP, DH), F32) for _ in range(4)]
    for n in range(32):
        slot = slots[n]
        weights[slot] = wide[n].astype(BF16)
        for i in range(4):
            held[i] = jnp.where(lane + 8 * i == slot, jnp.where(lane < 8, mass[n], 0.0), held[i])
    for i, out in enumerate(outs):
        out[0:8] = weights[8 * i : 8 * i + 8]
        out[8] = order.astype(BF16)
        out[9:17] = scores[8 * i : 8 * i + 8].astype(BF16)
        out[17] = split_tile(jnp.where(lane < 8, held[i], 0.0), 8)


def local_parts(q, prompt, table, length, new, pool):
    out = jax.ShapeDtypeStruct((18, GROUP, DH), BF16)
    return pl.pallas_call(
        local_body,
        out_shape=[out] * 4,
        in_specs=[HBM] * 6,
        out_specs=[VMEM] * 4,
        scratch_shapes=[
            pltpu.VMEM((32, GROUP * DH), BF16),
            pltpu.SMEM((32,), jnp.int32),
            pltpu.SMEM((8, 32), jnp.int32),
            pltpu.SMEM((32,), jnp.int32),
            pltpu.VMEM((2, 32, DH), BF16),
            pltpu.VMEM((2, 256, GROUP, DH), BF16),
            pltpu.VMEM((32, GROUP, DH), F32),
            pltpu.VMEM((32, GROUP, DH), F32),
            pltpu.VMEM((32, GROUP, DH), BF16),
            pltpu.SMEM((40,), jnp.int32),
            pltpu.SemaphoreType.DMA((7,)),
        ],
        compiler_params=params(54),
        name="local_parts",
    )(q, prompt, table, length, new, pool)


def regroup_body(a2, a1, a3, a0, same, across):
    x, _, _, z = position()
    for i, a in enumerate((a0, a1, a2, a3)):
        same[4 * i : 4 * i + 4] = a[0:4]
        across[4 * i : 4 * i + 4] = a[4:8]
        across[17 + 5 * i : 22 + 5 * i] = a[13:18]

        @pl.when(x ^ (z >> 1) == i)
        def _(a=a):
            same[16] = a[8]
            across[16] = a[8]


def regroup(parts):
    return pl.pallas_call(
        regroup_body,
        out_shape=[
            jax.ShapeDtypeStruct((17, GROUP, DH), BF16),
            jax.ShapeDtypeStruct((37, GROUP, DH), BF16),
        ],
        in_specs=[VMEM] * 4,
        out_specs=[VMEM] * 2,
        compiler_params=params(),
        name="regroup",
    )(parts[2], parts[1], parts[3], parts[0])


ROWS = 256


def prefix_part(q, kv):
    s = dot(q, kv[0], NT)
    peak = jnp.max(s, axis=1, keepdims=True)
    w = jnp.exp2((s - peak) * (SCALE * LOG2E))
    return dot(w.astype(BF16), kv[1]), peak * SCALE, jnp.sum(w, axis=1, keepdims=True)


def prefix_block(q, kv0, kv1):
    mixed0, peak0, total0 = prefix_part(q, kv0)
    mixed1, peak1, total1 = prefix_part(q, kv1)
    top = jnp.maximum(peak0, peak1)
    f0, f1 = jnp.exp(peak0 - top), jnp.exp(peak1 - top)
    total = total0 * f0 + total1 * f1
    return (mixed0 * f0 + mixed1 * f1) * (1.0 / total), top + jnp.log(total)


COUNT = ROWS // GROUP


def prefix_send_body(qa, qb, kv0, kv1, after, out):
    lane = lanes()
    tile = jnp.zeros((GROUP, DH), F32)
    for half, q in enumerate((qa, qb)):
        for i in range(256 // ROWS):
            rows = q[i * COUNT : (i + 1) * COUNT].reshape(ROWS, DH)
            mixed, mass = prefix_block(rows, kv0, kv1)
            at = half * 16 + i * COUNT
            out[at : at + COUNT] = mixed.reshape(COUNT, GROUP, DH).astype(BF16)
            for n in range(COUNT):
                tile = jnp.where(lane == at + n, mass[n * GROUP : (n + 1) * GROUP], tile)
    out[32] = split_tile(tile, 32)


def prefix_keep_body(q, kv0, kv1, out, masses):
    for i in range(256 // ROWS):
        rows = q[i * COUNT : (i + 1) * COUNT].reshape(ROWS, DH)
        mixed, mass = prefix_block(rows, kv0, kv1)
        at = i * COUNT
        out[at : at + COUNT] = mixed.reshape(COUNT, GROUP, DH)
        masses[at : at + COUNT] = jnp.broadcast_to(mass, (ROWS, DH)).reshape(COUNT, GROUP, DH)


def prefix_cost(rows):
    return pl.CostEstimate(
        flops=4 * rows * 4096 * 128, bytes_accessed=2_500_000, transcendentals=rows * 4096
    )


def prefix_send(qa, qb, kv0, kv1, after):
    return pl.pallas_call(
        prefix_send_body,
        out_shape=jax.ShapeDtypeStruct((33, GROUP, DH), BF16),
        in_specs=[VMEM] * 4 + [ANY],
        out_specs=VMEM,
        compiler_params=params(24),
        cost_estimate=prefix_cost(512),
        name="prefix_send",
    )(qa, qb, kv0, kv1, after)


def prefix_keep(q, kv0, kv1):
    out = jax.ShapeDtypeStruct((16, GROUP, DH), F32)
    return pl.pallas_call(
        prefix_keep_body,
        out_shape=[out, out],
        in_specs=[VMEM] * 3,
        out_specs=[VMEM, VMEM],
        compiler_params=params(24),
        cost_estimate=prefix_cost(256),
        name="prefix_keep",
    )(q, kv0, kv1)


def combine_body(
    own, own_masses, cross, cross_masses, message, s0, s1, s2, s3, far, out, held
):
    x, y, _, z = position()
    y_high = y >> 1
    theirs = join_tile(message[32], 32)
    near = [join_tile(s[17], 8) for s in (s0, s1, s2, s3)]
    across = [join_tile(far[21 + 5 * i], 8) for i in range(4)]
    for g in range(2):
        for kx in range(4):
            for k in range(4):
                n = g * 16 + kx * 4 + k
                at = kx * 4 + k
                a, la = ((own, own_masses), (cross, cross_masses))[g]
                a, la = a[at], la[at]
                b = message[n].astype(F32)
                lb = jnp.broadcast_to(theirs[:, n : n + 1], (GROUP, DH))
                if g == 0:
                    s = (s0, s1, s2, s3)[kx][9 + k].astype(F32)
                    ls = jnp.broadcast_to(near[kx][:, k : k + 1], (GROUP, DH))
                else:
                    s = far[17 + 5 * kx + k].astype(F32)
                    ls = jnp.broadcast_to(across[kx][:, 4 + k : 5 + k], (GROUP, DH))
                top = jnp.maximum(jnp.maximum(la, lb), ls)
                ea, eb, es = jnp.exp(la - top), jnp.exp(lb - top), jnp.exp(ls - top)
                row = (ea * a + eb * b + es * s) / (ea + eb + es)
                target = (x ^ kx) * 2 + (y_high ^ g)
                held[((target - z - 2) & 7) * 4 + k] = row
    for h in range(GROUP):
        out[:, h * DH : (h + 1) * DH] = held[:, h, :].astype(BF16)


def combine(own, cross, message, near, far):
    return pl.pallas_call(
        combine_body,
        out_shape=jax.ShapeDtypeStruct((32, GROUP * DH), BF16),
        in_specs=[VMEM] * 10,
        out_specs=VMEM,
        scratch_shapes=[pltpu.VMEM((32, GROUP, DH), F32)],
        compiler_params=params(),
        name="combine",
    )(*own, *cross, message, *near, far)


def by_target(total):
    low = lax.broadcasted_iota(jnp.int32, (8, total.shape[1]), 0) < 4
    chunks = []
    for g in range(2):
        even, odd = [], []
        for j in (0, 2):
            first = total[j * 16 + g * 8 : j * 16 + g * 8 + 8]
            second = total[(j + 1) * 16 + g * 8 : (j + 1) * 16 + g * 8 + 8]
            even.append(jnp.where(low, first, pltpu.roll(second, 4, 0)))
            odd.append(jnp.where(low, pltpu.roll(first, 4, 0), second))
        chunks += [jnp.concatenate(even, axis=0), jnp.concatenate(odd, axis=0)]
    return chunks


def project_body(a, b, c, w0, w1, out):
    rows = jnp.concatenate([a[...], b[...], c[...]], axis=0)
    for side, weight in enumerate((w0, w1)):
        total = dot(rows, weight[...])
        for i in range(3):
            for d, chunk in enumerate(by_target(total[64 * i : 64 * i + 64])):
                out[d, i * 16 : i * 16 + 16, side * 512 : side * 512 + 512] = chunk


def project(blocks, weights):
    return pl.pallas_call(
        project_body,
        out_shape=jax.ShapeDtypeStruct((4, 48, 1024), F32),
        in_specs=[VMEM] * 5,
        out_specs=VMEM,
        compiler_params=params(),
        cost_estimate=pl.CostEstimate(
            flops=2 * 192 * 2048 * 1024, bytes_accessed=4_500_000, transcendentals=0
        ),
        name="project",
    )(*blocks, *weights)


def last_chunks(a, b, w0, w1, first):
    rows = jnp.concatenate([a[...], b[...]], axis=0)
    for side, weight in enumerate((w0, w1)):
        columns = slice(side * 512, side * 512 + 512)
        for d, chunk in enumerate(by_target(dot(rows, weight[...]))):
            yield side, columns, d, jnp.concatenate([first[d, :, columns], chunk], axis=0)


def far_body(a, b, w0, w1, first, keep, up, down, direct):
    for _, columns, d, whole in last_chunks(a, b, w0, w1, first):
        if d == 0:
            keep[:, columns] = whole
        else:
            (up, direct, down)[d - 1][:, columns] = whole.astype(BF16)


def near_body(a, b, w0, w1, first, keep6, down, keep0, up):
    for _, columns, d, whole in last_chunks(a, b, w0, w1, first):
        if d in (0, 2):
            (keep6, keep0)[d // 2][:, columns] = whole
        else:
            (down, up)[d // 2][:, columns] = whole.astype(BF16)


SUM = jax.ShapeDtypeStruct((64, 1024), F32)
SENT = jax.ShapeDtypeStruct((64, 1024), BF16)
HALF = jax.ShapeDtypeStruct((64, 512), BF16)


def plain(body, out_shape, *args):
    return pl.pallas_call(
        body,
        out_shape=out_shape,
        in_specs=[VMEM] * len(args),
        out_specs=[VMEM] * len(out_shape),
        compiler_params=params(),
        name=body.__name__[:-5],
    )(*args)


def middle_body(keep2, keep6, below, above, up, down):
    up[...] = (keep2[...] + below[...].astype(F32)).astype(BF16)
    down[...] = (keep6[...] + above[...].astype(F32)).astype(BF16)


def total_body(keep, below1, above1, below2, above2, opposite, own, other):
    near = keep[...] + below1[...].astype(F32) + above1[...].astype(F32)
    whole = near + below2[...].astype(F32) + above2[...].astype(F32)
    whole = (whole + opposite[...].astype(F32)).astype(BF16)
    own[...] = whole[:, :512]
    other[...] = whole[:, 512:]


def order_body(orders, pick):
    x, y, core, z = position()
    lane = lanes()
    order = jnp.zeros((GROUP, DH), F32)
    for block in range(4):
        dy = (2 * (z & 1) + block // 2) ^ y
        tile = orders[((block % 2) ^ core) * 4 + dy].astype(F32)
        order = jnp.where(lane >> 5 == block, pltpu.roll(tile, 32 * block, 1), order)
    order = order.astype(jnp.int32)
    prompt, k = order >> 2, order & 3
    block = lane >> 5
    far = block & 1
    dx = (prompt >> 1) ^ x
    dy = (2 * (prompt & 1) + (block >> 1)) ^ y
    first = jnp.where(far == 0, dx, dy)
    second = jnp.where(far == 0, dy, dx)
    first = jnp.where((first == 1) | (first == 2), 3 - first, first)
    second = jnp.where(second >= 2, 5 - second, second)
    source = ((far ^ core) * 16 + second * 4 + first) * 4 + k
    row = lax.broadcasted_iota(jnp.int32, (128, 128), 0)
    pick[...] = (row == source[0:1]).astype(F32).astype(BF16)


def order_rows(orders):
    return pl.pallas_call(
        order_body,
        out_shape=jax.ShapeDtypeStruct((128, 128), BF16),
        in_specs=[VMEM],
        out_specs=VMEM,
        compiler_params=params(),
        name="order_rows",
    )(orders)


def finish_body(own, other, pick, out):
    dims = (((0,), (0,)), ((), ()))
    mixed = dot(pick[0:64], own[...], dims) + dot(pick[64:128], other[...], dims)
    out[...] = mixed.astype(BF16)


def finish(own, other, pick):
    return pl.pallas_call(
        finish_body,
        out_shape=jax.ShapeDtypeStruct((128, 512), BF16),
        in_specs=[VMEM] * 3,
        out_specs=VMEM,
        compiler_params=params(),
        name="finish",
    )(own, other, pick)


def along(value, shift, k):
    return lax.ppermute(value, "batch", [(i, i ^ (k << shift)) for i in range(BATCH)])


def along_x(value, k):
    return along(value, 3, k)


def along_y(value, k):
    return along(value, 1, k)


def other_core(value):
    return along(value, 0, 1)


def turned(value, k, phase):
    pairs = [(i, i ^ (k << (3 if (i & 1) == phase else 1))) for i in range(BATCH)]
    return lax.ppermute(value, "batch", pairs)


def gathered(parts):
    ring0 = jnp.concatenate(parts, axis=0)
    ring1, ring3 = turned(ring0, 1, 1), turned(ring0, 3, 1)
    return ring0, ring1, ring3, [turned(ring3[:32], 1, 1), turned(ring1[32:], 3, 1)]


def along_z(value, k):
    return lax.ppermute(value, "head", [(i, (i + k) % HEADS) for i in range(HEADS)])


def shards(queries, new_kv, prefix_kv, suffix_kv, page_table, suffix_len, prompt_of, out_weight):
    prefix_other = other_core(prefix_kv)
    weights = [out_weight, other_core(out_weight)]

    sent = local_parts(queries, prompt_of, page_table.T, suffix_len, new_kv, suffix_kv)
    x2, x1, x3 = (along_x(sent[k], k) for k in (2, 1, 3))
    by_x = [sent[0], x1, x2, x3]
    same, across = regroup(by_x)
    from1, from3 = along_y(same, 1), along_y(across, 3)

    own = prefix_keep(same, prefix_kv, prefix_other)
    passed, own = lax.optimization_barrier((from3, own))
    from2 = along_y(passed, 1)
    message = prefix_send(from1, from3, prefix_kv, prefix_other, own[1])
    message, from2 = lax.optimization_barrier((message, from2))
    message = along_y(message, 1)
    cross = prefix_keep(from2, prefix_kv, prefix_other)
    attended = combine(own, cross, message, by_x, from2)

    orders = jnp.stack([same[16], from1[16], from2[16], from3[16]])
    orders = jnp.concatenate([orders, other_core(orders)], axis=0)
    pick = order_rows(orders)

    next2, next1, next3 = (turned(attended, k, 0) for k in (2, 1, 3))
    parts = [attended, next2, next1, next3]
    far, near = [gathered([a[i : i + 16] for a in parts]) for i in (0, 16)]
    first_far, first_near = project(far[:3], weights), project(near[:3], weights)
    keep2, up3, down3, up4 = plain(
        far_body, [SUM, SENT, SENT, SENT], *far[3], *weights, first_far
    )
    below3, above3 = along_z(up3, 1), along_z(down3, -1)
    opposite = along_z(up4, 4)
    keep6, down1, keep0, up1 = plain(
        near_body, [SUM, SENT, SUM, SENT], *near[3], *weights, first_near
    )
    up2, down2 = plain(middle_body, [SENT, SENT], keep2, keep6, below3, above3)
    below2, above2 = along_z(up2, 2), along_z(down2, -2)
    up1, down1, opposite = lax.optimization_barrier((up1, down1, opposite))
    below1, above1 = along_z(up1, 1), along_z(down1, -1)
    own, other = plain(total_body, [HALF, HALF], keep0, below1, above1, below2, above2, opposite)
    return finish(own, other_core(other), pick)


def solution(mesh):
    placed = (
        P("batch", "head"),
        P(None, "batch", "head"),
        P(None, "batch", "head"),
        P(None, "batch", None, "head"),
        P("batch", None),
        P("batch"),
        P("batch"),
        P("head", "batch"),
    )
    return jax.shard_map(
        shards, mesh=mesh, in_specs=placed, out_specs=P("head", "batch"), check_vma=False
    )
```

```python
import jax
import jax.numpy as jnp
from jax import lax
from jax.experimental import pallas as pl
from jax.experimental.pallas import tpu as pltpu
from jax.sharding import PartitionSpec as P

DH = 128
GROUP = 16
SCALE = DH**-0.5
LOG2E = 1.4426950408889634
BATCH = 32
HEADS = 8
VMEM = pl.BlockSpec(memory_space=pltpu.VMEM)
SMEM = pl.BlockSpec(memory_space=pltpu.SMEM)
F32 = jnp.float32
BF16 = jnp.bfloat16
NT = (((1,), (1,)), ((), ()))
NN = (((1,), (0,)), ((), ()))


ANY = pl.BlockSpec(memory_space=pl.ANY)
HBM = pl.BlockSpec(memory_space=pltpu.HBM)


def params(mib=16):
    return pltpu.CompilerParams(vmem_limit_bytes=mib * 1024 * 1024)


def dot(a, b, dims=NN):
    return lax.dot_general(a, b, dims, preferred_element_type=F32)


def position():
    index = lax.axis_index("batch")
    return index >> 3, (index >> 1) & 3, index & 1, lax.axis_index("head")


def lanes():
    return lax.broadcasted_iota(jnp.int32, (GROUP, DH), 1)


def split_tile(tile, step):
    high = tile.astype(BF16).astype(F32)
    rest = tile - high
    middle = rest.astype(BF16).astype(F32)
    low = rest - middle
    joined = high + pltpu.roll(middle, step, 1) + pltpu.roll(low, 2 * step, 1)
    return joined.astype(BF16)


def join_tile(tile, step):
    wide = tile.astype(F32)
    return (wide + pltpu.roll(wide, DH - step, 1)) + pltpu.roll(wide, DH - 2 * step, 1)


def local_body(
    q_in, prompt_in, table_in, length_in, new_in, pool_in, o0, o1, o2, o3,
    q, prompt, table, length, new, pool, wide, scores, weights, slots, sems,
):
    pairs = [
        (q_in, q),
        (prompt_in, prompt),
        (table_in, table),
        (length_in, length),
        (new_in, new),
        (pool_in.at[0], pool.at[0]),
        (pool_in.at[1], pool.at[1]),
    ]
    copies = [pltpu.make_async_copy(a, b, sems.at[i]) for i, (a, b) in enumerate(pairs)]
    for copy in copies:
        copy.start()
    outs = (o0, o1, o2, o3)
    lane = lanes()
    x, y, _, _ = position()
    mask = 8 * x + 4 * (y >> 1)
    copies[0].wait()
    for h in range(GROUP):
        wide[:, h, :] = q[:, h * DH : (h + 1) * DH].astype(F32)
    copies[1].wait()
    for p in range(8):
        slots[32 + p] = 0
    order = jnp.zeros((GROUP, DH), F32)
    for n in range(32):
        p = prompt[n]
        k = slots[32 + p]
        slots[32 + p] = k + 1
        slots[n] = (4 * p + k) ^ mask
        order = jnp.where(lane == n, (4 * p + k).astype(F32), order)
    for copy in copies[2:6]:
        copy.wait()
    base = lax.axis_index("batch") * 256
    for n in range(32):
        keys = jnp.concatenate([pool[0, table[j, n] - base] for j in range(8)], axis=0)
        s = dot(wide[n].astype(BF16), keys, NT) * SCALE
        scores[n] = jnp.where(lane < length[n], s, -1e30)
    own_keys = new[0].astype(F32)
    own_values = new[1].astype(F32)
    own = jnp.stack(
        [jnp.sum(wide[n] * own_keys[n : n + 1], axis=1, keepdims=True) for n in range(32)]
    ) * SCALE
    s = scores[...]
    peak = jnp.maximum(jnp.max(s, axis=2, keepdims=True), own)
    w = jnp.exp(s - peak)
    own_weight = jnp.exp(own - peak)
    total = jnp.sum(w, axis=2, keepdims=True) + own_weight
    weights[...] = w.astype(BF16)
    own_weight = own_weight.astype(BF16).astype(F32)
    mass = peak + jnp.log(total)
    inverse = 1.0 / total
    copies[6].wait()
    for n in range(32):
        values = jnp.concatenate([pool[1, table[j, n] - base] for j in range(8)], axis=0)
        mixed = dot(weights[n], values) + own_weight[n] * own_values[n : n + 1]
        scores[slots[n]] = mixed * inverse[n]
    held = [jnp.zeros((GROUP, DH), F32) for _ in range(4)]
    for n in range(32):
        slot = slots[n]
        weights[slot] = wide[n].astype(BF16)
        for i in range(4):
            held[i] = jnp.where(lane + 8 * i == slot, jnp.where(lane < 8, mass[n], 0.0), held[i])
    for i, out in enumerate(outs):
        out[0:8] = weights[8 * i : 8 * i + 8]
        out[8] = order.astype(BF16)
        out[9:17] = scores[8 * i : 8 * i + 8].astype(BF16)
        out[17] = split_tile(jnp.where(lane < 8, held[i], 0.0), 8)


def local_parts(q, prompt, table, length, new, pool):
    out = jax.ShapeDtypeStruct((18, GROUP, DH), BF16)
    return pl.pallas_call(
        local_body,
        out_shape=[out] * 4,
        in_specs=[HBM] * 6,
        out_specs=[VMEM] * 4,
        scratch_shapes=[
            pltpu.VMEM((32, GROUP * DH), BF16),
            pltpu.SMEM((32,), jnp.int32),
            pltpu.SMEM((8, 32), jnp.int32),
            pltpu.SMEM((32,), jnp.int32),
            pltpu.VMEM((2, 32, DH), BF16),
            pltpu.VMEM((2, 256, GROUP, DH), BF16),
            pltpu.VMEM((32, GROUP, DH), F32),
            pltpu.VMEM((32, GROUP, DH), F32),
            pltpu.VMEM((32, GROUP, DH), BF16),
            pltpu.SMEM((40,), jnp.int32),
            pltpu.SemaphoreType.DMA((7,)),
        ],
        compiler_params=params(54),
        name="local_parts",
    )(q, prompt, table, length, new, pool)


def regroup_body(a2, a1, a3, a0, same, across):
    x, _, _, z = position()
    for i, a in enumerate((a0, a1, a2, a3)):
        same[4 * i : 4 * i + 4] = a[0:4]
        across[4 * i : 4 * i + 4] = a[4:8]
        across[17 + 5 * i : 22 + 5 * i] = a[13:18]

        @pl.when(x ^ (z >> 1) == i)
        def _(a=a):
            same[16] = a[8]
            across[16] = a[8]


def regroup(parts):
    return pl.pallas_call(
        regroup_body,
        out_shape=[
            jax.ShapeDtypeStruct((17, GROUP, DH), BF16),
            jax.ShapeDtypeStruct((37, GROUP, DH), BF16),
        ],
        in_specs=[VMEM] * 4,
        out_specs=[VMEM] * 2,
        compiler_params=params(),
        name="regroup",
    )(parts[2], parts[1], parts[3], parts[0])


ROWS = 256


def prefix_part(q, kv):
    s = dot(q, kv[0], NT)
    peak = jnp.max(s, axis=1, keepdims=True)
    w = jnp.exp2((s - peak) * (SCALE * LOG2E))
    return dot(w.astype(BF16), kv[1]), peak * SCALE, jnp.sum(w, axis=1, keepdims=True)


def prefix_block(q, kv0, kv1):
    mixed0, peak0, total0 = prefix_part(q, kv0)
    mixed1, peak1, total1 = prefix_part(q, kv1)
    top = jnp.maximum(peak0, peak1)
    f0, f1 = jnp.exp(peak0 - top), jnp.exp(peak1 - top)
    total = total0 * f0 + total1 * f1
    return (mixed0 * f0 + mixed1 * f1) * (1.0 / total), top + jnp.log(total)


COUNT = ROWS // GROUP


def prefix_send_body(qa, qb, kv0, kv1, after, out):
    lane = lanes()
    tile = jnp.zeros((GROUP, DH), F32)
    for half, q in enumerate((qa, qb)):
        for i in range(256 // ROWS):
            rows = q[i * COUNT : (i + 1) * COUNT].reshape(ROWS, DH)
            mixed, mass = prefix_block(rows, kv0, kv1)
            at = half * 16 + i * COUNT
            out[at : at + COUNT] = mixed.reshape(COUNT, GROUP, DH).astype(BF16)
            for n in range(COUNT):
                tile = jnp.where(lane == at + n, mass[n * GROUP : (n + 1) * GROUP], tile)
    out[32] = split_tile(tile, 32)


def prefix_keep_body(q, kv0, kv1, out, masses):
    for i in range(256 // ROWS):
        rows = q[i * COUNT : (i + 1) * COUNT].reshape(ROWS, DH)
        mixed, mass = prefix_block(rows, kv0, kv1)
        at = i * COUNT
        out[at : at + COUNT] = mixed.reshape(COUNT, GROUP, DH)
        masses[at : at + COUNT] = jnp.broadcast_to(mass, (ROWS, DH)).reshape(COUNT, GROUP, DH)


def prefix_cost(rows):
    return pl.CostEstimate(
        flops=4 * rows * 4096 * 128, bytes_accessed=2_500_000, transcendentals=rows * 4096
    )


def prefix_send(qa, qb, kv0, kv1, after):
    return pl.pallas_call(
        prefix_send_body,
        out_shape=jax.ShapeDtypeStruct((33, GROUP, DH), BF16),
        in_specs=[VMEM] * 4 + [ANY],
        out_specs=VMEM,
        compiler_params=params(24),
        cost_estimate=prefix_cost(512),
        name="prefix_send",
    )(qa, qb, kv0, kv1, after)


def prefix_keep(q, kv0, kv1):
    out = jax.ShapeDtypeStruct((16, GROUP, DH), F32)
    return pl.pallas_call(
        prefix_keep_body,
        out_shape=[out, out],
        in_specs=[VMEM] * 3,
        out_specs=[VMEM, VMEM],
        compiler_params=params(24),
        cost_estimate=prefix_cost(256),
        name="prefix_keep",
    )(q, kv0, kv1)


def combine_body(
    own, own_masses, cross, cross_masses, message, s0, s1, s2, s3, far, out, held
):
    x, y, _, z = position()
    y_high = y >> 1
    theirs = join_tile(message[32], 32)
    near = [join_tile(s[17], 8) for s in (s0, s1, s2, s3)]
    across = [join_tile(far[21 + 5 * i], 8) for i in range(4)]
    for g in range(2):
        for kx in range(4):
            for k in range(4):
                n = g * 16 + kx * 4 + k
                at = kx * 4 + k
                a, la = ((own, own_masses), (cross, cross_masses))[g]
                a, la = a[at], la[at]
                b = message[n].astype(F32)
                lb = jnp.broadcast_to(theirs[:, n : n + 1], (GROUP, DH))
                if g == 0:
                    s = (s0, s1, s2, s3)[kx][9 + k].astype(F32)
                    ls = jnp.broadcast_to(near[kx][:, k : k + 1], (GROUP, DH))
                else:
                    s = far[17 + 5 * kx + k].astype(F32)
                    ls = jnp.broadcast_to(across[kx][:, 4 + k : 5 + k], (GROUP, DH))
                top = jnp.maximum(jnp.maximum(la, lb), ls)
                ea, eb, es = jnp.exp(la - top), jnp.exp(lb - top), jnp.exp(ls - top)
                row = (ea * a + eb * b + es * s) / (ea + eb + es)
                target = (x ^ kx) * 2 + (y_high ^ g)
                held[((target - z - 2) & 7) * 4 + k] = row
    for h in range(GROUP):
        out[:, h * DH : (h + 1) * DH] = held[:, h, :].astype(BF16)


def combine(own, cross, message, near, far):
    return pl.pallas_call(
        combine_body,
        out_shape=jax.ShapeDtypeStruct((32, GROUP * DH), BF16),
        in_specs=[VMEM] * 10,
        out_specs=VMEM,
        scratch_shapes=[pltpu.VMEM((32, GROUP, DH), F32)],
        compiler_params=params(),
        name="combine",
    )(*own, *cross, message, *near, far)


def by_target(total):
    low = lax.broadcasted_iota(jnp.int32, (8, total.shape[1]), 0) < 4
    chunks = []
    for g in range(2):
        even, odd = [], []
        for j in (0, 2):
            first = total[j * 16 + g * 8 : j * 16 + g * 8 + 8]
            second = total[(j + 1) * 16 + g * 8 : (j + 1) * 16 + g * 8 + 8]
            even.append(jnp.where(low, first, pltpu.roll(second, 4, 0)))
            odd.append(jnp.where(low, pltpu.roll(first, 4, 0), second))
        chunks += [jnp.concatenate(even, axis=0), jnp.concatenate(odd, axis=0)]
    return chunks


def project_body(a, b, c, w0, w1, out):
    rows = jnp.concatenate([a[...], b[...], c[...]], axis=0)
    for side, weight in enumerate((w0, w1)):
        total = dot(rows, weight[...])
        for i in range(3):
            for d, chunk in enumerate(by_target(total[64 * i : 64 * i + 64])):
                out[d, i * 16 : i * 16 + 16, side * 512 : side * 512 + 512] = chunk


def project(blocks, weights):
    return pl.pallas_call(
        project_body,
        out_shape=jax.ShapeDtypeStruct((4, 48, 1024), F32),
        in_specs=[VMEM] * 5,
        out_specs=VMEM,
        compiler_params=params(),
        cost_estimate=pl.CostEstimate(
            flops=2 * 192 * 2048 * 1024, bytes_accessed=4_500_000, transcendentals=0
        ),
        name="project",
    )(*blocks, *weights)


def last_chunks(a, b, w0, w1, first):
    rows = jnp.concatenate([a[...], b[...]], axis=0)
    for side, weight in enumerate((w0, w1)):
        columns = slice(side * 512, side * 512 + 512)
        for d, chunk in enumerate(by_target(dot(rows, weight[...]))):
            yield side, columns, d, jnp.concatenate([first[d, :, columns], chunk], axis=0)


def far_body(a, b, w0, w1, first, keep, up, down, direct):
    for _, columns, d, whole in last_chunks(a, b, w0, w1, first):
        if d == 0:
            keep[:, columns] = whole
        else:
            (up, direct, down)[d - 1][:, columns] = whole.astype(BF16)


def near_body(a, b, w0, w1, first, keep6, down, keep0, up):
    for _, columns, d, whole in last_chunks(a, b, w0, w1, first):
        if d in (0, 2):
            (keep6, keep0)[d // 2][:, columns] = whole
        else:
            (down, up)[d // 2][:, columns] = whole.astype(BF16)


SUM = jax.ShapeDtypeStruct((64, 1024), F32)
SENT = jax.ShapeDtypeStruct((64, 1024), BF16)
HALF = jax.ShapeDtypeStruct((64, 512), BF16)


def plain(body, out_shape, *args):
    return pl.pallas_call(
        body,
        out_shape=out_shape,
        in_specs=[VMEM] * len(args),
        out_specs=[VMEM] * len(out_shape),
        compiler_params=params(),
        name=body.__name__[:-5],
    )(*args)


def middle_body(keep2, keep6, below, above, up, down):
    up[...] = (keep2[...] + below[...].astype(F32)).astype(BF16)
    down[...] = (keep6[...] + above[...].astype(F32)).astype(BF16)


def total_body(keep, below2, above2, below1, above1, opposite, own, other):
    near = keep[...] + below1[...].astype(F32) + above1[...].astype(F32)
    whole = near + below2[...].astype(F32) + above2[...].astype(F32)
    whole = (whole + opposite[...].astype(F32)).astype(BF16)
    own[...] = whole[:, :512]
    other[...] = whole[:, 512:]


def order_body(orders, pick):
    x, y, core, z = position()
    lane = lanes()
    order = jnp.zeros((GROUP, DH), F32)
    for block in range(4):
        dy = (2 * (z & 1) + block // 2) ^ y
        tile = orders[((block % 2) ^ core) * 4 + dy].astype(F32)
        order = jnp.where(lane >> 5 == block, pltpu.roll(tile, 32 * block, 1), order)
    order = order.astype(jnp.int32)
    prompt, k = order >> 2, order & 3
    block = lane >> 5
    far = block & 1
    dx = (prompt >> 1) ^ x
    dy = (2 * (prompt & 1) + (block >> 1)) ^ y
    first = jnp.where(far == 0, dx, dy)
    second = jnp.where(far == 0, dy, dx)
    first = jnp.where((first == 1) | (first == 2), 3 - first, first)
    second = jnp.where(second >= 2, 5 - second, second)
    source = ((far ^ core) * 16 + second * 4 + first) * 4 + k
    row = lax.broadcasted_iota(jnp.int32, (128, 128), 0)
    pick[...] = (row == source[0:1]).astype(F32).astype(BF16)


def order_rows(orders):
    return pl.pallas_call(
        order_body,
        out_shape=jax.ShapeDtypeStruct((128, 128), BF16),
        in_specs=[VMEM],
        out_specs=VMEM,
        compiler_params=params(),
        name="order_rows",
    )(orders)


def finish_body(own, other, pick, out):
    dims = (((0,), (0,)), ((), ()))
    mixed = dot(pick[0:64], own[...], dims) + dot(pick[64:128], other[...], dims)
    out[...] = mixed.astype(BF16)


def finish(own, other, pick):
    return pl.pallas_call(
        finish_body,
        out_shape=jax.ShapeDtypeStruct((128, 512), BF16),
        in_specs=[VMEM] * 3,
        out_specs=VMEM,
        compiler_params=params(),
        name="finish",
    )(own, other, pick)


def along(value, shift, k):
    return lax.ppermute(value, "batch", [(i, i ^ (k << shift)) for i in range(BATCH)])


def along_x(value, k):
    return along(value, 3, k)


def along_y(value, k):
    return along(value, 1, k)


def other_core(value):
    return along(value, 0, 1)


def turned(value, k, phase):
    pairs = [(i, i ^ (k << (3 if (i & 1) == phase else 1))) for i in range(BATCH)]
    return lax.ppermute(value, "batch", pairs)


def gathered(parts):
    ring0 = jnp.concatenate(parts, axis=0)
    ring1, ring3 = turned(ring0, 1, 1), turned(ring0, 3, 1)
    return ring0, ring1, ring3, [turned(ring3[:32], 1, 1), turned(ring1[32:], 3, 1)]


def along_z(value, k):
    return lax.ppermute(value, "head", [(i, (i + k) % HEADS) for i in range(HEADS)])


def shards(queries, new_kv, prefix_kv, suffix_kv, page_table, suffix_len, prompt_of, out_weight):
    prefix_other = other_core(prefix_kv)
    weights = [out_weight, other_core(out_weight)]

    sent = local_parts(queries, prompt_of, page_table.T, suffix_len, new_kv, suffix_kv)
    x2, x1, x3 = (along_x(sent[k], k) for k in (2, 1, 3))
    by_x = [sent[0], x1, x2, x3]
    same, across = regroup(by_x)
    from1, from3 = along_y(same, 1), along_y(across, 3)

    own = prefix_keep(same, prefix_kv, prefix_other)
    passed, own = lax.optimization_barrier((from3, own))
    from2 = along_y(passed, 1)
    message = prefix_send(from1, from3, prefix_kv, prefix_other, own[1])
    message, from2 = lax.optimization_barrier((message, from2))
    message = along_y(message, 1)
    cross = prefix_keep(from2, prefix_kv, prefix_other)
    attended = combine(own, cross, message, by_x, from2)

    orders = jnp.stack([same[16], from1[16], from2[16], from3[16]])
    orders = jnp.concatenate([orders, other_core(orders)], axis=0)
    pick = order_rows(orders)

    next2, next1, next3 = (turned(attended, k, 0) for k in (2, 1, 3))
    parts = [attended, next2, next1, next3]
    far, near = [gathered([a[i : i + 16] for a in parts]) for i in (0, 16)]
    first_far, first_near = project(far[:3], weights), project(near[:3], weights)
    keep2, up3, down3, up4 = plain(
        far_body, [SUM, SENT, SENT, SENT], *far[3], *weights, first_far
    )
    below3, above3 = along_z(up3, 1), along_z(down3, -1)
    opposite = along_z(up4, 4)
    keep6, down1, keep0, up1 = plain(
        near_body, [SUM, SENT, SUM, SENT], *near[3], *weights, first_near
    )
    up2, down2 = plain(middle_body, [SENT, SENT], keep2, keep6, below3, above3)
    up1, down1, up2, down2 = lax.optimization_barrier((up1, down1, up2, down2))
    below2, above2 = along_z(up2, 2), along_z(down2, -2)
    below1, above1 = along_z(up1, 1), along_z(down1, -1)
    own, other = plain(total_body, [HALF, HALF], keep0, below2, above2, below1, above1, opposite)
    return finish(own, other_core(other), pick)


def solution(mesh):
    placed = (
        P("batch", "head"),
        P(None, "batch", "head"),
        P(None, "batch", "head"),
        P(None, "batch", None, "head"),
        P("batch", None),
        P("batch"),
        P("batch"),
        P("head", "batch"),
    )
    return jax.shard_map(
        shards, mesh=mesh, in_specs=placed, out_specs=P("head", "batch"), check_vma=False
    )
```

```python
import jax
import jax.numpy as jnp
from jax import lax
from jax.experimental import pallas as pl
from jax.experimental.pallas import tpu as pltpu
from jax.sharding import PartitionSpec as P

DH = 128
GROUP = 16
SCALE = DH**-0.5
LOG2E = 1.4426950408889634
BATCH = 32
HEADS = 8
VMEM = pl.BlockSpec(memory_space=pltpu.VMEM)
SMEM = pl.BlockSpec(memory_space=pltpu.SMEM)
F32 = jnp.float32
BF16 = jnp.bfloat16
NT = (((1,), (1,)), ((), ()))
NN = (((1,), (0,)), ((), ()))


ANY = pl.BlockSpec(memory_space=pl.ANY)
HBM = pl.BlockSpec(memory_space=pltpu.HBM)


def params(mib=16):
    return pltpu.CompilerParams(vmem_limit_bytes=mib * 1024 * 1024)


def dot(a, b, dims=NN):
    return lax.dot_general(a, b, dims, preferred_element_type=F32)


def position():
    index = lax.axis_index("batch")
    return index >> 3, (index >> 1) & 3, index & 1, lax.axis_index("head")


def lanes():
    return lax.broadcasted_iota(jnp.int32, (GROUP, DH), 1)


def split_tile(tile, step):
    high = tile.astype(BF16).astype(F32)
    rest = tile - high
    middle = rest.astype(BF16).astype(F32)
    low = rest - middle
    joined = high + pltpu.roll(middle, step, 1) + pltpu.roll(low, 2 * step, 1)
    return joined.astype(BF16)


def join_tile(tile, step):
    wide = tile.astype(F32)
    return (wide + pltpu.roll(wide, DH - step, 1)) + pltpu.roll(wide, DH - 2 * step, 1)


def local_body(
    q_in, prompt_in, table_in, length_in, new_in, pool_in, o0, o1, o2, o3,
    q, prompt, table, length, new, pool, wide, scores, weights, slots, sems,
):
    pairs = [
        (q_in, q),
        (prompt_in, prompt),
        (table_in, table),
        (length_in, length),
        (new_in, new),
        (pool_in.at[0], pool.at[0]),
        (pool_in.at[1], pool.at[1]),
    ]
    copies = [pltpu.make_async_copy(a, b, sems.at[i]) for i, (a, b) in enumerate(pairs)]
    for copy in copies:
        copy.start()
    outs = (o0, o1, o2, o3)
    lane = lanes()
    x, y, _, _ = position()
    mask = 8 * x + 4 * (y >> 1)
    copies[0].wait()
    for h in range(GROUP):
        wide[:, h, :] = q[:, h * DH : (h + 1) * DH].astype(F32)
    copies[1].wait()
    for p in range(8):
        slots[32 + p] = 0
    order = jnp.zeros((GROUP, DH), F32)
    for n in range(32):
        p = prompt[n]
        k = slots[32 + p]
        slots[32 + p] = k + 1
        slots[n] = (4 * p + k) ^ mask
        order = jnp.where(lane == n, (4 * p + k).astype(F32), order)
    for copy in copies[2:6]:
        copy.wait()
    base = lax.axis_index("batch") * 256
    for n in range(32):
        keys = jnp.concatenate([pool[0, table[j, n] - base] for j in range(8)], axis=0)
        s = dot(wide[n].astype(BF16), keys, NT) * SCALE
        scores[n] = jnp.where(lane < length[n], s, -1e30)
    own_keys = new[0].astype(F32)
    own_values = new[1].astype(F32)
    own = jnp.stack(
        [jnp.sum(wide[n] * own_keys[n : n + 1], axis=1, keepdims=True) for n in range(32)]
    ) * SCALE
    s = scores[...]
    peak = jnp.maximum(jnp.max(s, axis=2, keepdims=True), own)
    w = jnp.exp(s - peak)
    own_weight = jnp.exp(own - peak)
    total = jnp.sum(w, axis=2, keepdims=True) + own_weight
    weights[...] = w.astype(BF16)
    own_weight = own_weight.astype(BF16).astype(F32)
    mass = peak + jnp.log(total)
    inverse = 1.0 / total
    copies[6].wait()
    for n in range(32):
        values = jnp.concatenate([pool[1, table[j, n] - base] for j in range(8)], axis=0)
        mixed = dot(weights[n], values) + own_weight[n] * own_values[n : n + 1]
        scores[slots[n]] = mixed * inverse[n]
    held = [jnp.zeros((GROUP, DH), F32) for _ in range(4)]
    for n in range(32):
        slot = slots[n]
        weights[slot] = wide[n].astype(BF16)
        for i in range(4):
            held[i] = jnp.where(lane + 8 * i == slot, jnp.where(lane < 8, mass[n], 0.0), held[i])
    for i, out in enumerate(outs):
        out[0:8] = weights[8 * i : 8 * i + 8]
        out[8] = order.astype(BF16)
        out[9:17] = scores[8 * i : 8 * i + 8].astype(BF16)
        out[17] = split_tile(jnp.where(lane < 8, held[i], 0.0), 8)


def local_parts(q, prompt, table, length, new, pool):
    out = jax.ShapeDtypeStruct((18, GROUP, DH), BF16)
    return pl.pallas_call(
        local_body,
        out_shape=[out] * 4,
        in_specs=[HBM] * 6,
        out_specs=[VMEM] * 4,
        scratch_shapes=[
            pltpu.VMEM((32, GROUP * DH), BF16),
            pltpu.SMEM((32,), jnp.int32),
            pltpu.SMEM((8, 32), jnp.int32),
            pltpu.SMEM((32,), jnp.int32),
            pltpu.VMEM((2, 32, DH), BF16),
            pltpu.VMEM((2, 256, GROUP, DH), BF16),
            pltpu.VMEM((32, GROUP, DH), F32),
            pltpu.VMEM((32, GROUP, DH), F32),
            pltpu.VMEM((32, GROUP, DH), BF16),
            pltpu.SMEM((40,), jnp.int32),
            pltpu.SemaphoreType.DMA((7,)),
        ],
        compiler_params=params(54),
        name="local_parts",
    )(q, prompt, table, length, new, pool)


def regroup_body(a2, a1, a3, a0, same, across):
    x, _, _, z = position()
    for i, a in enumerate((a0, a1, a2, a3)):
        same[4 * i : 4 * i + 4] = a[0:4]
        across[4 * i : 4 * i + 4] = a[4:8]
        across[17 + 5 * i : 22 + 5 * i] = a[13:18]

        @pl.when(x ^ (z >> 1) == i)
        def _(a=a):
            same[16] = a[8]
            across[16] = a[8]


def regroup(parts):
    return pl.pallas_call(
        regroup_body,
        out_shape=[
            jax.ShapeDtypeStruct((17, GROUP, DH), BF16),
            jax.ShapeDtypeStruct((37, GROUP, DH), BF16),
        ],
        in_specs=[VMEM] * 4,
        out_specs=[VMEM] * 2,
        compiler_params=params(),
        name="regroup",
    )(parts[2], parts[1], parts[3], parts[0])


ROWS = 256


def prefix_part(q, kv):
    s = dot(q, kv[0], NT)
    peak = jnp.max(s, axis=1, keepdims=True)
    w = jnp.exp2((s - peak) * (SCALE * LOG2E))
    return dot(w.astype(BF16), kv[1]), peak * SCALE, jnp.sum(w, axis=1, keepdims=True)


def prefix_block(q, kv0, kv1):
    mixed0, peak0, total0 = prefix_part(q, kv0)
    mixed1, peak1, total1 = prefix_part(q, kv1)
    top = jnp.maximum(peak0, peak1)
    f0, f1 = jnp.exp(peak0 - top), jnp.exp(peak1 - top)
    total = total0 * f0 + total1 * f1
    return (mixed0 * f0 + mixed1 * f1) * (1.0 / total), top + jnp.log(total)


COUNT = ROWS // GROUP


def prefix_send_body(qa, qb, kv0, kv1, after, out):
    lane = lanes()
    tile = jnp.zeros((GROUP, DH), F32)
    for half, q in enumerate((qa, qb)):
        for i in range(256 // ROWS):
            rows = q[i * COUNT : (i + 1) * COUNT].reshape(ROWS, DH)
            mixed, mass = prefix_block(rows, kv0, kv1)
            at = half * 16 + i * COUNT
            out[at : at + COUNT] = mixed.reshape(COUNT, GROUP, DH).astype(BF16)
            for n in range(COUNT):
                tile = jnp.where(lane == at + n, mass[n * GROUP : (n + 1) * GROUP], tile)
    out[32] = split_tile(tile, 32)


def prefix_keep_body(q, kv0, kv1, out, masses):
    for i in range(256 // ROWS):
        rows = q[i * COUNT : (i + 1) * COUNT].reshape(ROWS, DH)
        mixed, mass = prefix_block(rows, kv0, kv1)
        at = i * COUNT
        out[at : at + COUNT] = mixed.reshape(COUNT, GROUP, DH)
        masses[at : at + COUNT] = jnp.broadcast_to(mass, (ROWS, DH)).reshape(COUNT, GROUP, DH)


def prefix_cost(rows):
    return pl.CostEstimate(
        flops=4 * rows * 4096 * 128, bytes_accessed=2_500_000, transcendentals=rows * 4096
    )


def prefix_send(qa, qb, kv0, kv1, after):
    return pl.pallas_call(
        prefix_send_body,
        out_shape=jax.ShapeDtypeStruct((33, GROUP, DH), BF16),
        in_specs=[VMEM] * 4 + [ANY],
        out_specs=VMEM,
        compiler_params=params(24),
        cost_estimate=prefix_cost(512),
        name="prefix_send",
    )(qa, qb, kv0, kv1, after)


def prefix_keep(q, kv0, kv1):
    out = jax.ShapeDtypeStruct((16, GROUP, DH), F32)
    return pl.pallas_call(
        prefix_keep_body,
        out_shape=[out, out],
        in_specs=[VMEM] * 3,
        out_specs=[VMEM, VMEM],
        compiler_params=params(24),
        cost_estimate=prefix_cost(256),
        name="prefix_keep",
    )(q, kv0, kv1)


def combine_body(
    own, own_masses, cross, cross_masses, message, s0, s1, s2, s3, far, out, held
):
    x, y, _, z = position()
    y_high = y >> 1
    theirs = join_tile(message[32], 32)
    near = [join_tile(s[17], 8) for s in (s0, s1, s2, s3)]
    across = [join_tile(far[21 + 5 * i], 8) for i in range(4)]
    for g in range(2):
        for kx in range(4):
            for k in range(4):
                n = g * 16 + kx * 4 + k
                at = kx * 4 + k
                a, la = ((own, own_masses), (cross, cross_masses))[g]
                a, la = a[at], la[at]
                b = message[n].astype(F32)
                lb = jnp.broadcast_to(theirs[:, n : n + 1], (GROUP, DH))
                if g == 0:
                    s = (s0, s1, s2, s3)[kx][9 + k].astype(F32)
                    ls = jnp.broadcast_to(near[kx][:, k : k + 1], (GROUP, DH))
                else:
                    s = far[17 + 5 * kx + k].astype(F32)
                    ls = jnp.broadcast_to(across[kx][:, 4 + k : 5 + k], (GROUP, DH))
                top = jnp.maximum(jnp.maximum(la, lb), ls)
                ea, eb, es = jnp.exp(la - top), jnp.exp(lb - top), jnp.exp(ls - top)
                row = (ea * a + eb * b + es * s) / (ea + eb + es)
                target = (x ^ kx) * 2 + (y_high ^ g)
                held[((target - z - 2) & 7) * 4 + k] = row
    for h in range(GROUP):
        out[:, h * DH : (h + 1) * DH] = held[:, h, :].astype(BF16)


def combine(own, cross, message, near, far):
    return pl.pallas_call(
        combine_body,
        out_shape=jax.ShapeDtypeStruct((32, GROUP * DH), BF16),
        in_specs=[VMEM] * 10,
        out_specs=VMEM,
        scratch_shapes=[pltpu.VMEM((32, GROUP, DH), F32)],
        compiler_params=params(),
        name="combine",
    )(*own, *cross, message, *near, far)


def by_target(total):
    low = lax.broadcasted_iota(jnp.int32, (8, total.shape[1]), 0) < 4
    chunks = []
    for g in range(2):
        even, odd = [], []
        for j in (0, 2):
            first = total[j * 16 + g * 8 : j * 16 + g * 8 + 8]
            second = total[(j + 1) * 16 + g * 8 : (j + 1) * 16 + g * 8 + 8]
            even.append(jnp.where(low, first, pltpu.roll(second, 4, 0)))
            odd.append(jnp.where(low, pltpu.roll(first, 4, 0), second))
        chunks += [jnp.concatenate(even, axis=0), jnp.concatenate(odd, axis=0)]
    return chunks


def project_body(a, b, c, w0, w1, out):
    rows = jnp.concatenate([a[...], b[...], c[...]], axis=0)
    for side, weight in enumerate((w0, w1)):
        total = dot(rows, weight[...])
        for i in range(3):
            for d, chunk in enumerate(by_target(total[64 * i : 64 * i + 64])):
                out[d, i * 16 : i * 16 + 16, side * 512 : side * 512 + 512] = chunk


def project(blocks, weights):
    return pl.pallas_call(
        project_body,
        out_shape=jax.ShapeDtypeStruct((4, 48, 1024), F32),
        in_specs=[VMEM] * 5,
        out_specs=VMEM,
        compiler_params=params(),
        cost_estimate=pl.CostEstimate(
            flops=2 * 192 * 2048 * 1024, bytes_accessed=4_500_000, transcendentals=0
        ),
        name="project",
    )(*blocks, *weights)


def last_chunks(a, b, w0, w1, first):
    rows = jnp.concatenate([a[...], b[...]], axis=0)
    for side, weight in enumerate((w0, w1)):
        columns = slice(side * 512, side * 512 + 512)
        for d, chunk in enumerate(by_target(dot(rows, weight[...]))):
            yield side, columns, d, jnp.concatenate([first[d, :, columns], chunk], axis=0)


def far_body(a, b, w0, w1, first, keep, up, down, direct):
    for _, columns, d, whole in last_chunks(a, b, w0, w1, first):
        if d == 0:
            keep[:, columns] = whole
        else:
            (up, direct, down)[d - 1][:, columns] = whole.astype(BF16)


def near_body(a, b, w0, w1, first, keep6, down, keep0, up):
    for _, columns, d, whole in last_chunks(a, b, w0, w1, first):
        if d in (0, 2):
            (keep6, keep0)[d // 2][:, columns] = whole
        else:
            (down, up)[d // 2][:, columns] = whole.astype(BF16)


SUM = jax.ShapeDtypeStruct((64, 1024), F32)
SENT = jax.ShapeDtypeStruct((64, 1024), BF16)
HALF = jax.ShapeDtypeStruct((64, 512), BF16)


def plain(body, out_shape, *args):
    return pl.pallas_call(
        body,
        out_shape=out_shape,
        in_specs=[VMEM] * len(args),
        out_specs=[VMEM] * len(out_shape),
        compiler_params=params(),
        name=body.__name__[:-5],
    )(*args)


def middle_body(keep2, keep6, below, above, up, down):
    up[...] = (keep2[...] + below[...].astype(F32)).astype(BF16)
    down[...] = (keep6[...] + above[...].astype(F32)).astype(BF16)


def total_body(keep, below1, above1, below2, above2, opposite, own, other):
    near = keep[...] + below1[...].astype(F32) + above1[...].astype(F32)
    whole = near + below2[...].astype(F32) + above2[...].astype(F32)
    whole = (whole + opposite[...].astype(F32)).astype(BF16)
    own[...] = whole[:, :512]
    other[...] = whole[:, 512:]


def order_body(orders, pick):
    x, y, core, z = position()
    lane = lanes()
    order = jnp.zeros((GROUP, DH), F32)
    for block in range(4):
        dy = (2 * (z & 1) + block // 2) ^ y
        tile = orders[((block % 2) ^ core) * 4 + dy].astype(F32)
        order = jnp.where(lane >> 5 == block, pltpu.roll(tile, 32 * block, 1), order)
    order = order.astype(jnp.int32)
    prompt, k = order >> 2, order & 3
    block = lane >> 5
    far = block & 1
    dx = (prompt >> 1) ^ x
    dy = (2 * (prompt & 1) + (block >> 1)) ^ y
    first = jnp.where(far == 0, dx, dy)
    second = jnp.where(far == 0, dy, dx)
    first = jnp.where((first == 1) | (first == 2), 3 - first, first)
    second = jnp.where(second >= 2, 5 - second, second)
    source = ((far ^ core) * 16 + second * 4 + first) * 4 + k
    row = lax.broadcasted_iota(jnp.int32, (128, 128), 0)
    pick[...] = (row == source[0:1]).astype(F32).astype(BF16)


def order_rows(orders):
    return pl.pallas_call(
        order_body,
        out_shape=jax.ShapeDtypeStruct((128, 128), BF16),
        in_specs=[VMEM],
        out_specs=VMEM,
        compiler_params=params(),
        name="order_rows",
    )(orders)


def finish_body(own, other, pick, out):
    dims = (((0,), (0,)), ((), ()))
    mixed = dot(pick[0:64], own[...], dims) + dot(pick[64:128], other[...], dims)
    out[...] = mixed.astype(BF16)


def finish(own, other, pick):
    return pl.pallas_call(
        finish_body,
        out_shape=jax.ShapeDtypeStruct((128, 512), BF16),
        in_specs=[VMEM] * 3,
        out_specs=VMEM,
        compiler_params=params(),
        name="finish",
    )(own, other, pick)


def along(value, shift, k):
    return lax.ppermute(value, "batch", [(i, i ^ (k << shift)) for i in range(BATCH)])


def along_x(value, k):
    return along(value, 3, k)


def along_y(value, k):
    return along(value, 1, k)


def other_core(value):
    return along(value, 0, 1)


def turned(value, k, phase):
    pairs = [(i, i ^ (k << (3 if (i & 1) == phase else 1))) for i in range(BATCH)]
    return lax.ppermute(value, "batch", pairs)


def gathered(parts):
    ring0 = jnp.concatenate(parts, axis=0)
    ring1, ring3 = turned(ring0, 1, 1), turned(ring0, 3, 1)
    return ring0, ring1, ring3, [turned(ring3[:32], 1, 1), turned(ring1[32:], 3, 1)]


def along_z(value, k):
    return lax.ppermute(value, "head", [(i, (i + k) % HEADS) for i in range(HEADS)])


def shards(queries, new_kv, prefix_kv, suffix_kv, page_table, suffix_len, prompt_of, out_weight):
    prefix_other = other_core(prefix_kv)
    weights = [out_weight, other_core(out_weight)]

    sent = local_parts(queries, prompt_of, page_table.T, suffix_len, new_kv, suffix_kv)
    x2, x1, x3 = (along_x(sent[k], k) for k in (2, 1, 3))
    by_x = [sent[0], x1, x2, x3]
    same, across = regroup(by_x)
    from1, from3 = along_y(same, 1), along_y(across, 3)

    own = prefix_keep(same, prefix_kv, prefix_other)
    passed, own = lax.optimization_barrier((from3, own))
    from2 = along_y(passed, 1)
    message = prefix_send(from1, from3, prefix_kv, prefix_other, own[1])
    message, from2 = lax.optimization_barrier((message, from2))
    message = along_y(message, 1)
    cross = prefix_keep(from2, prefix_kv, prefix_other)
    attended = combine(own, cross, message, by_x, from2)

    orders = jnp.stack([same[16], from1[16], from2[16], from3[16]])
    orders = jnp.concatenate([orders, other_core(orders)], axis=0)
    pick = order_rows(orders)

    next2, next1, next3 = (turned(attended, k, 0) for k in (2, 1, 3))
    parts = [attended, next2, next1, next3]
    far, near = [gathered([a[i : i + 16] for a in parts]) for i in (0, 16)]
    first_far, first_near = project(far[:3], weights), project(near[:3], weights)
    keep2, up3, down3, up4 = plain(
        far_body, [SUM, SENT, SENT, SENT], *far[3], *weights, first_far
    )
    below3, above3 = along_z(up3, 1), along_z(down3, -1)
    opposite = along_z(up4, 4)
    keep6, down1, keep0, up1 = plain(
        near_body, [SUM, SENT, SUM, SENT], *near[3], *weights, first_near
    )
    below1, above1 = along_z(up1, 1), along_z(down1, -1)
    up2, down2 = plain(middle_body, [SENT, SENT], keep2, keep6, below3, above3)
    below2, above2 = along_z(up2, 2), along_z(down2, -2)
    own, other = plain(total_body, [HALF, HALF], keep0, below1, above1, below2, above2, opposite)
    return finish(own, other_core(other), pick)


def solution(mesh):
    placed = (
        P("batch", "head"),
        P(None, "batch", "head"),
        P(None, "batch", "head"),
        P(None, "batch", None, "head"),
        P("batch", None),
        P("batch"),
        P("batch"),
        P("head", "batch"),
    )
    return jax.shard_map(
        shards, mesh=mesh, in_specs=placed, out_specs=P("head", "batch"), check_vma=False
    )
```
